32 devices in a mesh: member: 2 (over x), tile: 16 (over z, y, core).
Axes of the slice: x: 2, y: 2, z: 4, core: 2. Of those that a mesh axis runs over, the one named last changes fastest.
Arguments:
- ocean: float32 [4, 4, 128, 3600], P('member', None, 'tile'), parts along dimension 0, may hold values from 0.5 to 2
- kappa: float32 [128, 3600], P('tile'), may hold values from 0.1 to 0.2
- atmos: float32 [4, 8, 256, 384], P('member', None, 'tile'), parts along dimension 0, may hold values from 0.5 to 2
- piston: float32 [256, 384], P('tile'), may hold values from 0.2 to 1
- atmos_mix: float32 [256, 384], P('tile'), may hold values from 0.05 to 0.25
- fold_map: int32 [3600], replicated, may hold values from 0 to 3599, each once
- send_tile: int32 [16, 8, 16], P('tile'), may hold values from 0 to 224
- slot_counts: int32 [16, 8], P('tile'), may hold values from 0 to 16, as said below
- out_slot: int32 [16, 128], P('tile'), may hold values from 0 to 63, as said below
- out_tile: int32 [16, 8, 8], P('tile'), may hold values from 0 to 47
- remap_w: bfloat16 [16, 128, 128, 128], P('tile'), may hold values from 0 to 0.01171875
Outputs:
- ocean_next: float32 [4, 4, 128, 3600], P('member', None, 'tile'), parts along dimension 0
- atmos_next: float32 [4, 8, 256, 384], P('member', None, 'tile'), parts along dimension 0
The draws below stay inside these ranges and needn't reach their ends.
There are 2 independent parts, one for each index of `member`. The reference program is written for one: setup_inputs(seed, part) draws one part's arguments, and reference() takes and returns one part's arrays. A program takes and returns all parts, laid end to end along the dimension named above; an argument that names none is the same for every part. Nothing has to cross between parts.
Inputs may be any that keep to these rules, and one draw needn't show every extreme that they name: `send_tile`: local ocean tile index; slots at or past the coupler's live count are not read. `slot_counts`: zero where the source device c - d + 4 lies outside the devices. `out_slot`: the owner c + q // 8 - 4 of slot q lies inside the devices. `out_tile`: local atmosphere tile index. `fold_map`: a permutation of the columns.
All inputs are finite; a program needn't handle non-finite values.
Results may differ from the reference program's by a relative error of at most 0.00085.
Values may be sent and summed in bfloat16 or wider, within the bound.
No kernel may reach another device: no remote copies, remote signals or barrier semaphores. Data moves between devices by JAX's collectives and lax.ppermute only.
A program may use at most 64 MiB of HBM per device.

```python
import math
import jax
import jax.numpy as jnp
from jax import lax

TR = 2
TILE = 128
OX = 3600
OLEV = 4
OSTEPS = 4
AX = 384
ALEV = 8
ASTEPS = 4
WIN = 8
HALF = 4
CAP = 16
CAP2 = 8
OY = 128
AY = 256
OT = 225
AT = 48
N_TILE = 16


def draw_slot_counts(key, part):
    key = jax.random.fold_in(key, 11)
    key_heavy, key_count, key_pick = jax.random.split(key, 3)
    heavy = jax.random.randint(key_heavy, (N_TILE, 1), 1, 5)
    limit = heavy * CAP // 4 + 1
    counts = jax.random.randint(key_count, (N_TILE, WIN), 0, limit)
    source = jnp.arange(N_TILE)[:, None] - jnp.arange(WIN)[None, :] + HALF
    valid = (source >= 0) & (source < N_TILE)
    counts = jnp.where(valid, counts, 0)
    chosen = jax.random.randint(key_pick, (), 0, N_TILE)
    counts = counts.at[chosen, HALF].set(CAP)
    return counts.astype(jnp.int32)


def draw_out_slot(key, part):
    key = jax.random.fold_in(key, 23)
    key_group, key_slot = jax.random.split(key, 2)
    rows = jnp.arange(N_TILE)[:, None]
    lowest = jnp.maximum(0, HALF - rows)
    highest = jnp.minimum(WIN, N_TILE + HALF - rows)
    group = jax.random.randint(key_group, (N_TILE, WIN * CAP), lowest, highest)
    within = jax.random.randint(key_slot, (N_TILE, WIN * CAP), 0, CAP2)
    result = group * CAP2 + within
    result = result.at[0, 0].set(WIN * CAP2 - 1)
    result = result.at[N_TILE - 1, 0].set(0)
    return result.astype(jnp.int32)


def plant(values, rng, least, top_value):
    index_at = [jax.random.randint(jax.random.fold_in(rng, axis), (), 0, length) for axis, length in enumerate(values.shape)]
    widest = values.shape.index(max(values.shape))
    neighbour = index_at[:widest] + [(index_at[widest] + 1) % values.shape[widest]] + index_at[widest + 1:]
    return values.at[tuple(index_at)].set(least).at[tuple(neighbour)].set(top_value)


def block_levels(stream_key, extent, cuts, least, largest):
    level, own = 1.0, jax.random.fold_in(stream_key, 6)
    for dim, blocks in cuts:
        steps = jnp.exp(jax.random.uniform(jax.random.fold_in(own, dim), (blocks,), jnp.float32, least / len(cuts), largest / len(cuts)))
        level = level * jnp.repeat(steps, extent[dim] // blocks).reshape([-1 if axis == dim else 1 for axis in range(len(extent))])
    return level


def setup_inputs(seed: int = 0, part: int = 0) -> dict:
    key_of = jax.random.split(jax.random.key(seed), 12)
    part_keys = jax.random.split(jax.random.fold_in(key_of[11], part), 12)
    ocean = jnp.clip(0.5 + 1.5 * jax.random.uniform(part_keys[0], (TR, OLEV, OY, OX), jnp.float32) ** block_levels(part_keys[0], (TR, OLEV, OY, OX), ((2, 16),), -0.2, 0.2), 0.5, 2.0)
    kappa = jnp.clip(jnp.exp(math.log(0.2) - 0.6931472 * jax.random.uniform(key_of[1], (OY, OX), jnp.float32) ** block_levels(key_of[1], (OY, OX), ((0, 16),), -0.2, 0.2)), 0.1, 0.2)
    atmos = jnp.clip(0.5 + 1.5 * jax.random.uniform(part_keys[2], (TR, ALEV, AY, AX), jnp.float32) ** block_levels(part_keys[2], (TR, ALEV, AY, AX), ((2, 16),), -0.2, 0.2), 0.5, 2.0)
    piston = jnp.clip(jnp.exp(math.log(1.0) - 1.609438 * jax.random.uniform(key_of[3], (AY, AX), jnp.float32) ** block_levels(key_of[3], (AY, AX), ((0, 16),), -0.2, 0.2)), 0.2, 1.0)
    atmos_mix = jnp.clip(jnp.exp(math.log(0.25) - 1.609438 * jax.random.uniform(key_of[4], (AY, AX), jnp.float32) ** block_levels(key_of[4], (AY, AX), ((0, 16),), -0.2, 0.2)), 0.05, 0.25)
    fold_map = jax.random.permutation(key_of[5], OX).astype(jnp.int32)
    send_tile = plant(jax.random.randint(key_of[6], (N_TILE, WIN, CAP), 0, OT), jax.random.fold_in(key_of[6], 1), 0, OT - 1).astype(jnp.int32)
    slot_counts = draw_slot_counts(jax.random.fold_in(key_of[11], 71), part)
    out_slot = draw_out_slot(jax.random.fold_in(key_of[11], 71), part)
    out_tile = plant(jax.random.randint(key_of[9], (N_TILE, WIN, CAP2), 0, AT), jax.random.fold_in(key_of[9], 1), 0, AT - 1).astype(jnp.int32)
    remap_w = jnp.clip(0.01171875 * jax.random.uniform(key_of[10], (N_TILE, WIN * CAP, TILE, TILE), jnp.float32) ** block_levels(key_of[10], (N_TILE, WIN * CAP, TILE, TILE), ((0, 16),), -0.2, 0.2), 0.0, 0.01171875).astype(jnp.bfloat16)
    return dict(ocean=ocean, kappa=kappa, atmos=atmos, piston=piston, atmos_mix=atmos_mix, fold_map=fold_map, send_tile=send_tile, slot_counts=slot_counts, out_slot=out_slot, out_tile=out_tile, remap_w=remap_w)


vertical_mix = 0.1
ocean_rate = 4.0
atmos_rate = 0.5
solubility = 1.2


def ocean_sweep(padded, kappa):
    centre = padded[:, :, 1:-1]
    north_rows = padded[:, :, 2:]
    south_rows = padded[:, :, :-2]
    east_cells = jnp.roll(centre, -1, axis=3)
    west_cells = jnp.roll(centre, 1, axis=3)
    upper_level = jnp.concatenate([centre[:, :1], centre[:, :-1]], axis=1)
    lower_level = jnp.concatenate([centre[:, 1:], centre[:, -1:]], axis=1)
    horizontal = north_rows + south_rows + east_cells + west_cells - 4.0 * centre
    vertical = upper_level + lower_level - 2.0 * centre
    return centre + kappa * horizontal + vertical_mix * vertical


def atmos_sweeps(field, mixing):
    for sweep_index in range(ASTEPS):
        upper_level = jnp.concatenate([field[:, :1], field[:, :-1]], axis=1)
        lower_level = jnp.concatenate([field[:, 1:], field[:, -1:]], axis=1)
        field = field + mixing * (upper_level + lower_level - 2.0 * field)
    return field


def regroup(values, sign):
    total = values.shape[0]
    width = values.shape[1]
    offsets = jnp.arange(width).astype(jnp.int32)
    rows = jnp.arange(total).astype(jnp.int32)[:, None] + sign * (offsets[None, :] - HALF)
    valid = (rows >= 0) & (rows < total)
    picked = values[jnp.clip(rows, 0, total - 1), offsets[None, :]]
    shape = valid.shape + (1,) * (values.ndim - 2)
    return jnp.where(valid.reshape(shape), picked, jnp.zeros_like(picked))


def reference(ocean, kappa, atmos, piston, atmos_mix, fold_map, send_tile, slot_counts, out_slot, out_tile, remap_w):
    count = N_TILE
    surface = ocean[:, 0].astype(jnp.bfloat16)
    surface_tiles = surface.reshape(TR, count, OT, TILE).transpose(1, 2, 0, 3)
    sent = jax.vmap(lambda local, picks: local[picks])(surface_tiles, send_tile)
    received = regroup(sent, -1).reshape(count, WIN * CAP, TR, TILE)
    live_slot = (jnp.arange(CAP)[None, None, :] < slot_counts[:, :, None]).reshape(count, WIN * CAP)

    def forward_block(items):
        weights, data, alive, dest = items
        sums = jnp.einsum("pij,ptj->pti", weights.astype(jnp.float32), data.astype(jnp.float32),
                          precision=lax.Precision.HIGHEST)
        sums = jnp.where(alive[:, None, None], sums, 0.0)
        return jax.ops.segment_sum(sums, dest, num_segments=WIN * CAP2)

    partial_value = lax.map(forward_block, (remap_w, received, live_slot, out_slot))
    to_owner = regroup(partial_value.reshape(count, WIN, CAP2, TR, TILE), -1)
    remapped = jax.vmap(lambda parts, picks: jax.ops.segment_sum(
        parts.reshape(WIN * CAP2, TR, TILE), picks.reshape(-1), num_segments=AT))(to_owner, out_tile)
    atmos_tiles = atmos[:, 0].reshape(TR, count, AT, TILE).transpose(1, 2, 0, 3)
    piston_tiles = piston.reshape(count, AT, TILE)[:, :, None, :]
    flux = piston_tiles * (solubility * atmos_tiles - remapped)
    flux_round = flux.astype(jnp.bfloat16)
    flux_sent = jax.vmap(lambda local, picks: local[picks])(flux_round, out_tile)
    at_coupler = regroup(flux_sent, 1).reshape(count, WIN * CAP2, TR, TILE)

    def backward_block(items):
        weights, fluxes, alive, dest = items
        gathered = fluxes[dest]
        sums = jnp.einsum("pij,pti->ptj", weights.astype(jnp.float32), gathered.astype(jnp.float32),
                          precision=lax.Precision.HIGHEST)
        return jnp.where(alive[:, None, None], sums, 0.0)

    back_sums = lax.map(backward_block, (remap_w, at_coupler, live_slot, out_slot))
    to_source = regroup(back_sums.reshape(count, WIN, CAP, TR, TILE), 1)
    ocean_flux = jax.vmap(lambda parts, picks: jax.ops.segment_sum(
        parts.reshape(WIN * CAP, TR, TILE), picks.reshape(-1), num_segments=OT))(to_source, send_tile)
    ocean_flux = ocean_flux.transpose(2, 0, 1, 3).reshape(TR, OY, OX)

    state = ocean
    for sweep_index in range(OSTEPS):
        folded = jnp.take(state[:, :, -1:], fold_map, axis=3)
        padded = jnp.concatenate([jnp.zeros_like(folded), state, folded], axis=2)
        state = ocean_sweep(padded, kappa)
    ocean_next = state.at[:, 0].add(ocean_rate * ocean_flux)

    flux_grid = flux.transpose(2, 0, 1, 3).reshape(TR, AY, AX)
    atmos_start = atmos.at[:, 0].add(-atmos_rate * flux_grid)
    atmos_next = atmos_sweeps(atmos_start, atmos_mix)
    return ocean_next, atmos_next
```

```python
import functools

import jax
import jax.numpy as jnp
from jax import lax
from jax.experimental import pallas as pl
from jax.experimental.pallas import tpu as pltpu
from jax.sharding import PartitionSpec as P

OSTEPS = 4
ASTEPS = 4
LANES = 128

vertical_mix = 0.1
ocean_rate = 4.0
atmos_rate = 0.5
solubility = 1.2

VMEM_LIMIT = 40 * 1024 * 1024


def params():
    return pltpu.CompilerParams(vmem_limit_bytes=VMEM_LIMIT)


def vmem():
    return pl.BlockSpec(memory_space=pltpu.VMEM)


def smem():
    return pl.BlockSpec(memory_space=pltpu.SMEM)


def iota(shape, dim):
    return lax.broadcasted_iota(jnp.int32, shape, dim)


def split_dot(table, values, dims):
    high = values.astype(jnp.bfloat16)
    low = (values - high.astype(jnp.float32)).astype(jnp.bfloat16)
    dot = functools.partial(
        lax.dot_general, dimension_numbers=(dims, ((), ())), preferred_element_type=jnp.float32
    )
    return dot(table, high) + dot(table, low)


def shear(tile, sign, shift):
    lane = iota(tile.shape, 1)
    row = iota(tile.shape, 0)
    source = (lane - sign * shift * row) & (LANES - 1)
    return jnp.take_along_axis(tile, source, axis=1, mode="promise_in_bounds")


def regroup_in(ocean_ref, grouped):
    columns = ocean_ref.shape[1]
    for k in range(grouped.shape[0]):
        width = min(LANES, columns - k * LANES)
        grouped[k, :, :width] = ocean_ref[:, k * LANES : k * LANES + width]


def pack_kernel(
    me_ref, send_ref, ocean_ref, kappa_ref, out_ref, even_ref, odd_ref, tiles, rows, tail, grouped
):
    me = me_ref[0]
    peers = out_ref.shape[0]
    _, window, slots = send_ref.shape
    tracers = tiles.shape[0]
    planes = ocean_ref.shape[0] // 8
    levels = planes // tracers
    columns = ocean_ref.shape[1]
    full = columns // LANES
    rest = columns - full * LANES
    lane = iota((8, LANES), 1)
    row = iota((8, LANES), 0)
    wraps = lane < rest * row
    for tracer in range(tracers):
        top = tracer * levels * 8
        tail[:, :rest] = ocean_ref[top : top + 8, full * LANES :]
        before = jnp.zeros((8, LANES), jnp.float32)
        first = None
        for k in range(full + 1):
            part = tail[...] if k == full else ocean_ref[top : top + 8, k * LANES : (k + 1) * LANES]
            turned = shear(part, 1, rest)
            value = jnp.where(wraps, before, turned)
            before = turned
            if k == 0:
                first = value
            else:
                tiles[tracer, k * 8 : (k + 1) * 8] = value
        tiles[tracer, 0:8] = jnp.where(wraps, pltpu.roll(value, 1, 0), first)
    for d in range(window):
        for k in range(slots):
            index = send_ref[0, d, k]
            over = index // full
            place = jnp.where(index == 8 * full, 8 * full + 7, (index - over * full) * 8 + over)
            for tracer in range(tracers):
                rows[d, pl.ds(tracer * slots + k, 1), :] = tiles[tracer, pl.ds(place, 1), :]
    out_ref[...] = jnp.zeros_like(out_ref)
    for d in range(window):
        peer = me + d - window // 2

        @pl.when((peer >= 0) & (peer < peers))
        def _():
            out_ref[peer] = rows[d].astype(jnp.bfloat16)

    odd = lax.rem(me, 2)
    regroup_in(ocean_ref, grouped)
    for target, base in ((even_ref, 4 * (1 - odd)), (odd_ref, 4 * odd)):
        for r in range(4):
            target[pl.ds(4 * planes + r, 1), :] = kappa_ref[pl.ds(base + r, 1), :]
            for k in range(full + 1):
                width = min(LANES, columns - k * LANES)
                value = grouped[k, pl.ds(base + r, planes, stride=8), :]
                target[r * planes : (r + 1) * planes, k * LANES : k * LANES + width] = value[:, :width]


def sweeps_kernel(
    me_ref, ocean_ref, kappa_ref, even_ref, odd_ref, fold_ref, out_ref, state, kap, fold, grouped, peers
):
    me = me_ref[0]
    planes, columns = ocean_ref.shape[0] // 8, ocean_ref.shape[1]
    full = columns // LANES
    rest = columns - full * LANES
    tiles = full + 1
    levels = 4
    odd = lax.rem(me, 2) == 1
    last = me == peers - 1
    lane = iota((8, LANES), 1)
    plane = iota((8, LANES), 0)
    level = plane & (levels - 1)

    regroup_in(ocean_ref, grouped)
    for r in range(8):
        for k in range(tiles):
            at = slice(k * LANES, (k + 1) * LANES)
            state[0, 4 + r, :, at] = grouped[k, pl.ds(r, planes, stride=8), :]

    for k in range(tiles):
        width = min(LANES, columns - k * LANES)
        kap[k, 4:12, :width] = kappa_ref[:, k * LANES : k * LANES + width]

    def place_halo(above, below):
        for r in range(4):
            state[0, r, :, :columns] = below[r * planes : (r + 1) * planes, :]
            state[0, 12 + r, :, :columns] = above[r * planes : (r + 1) * planes, :]
        for k in range(tiles):
            width = min(LANES, columns - k * LANES)
            at = slice(k * LANES, k * LANES + width)
            kap[k, 0:4, :width] = below[4 * planes : 4 * planes + 4, at]
            kap[k, 12:16, :width] = above[4 * planes : 4 * planes + 4, at]

    @pl.when(odd)
    def _():
        place_halo(odd_ref, even_ref)

    @pl.when(jnp.logical_not(odd))
    def _():
        place_halo(even_ref, odd_ref)

    @pl.when(last)
    def _():
        fold[:, :columns] = jnp.broadcast_to(fold_ref[...], (8, columns))

    def sweep(now, later, low, high):
        @pl.when(last)
        def _():
            def gather(j, carry):
                at = pl.ds(pl.multiple_of(j * LANES, LANES), LANES)
                index = fold[:, at]
                inner = index & (LANES - 1)
                outer = index >> 7
                value = jnp.zeros((8, LANES), jnp.float32)
                for k in range(tiles):
                    part = state[now, 11, :, k * LANES : (k + 1) * LANES]
                    part = jnp.take_along_axis(part, inner, axis=1, mode="promise_in_bounds")
                    value = jnp.where(outer == k, part, value)
                state[now, 12, :, at] = value
                return carry

            lax.fori_loop(0, tiles, gather, 0)

        def body(r, carry):
            def cell(k):
                return state[now, r, :, k * LANES : (k + 1) * LANES]

            tiles_here = [cell(k) for k in range(tiles)]
            east_turned = [pltpu.roll(c, LANES - 1, 1) for c in tiles_here]
            west_turned = [pltpu.roll(c, 1, 1) for c in tiles_here]
            for k in range(tiles):
                centre = tiles_here[k]
                if k == full:
                    east = jnp.where(
                        lane == rest - 1, pltpu.roll(tiles_here[0], rest - 1, 1), east_turned[k]
                    )
                else:
                    east = jnp.where(lane == LANES - 1, east_turned[k + 1], east_turned[k])
                if k == 0:
                    west = jnp.where(
                        lane == 0, pltpu.roll(tiles_here[full], LANES - rest + 1, 1), west_turned[0]
                    )
                else:
                    west = jnp.where(lane == 0, west_turned[k - 1], west_turned[k])
                at = slice(k * LANES, (k + 1) * LANES)
                north = state[now, r + 1, :, at]
                south = state[now, r - 1, :, at]
                upper = jnp.where(level == 0, centre, pltpu.roll(centre, 1, 0))
                lower = jnp.where(level == levels - 1, centre, pltpu.roll(centre, 7, 0))
                horizontal = north + south + east + west - 4.0 * centre
                vertical = upper + lower - 2.0 * centre
                rate = kap[k, pl.ds(r, 1), :]
                value = centre + rate * horizontal + vertical_mix * vertical
                if later is None:
                    grouped[k, pl.ds(r - 4, planes, stride=8), :] = value
                else:
                    state[later, r, :, at] = value
            return carry

        lax.fori_loop(low, high, body, 0)

    for step in range(OSTEPS):
        later = None if step == OSTEPS - 1 else (step + 1) % 2
        sweep(step % 2, later, step + 1, 15 - step)
    for k in range(tiles):
        width = min(LANES, columns - k * LANES)
        out_ref[:, k * LANES : k * LANES + width] = grouped[k, :, :width]


def live_row(counts_ref, window, slots):
    at = iota((1, window * slots), 1)
    live = at < 0
    for d in range(window):
        live = live | ((at >= d * slots) & (at < d * slots + counts_ref[0, d]))
    return live


def forward_kernel(me_ref, counts_ref, recv_ref, slot_ref, w_ref, out_ref, sums):
    me = me_ref[0]
    peers = recv_ref.shape[0]
    window = counts_ref.shape[1]
    slots = w_ref.shape[0]
    tracers = sums.shape[0]
    d = pl.program_id(0)
    row = iota((slots, LANES), 0)
    source = jnp.clip(me - d + window // 2, 0, peers - 1)
    cells = recv_ref[source]
    found = [jnp.zeros((slots, LANES), jnp.float32) for _ in range(tracers)]
    for k in range(slots):
        product = lax.dot_general(
            cells, w_ref[k], (((1,), (1,)), ((), ())), preferred_element_type=jnp.float32
        )
        for t in range(tracers):
            found[t] = jnp.where(row == k, product[t * slots : (t + 1) * slots], found[t])
    for t in range(tracers):
        sums[t, pl.ds(pl.multiple_of(d * slots, slots), slots), :] = found[t]

    @pl.when(d == window - 1)
    def _():
        n_slots = window * 8
        live = live_row(counts_ref, window, slots)
        table = (iota((n_slots, window * slots), 0) == slot_ref[...]) & live
        table = jnp.where(table, 1.0, 0.0).astype(jnp.bfloat16)
        partial_sums = [split_dot(table, sums[t], ((1,), (0,))) for t in range(tracers)]
        out_ref[...] = jnp.zeros_like(out_ref)
        for g in range(window):
            peer = me + g - window // 2

            @pl.when((peer >= 0) & (peer < peers))
            def _():
                for t in range(tracers):
                    out_ref[peer, t * 8 : (t + 1) * 8, :] = partial_sums[t][g * 8 : (g + 1) * 8]


def flux_kernel(
    me_ref, parts_ref, place_ref, table_ref, atmos_ref, piston_ref, send_ref, flux_ref
):
    me = me_ref[0]
    peers = parts_ref.shape[0]
    tracers, _, rows, columns = atmos_ref.shape
    across = columns // LANES
    n_tiles = rows * across
    n_slots = place_ref.shape[1]
    window = n_slots // 8
    spread = jnp.where(iota((n_tiles, n_slots), 0) == place_ref[...], 1.0, 0.0)
    spread = spread.astype(jnp.bfloat16)
    piston = jnp.concatenate(
        [piston_ref[:, k * LANES : (k + 1) * LANES] for k in range(across)], axis=0
    )
    sent = []
    for t in range(tracers):
        parts = []
        for g in range(window):
            coupler = me - g + window // 2
            valid = (coupler >= 0) & (coupler < peers)
            block = parts_ref[jnp.clip(coupler, 0, peers - 1), t * 8 : (t + 1) * 8, :]
            parts.append(jnp.where(valid, block, 0.0))
        remapped = split_dot(spread, jnp.concatenate(parts, axis=0), ((1,), (0,)))
        surface = jnp.concatenate(
            [atmos_ref[t, 0, :, k * LANES : (k + 1) * LANES] for k in range(across)], axis=0
        )
        flux = piston * (solubility * surface - remapped)
        for k in range(across):
            flux_ref[t, :, k * LANES : (k + 1) * LANES] = flux[k * rows : (k + 1) * rows]
        sent.append(
            jnp.dot(table_ref[...], flux.astype(jnp.bfloat16), preferred_element_type=jnp.float32)
        )
    send_ref[...] = jnp.zeros_like(send_ref)
    for g in range(window):
        peer = me - g + window // 2

        @pl.when((peer >= 0) & (peer < peers))
        def _():
            block = jnp.concatenate([s[g * 8 : (g + 1) * 8] for s in sent], axis=0)
            send_ref[peer] = block.astype(jnp.bfloat16)


def backward_kernel(me_ref, counts_ref, recv_ref, table_ref, w_ref, out_ref, gathered):
    me = me_ref[0]
    peers = recv_ref.shape[0]
    window = counts_ref.shape[1]
    slots = w_ref.shape[0]
    tracers = gathered.shape[1] // slots
    d = pl.program_id(0)
    row = iota((slots, LANES), 0)

    @pl.when(d == 0)
    def _():
        parts = [[] for _ in range(tracers)]
        for g in range(window):
            owner = me + g - window // 2
            valid = (owner >= 0) & (owner < peers)
            block = recv_ref[jnp.clip(owner, 0, peers - 1)].astype(jnp.float32)
            block = jnp.where(valid, block, 0.0)
            for t in range(tracers):
                parts[t].append(block[t * 8 : (t + 1) * 8])
        for t in range(tracers):
            fluxes = jnp.concatenate(parts[t], axis=0).astype(jnp.bfloat16)
            picked = jnp.dot(table_ref[...], fluxes, preferred_element_type=jnp.float32)
            picked = picked.astype(jnp.bfloat16)
            for e in range(window):
                gathered[e, t * slots : (t + 1) * slots, :] = picked[e * slots : (e + 1) * slots]
        out_ref[...] = jnp.zeros_like(out_ref)

    cells = gathered[d]
    found = [jnp.zeros((slots, LANES), jnp.float32) for _ in range(tracers)]
    for k in range(slots):
        product = jnp.dot(cells, w_ref[k], preferred_element_type=jnp.float32)
        for t in range(tracers):
            found[t] = jnp.where(row == k, product[t * slots : (t + 1) * slots], found[t])
    live = row < counts_ref[0, d]
    peer = me - d + window // 2

    @pl.when((peer >= 0) & (peer < peers))
    def _():
        for t in range(tracers):
            out_ref[peer, t * slots : (t + 1) * slots, :] = jnp.where(live, found[t], 0.0)


def add_kernel(me_ref, returned_ref, place_ref, swept_ref, out_ref):
    me = me_ref[0]
    peers = returned_ref.shape[0]
    tracers, _, _, columns = swept_ref.shape
    n_rows = place_ref.shape[1]
    slots = returned_ref.shape[1] // tracers
    window = n_rows // slots
    full = columns // LANES
    rest = columns - full * LANES
    lane = iota((8, LANES), 1)
    row = iota((8, LANES), 0)
    stays = lane < LANES - rest * row
    table = jnp.where(iota(((full + 1) * 8, n_rows), 0) == place_ref[...], 1.0, 0.0)
    table = table.astype(jnp.bfloat16)
    for t in range(tracers):
        parts = []
        for d in range(window):
            coupler = me + d - window // 2
            valid = (coupler >= 0) & (coupler < peers)
            block = returned_ref[
                jnp.clip(coupler, 0, peers - 1), t * slots : (t + 1) * slots, :
            ]
            parts.append(jnp.where(valid, block, 0.0))
        tiles = split_dot(table, jnp.concatenate(parts, axis=0), ((1,), (0,)))
        rows = [tiles[k * 8 : (k + 1) * 8] for k in range(full + 1)]
        rows[full] = jnp.where(row == 7, rows[full], pltpu.roll(rows[0], 7, 0))
        turned = [shear(value, -1, rest) for value in rows]
        for k in range(full + 1):
            width = LANES
            value = turned[k]
            if k == full:
                width = rest
            else:
                value = jnp.where(stays, value, turned[k + 1])
            at = slice(k * LANES, k * LANES + width)
            out_ref[t, 0, :, at] = swept_ref[t, 0, :, at] + ocean_rate * value[:, :width]


def atmos_kernel(atmos_ref, flux_ref, mix_ref, out_ref):
    tracers, levels, rows, columns = atmos_ref.shape
    for t in range(tracers):
        for r in range(0, rows, 8):
            for c in range(0, columns, LANES):
                at = (slice(r, r + 8), slice(c, c + LANES))
                mixing = mix_ref[at]
                field = [atmos_ref[(t, v) + at] for v in range(levels)]
                field[0] = field[0] - atmos_rate * flux_ref[(t,) + at]
                for _ in range(ASTEPS):
                    field = [
                        field[v]
                        + mixing
                        * (field[max(v - 1, 0)] + field[min(v + 1, levels - 1)] - 2.0 * field[v])
                        for v in range(levels)
                    ]
                for v in range(levels):
                    out_ref[(t, v) + at] = field[v]


def local(
    ocean,
    kappa,
    atmos,
    piston,
    atmos_mix,
    fold_map,
    send_tile,
    slot_counts,
    out_slot,
    out_tile,
    remap_w,
):
    count = lax.axis_size("tile")
    me = lax.axis_index("tile").astype(jnp.int32).reshape(1)
    tracers, levels, ocean_rows, columns = ocean.shape
    planes = tracers * levels
    window, slots_in = send_tile.shape[1:]
    slots_out = out_tile.shape[2]
    blocks = window * slots_in
    n_slots = window * slots_out
    full = columns // LANES
    padded = (full + 1) * LANES
    atmos_rows, atmos_columns = atmos.shape[2:]
    across = atmos_columns // LANES
    n_tiles = atmos_rows * across
    shape = jax.ShapeDtypeStruct
    exchange = functools.partial(
        lax.all_to_all, axis_name="tile", split_axis=0, concat_axis=0, tiled=True
    )

    flat = ocean.reshape(planes * ocean_rows, columns)
    halo_shape = shape((4 * (planes + 1), columns), jnp.float32)
    sent, even, odd = pl.pallas_call(
        pack_kernel,
        out_shape=(
            shape((count, tracers * slots_in, LANES), jnp.bfloat16),
            halo_shape,
            halo_shape,
        ),
        in_specs=[smem(), smem(), vmem(), vmem()],
        out_specs=(vmem(), vmem(), vmem()),
        scratch_shapes=[
            pltpu.VMEM((tracers, (full + 1) * 8, LANES), jnp.float32),
            pltpu.VMEM((window, tracers * slots_in, LANES), jnp.float32),
            pltpu.VMEM((8, LANES), jnp.float32),
            pltpu.VMEM((full + 1, planes * ocean_rows, LANES), jnp.float32),
        ],
        compiler_params=params(),
        name="pack",
    )(me, send_tile, flat, kappa)

    even_pairs = [(i, i ^ 1) for i in range(count) if i ^ 1 < count]
    odd_pairs = [(i, i + 1) for i in range(1, count - 1, 2)]
    odd_pairs += [(b, a) for a, b in odd_pairs]
    received = exchange(sent)
    even = lax.ppermute(even, "tile", even_pairs)
    odd = lax.ppermute(odd, "tile", odd_pairs)

    swept = pl.pallas_call(
        functools.partial(sweeps_kernel, peers=count),
        out_shape=shape(flat.shape, jnp.float32),
        in_specs=[smem()] + [vmem()] * 5,
        out_specs=vmem(),
        scratch_shapes=[
            pltpu.VMEM((2, 16, planes, padded), jnp.float32),
            pltpu.VMEM((full + 1, 16, LANES), jnp.float32),
            pltpu.VMEM((8, padded), jnp.int32),
            pltpu.VMEM((full + 1, planes * ocean_rows, LANES), jnp.float32),
        ],
        compiler_params=params(),
        cost_estimate=pl.CostEstimate(flops=20_000_000, bytes_accessed=24_000_000, transcendentals=0),
        name="sweeps",
    )(me, flat, kappa, even, odd, fold_map.reshape(1, columns))

    weights = remap_w[0]
    w_spec = pl.BlockSpec((slots_in, LANES, LANES), lambda d: (d, 0, 0))

    def whole(*dims):
        return pl.BlockSpec(dims, lambda d: (0,) * len(dims))

    partial_sums = pl.pallas_call(
        forward_kernel,
        grid=(window,),
        out_shape=shape((count, tracers * slots_out, LANES), jnp.float32),
        in_specs=[
            smem(),
            smem(),
            whole(count, tracers * slots_in, LANES),
            whole(1, blocks),
            w_spec,
        ],
        out_specs=whole(count, tracers * slots_out, LANES),
        scratch_shapes=[pltpu.VMEM((tracers, blocks, LANES), jnp.float32)],
        compiler_params=params(),
        name="forward",
    )(me, slot_counts, received, out_slot, weights)
    owner_parts = exchange(partial_sums)

    tile_place = (out_tile % across) * atmos_rows + out_tile // across
    tile_place = tile_place.reshape(1, n_slots)
    tile_table = (tile_place.reshape(n_slots, 1) == jnp.arange(n_tiles)).astype(jnp.bfloat16)
    flux_sent, flux = pl.pallas_call(
        flux_kernel,
        grid=(1,),
        out_shape=(
            shape((count, tracers * slots_out, LANES), jnp.bfloat16),
            shape((tracers, atmos_rows, atmos_columns), jnp.float32),
        ),
        in_specs=[
            smem(),
            whole(count, tracers * slots_out, LANES),
            whole(1, n_slots),
            whole(n_slots, n_tiles),
            whole(tracers, 1, atmos_rows, atmos_columns),
            whole(atmos_rows, atmos_columns),
        ],
        out_specs=(
            whole(count, tracers * slots_out, LANES),
            whole(tracers, atmos_rows, atmos_columns),
        ),
        compiler_params=params(),
        name="flux",
    )(me, owner_parts, tile_place, tile_table, atmos, piston)
    at_coupler = exchange(flux_sent)

    atmos_next = pl.pallas_call(
        atmos_kernel,
        out_shape=shape(atmos.shape, jnp.float32),
        in_specs=[vmem()] * 3,
        out_specs=vmem(),
        compiler_params=params(),
        cost_estimate=pl.CostEstimate(flops=4_000_000, bytes_accessed=5_000_000, transcendentals=0),
        name="atmos",
    )(atmos, flux, atmos_mix)

    slot_table = (out_slot.reshape(blocks, 1) == jnp.arange(n_slots)).astype(jnp.bfloat16)
    back_sums = pl.pallas_call(
        backward_kernel,
        grid=(window,),
        out_shape=shape((count, tracers * slots_in, LANES), jnp.float32),
        in_specs=[
            smem(),
            smem(),
            whole(count, tracers * slots_out, LANES),
            whole(blocks, n_slots),
            w_spec,
        ],
        out_specs=whole(count, tracers * slots_in, LANES),
        scratch_shapes=[pltpu.VMEM((window, tracers * slots_in, LANES), jnp.bfloat16)],
        compiler_params=params(),
        name="backward",
    )(me, slot_counts, at_coupler, slot_table, weights)
    returned = exchange(back_sums)

    over = send_tile // full
    ocean_place = jnp.where(
        send_tile == 8 * full, 8 * full + 7, (send_tile - over * full) * 8 + over
    ).reshape(1, blocks)
    surface_spec = pl.BlockSpec(
        (tracers, 1, ocean_rows, columns), lambda d: (0, 0, 0, 0)
    )
    ocean_next = pl.pallas_call(
        add_kernel,
        grid=(1,),
        out_shape=shape(ocean.shape, jnp.float32),
        in_specs=[
            smem(),
            whole(count, tracers * slots_in, LANES),
            whole(1, blocks),
            surface_spec,
        ],
        out_specs=surface_spec,
        input_output_aliases={3: 0},
        compiler_params=params(),
        name="add",
    )(me, returned, ocean_place, swept.reshape(ocean.shape))
    return (ocean_next, atmos_next)


def solution(mesh):
    placed = (
        P("member", None, "tile", None),
        P("tile", None),
        P("member", None, "tile", None),
        P("tile", None),
        P("tile", None),
        P(),
        P("tile", None, None),
        P("tile", None),
        P("tile", None),
        P("tile", None, None),
        P("tile", None, None, None),
    )
    return jax.shard_map(
        local,
        mesh=mesh,
        in_specs=placed,
        out_specs=(P("member", None, "tile", None), P("member", None, "tile", None)),
        check_vma=False,
    )
```

```python
import functools

import jax
import jax.numpy as jnp
from jax import lax
from jax.experimental import pallas as pl
from jax.experimental.pallas import tpu as pltpu
from jax.sharding import PartitionSpec as P

OSTEPS = 4
ASTEPS = 4
LANES = 128

vertical_mix = 0.1
ocean_rate = 4.0
atmos_rate = 0.5
solubility = 1.2

MIB = 1024 * 1024


def params(mib=16):
    return pltpu.CompilerParams(vmem_limit_bytes=36 * MIB)


def vmem():
    return pl.BlockSpec(memory_space=pltpu.VMEM)


def smem():
    return pl.BlockSpec(memory_space=pltpu.SMEM)


def hbm():
    return pl.BlockSpec(memory_space=pltpu.HBM)


def anywhere():
    return pl.BlockSpec(memory_space=pl.ANY)


def iota(shape, dim):
    return lax.broadcasted_iota(jnp.int32, shape, dim)


def split_dot(table, values, dims):
    high = values.astype(jnp.bfloat16)
    low = (values - high.astype(jnp.float32)).astype(jnp.bfloat16)
    dot = functools.partial(
        lax.dot_general, dimension_numbers=(dims, ((), ())), preferred_element_type=jnp.float32
    )
    return dot(table, high) + dot(table, low)


def shear(tile, sign, shift):
    lane = iota(tile.shape, 1)
    row = iota(tile.shape, 0)
    source = (lane - sign * shift * row) & (LANES - 1)
    return jnp.take_along_axis(tile, source, axis=1, mode="promise_in_bounds")


def widths(columns):
    return [(c, min(LANES, columns - c)) for c in range(0, columns, LANES)]


def in_hbm(x):
    return pltpu.with_memory_space_constraint(x, pltpu.HBM)


def one_hot(mask):
    return jnp.where(mask, 1.0, 0.0).astype(jnp.bfloat16)


def pack_kernel(me_ref, send_hbm, ocean_hbm, out_ref, token, send, surface, tiles, rows, sems):
    me = me_ref[0]
    peers = out_ref.shape[0]
    _, window, slots = send.shape
    tracers, _, columns = surface.shape
    copies = [pltpu.make_async_copy(send_hbm, send, sems.at[tracers])]
    for t in range(tracers):
        copies.append(pltpu.make_async_copy(ocean_hbm.at[t, 0], surface.at[t], sems.at[t]))
    for copy in copies:
        copy.start()
    out_ref[...] = jnp.zeros_like(out_ref)
    token[...] = jnp.zeros_like(token)
    cuts = widths(columns)
    full = len(cuts) - 1
    rest = cuts[-1][1]
    lane = iota((8, LANES), 1)
    row = iota((8, LANES), 0)
    wraps = lane < rest * row
    for t in range(tracers):
        copies[1 + t].wait()
        before = jnp.zeros((8, LANES), jnp.float32)
        first = None
        for k, (start, width) in enumerate(cuts):
            part = surface[t, :, start : start + width]
            if width < LANES:
                part = jnp.concatenate(
                    [part, jnp.zeros((8, LANES - width), jnp.float32)], axis=1
                )
            turned = shear(part, 1, rest)
            value = jnp.where(wraps, before, turned)
            before = turned
            if k == 0:
                first = value
            else:
                tiles[t, k * 8 : (k + 1) * 8] = value
        tiles[t, 0:8] = jnp.where(wraps, pltpu.roll(value, 1, 0), first)
    copies[0].wait()
    for d in range(window):
        for k in range(slots):
            index = send[0, d, k]
            over = index // full
            place = jnp.where(index == 8 * full, 8 * full + 7, (index - over * full) * 8 + over)
            for t in range(tracers):
                rows[d, pl.ds(t * slots + k, 1), :] = tiles[t, pl.ds(place, 1), :]
    for d in range(window):
        peer = me + d - window // 2

        @pl.when((peer >= 0) & (peer < peers))
        def _():
            out_ref[peer] = rows[d].astype(jnp.bfloat16)


def halo_kernel(
    me_ref, after, ocean_hbm, kappa_hbm, even_ref, odd_ref, ocean, kappa, grouped, sems
):
    odd = lax.rem(me_ref[0], 2)
    planes = ocean.shape[0] // 8
    cuts = widths(ocean.shape[1])
    copies = [
        pltpu.make_async_copy(ocean_hbm, ocean, sems.at[0]),
        pltpu.make_async_copy(kappa_hbm, kappa, sems.at[1]),
    ]
    for copy in copies:
        copy.start()
    for copy in copies:
        copy.wait()
    for k, (start, width) in enumerate(cuts):
        grouped[k, :, :width] = ocean[:, start : start + width]
    for target, base in ((even_ref, 4 * (1 - odd)), (odd_ref, 4 * odd)):
        for k, (start, width) in enumerate(cuts):
            at = slice(start, start + LANES)
            for r in range(4):
                part = grouped[k, pl.ds(base + r, planes, stride=8), :]
                target[r * planes : (r + 1) * planes, at] = part

    @pl.when(odd == 0)
    def _():
        for start, width in cuts:
            at = slice(start, start + width)
            even_ref[4 * planes : 4 * planes + 4, at] = kappa[4:8, at]
            odd_ref[4 * planes : 4 * planes + 4, at] = kappa[0:4, at]

    @pl.when(odd == 1)
    def _():
        for start, width in cuts:
            at = slice(start, start + width)
            even_ref[4 * planes : 4 * planes + 4, at] = kappa[0:4, at]
            odd_ref[4 * planes : 4 * planes + 4, at] = kappa[4:8, at]


def prepare_kernel(
    me_ref,
    counts_ref,
    after,
    slot_ref,
    tile_place_ref,
    ocean_place_ref,
    atmos_hbm,
    piston_hbm,
    sum_ref,
    pick_ref,
    spread_ref,
    flux_pick_ref,
    scatter_ref,
    air_ref,
    rate_ref,
    surface,
    piston,
    sems,
):
    tracers, rows, columns = surface.shape
    copies = [pltpu.make_async_copy(piston_hbm, piston, sems.at[tracers])]
    for t in range(tracers):
        copies.append(pltpu.make_async_copy(atmos_hbm.at[t, 0], surface.at[t], sems.at[t]))
    for copy in copies:
        copy.start()
    n_slots, blocks = sum_ref.shape
    window = counts_ref.shape[1]
    slots = blocks // window
    at = iota((1, blocks), 1)
    live = at < 0
    for d in range(window):
        live = live | ((at >= d * slots) & (at < d * slots + counts_ref[0, d]))
    table = jnp.where((iota((LANES, blocks), 0) == slot_ref[...]) & live, 1.0, 0.0)
    sum_ref[...] = table[:n_slots].astype(jnp.bfloat16)
    pick_ref[...] = table.T[:, :n_slots].astype(jnp.bfloat16)
    spread = jnp.where(iota((LANES, LANES), 0) == tile_place_ref[...], 1.0, 0.0)
    n_tiles = spread_ref.shape[0]
    spread_ref[...] = spread[:n_tiles, :n_slots].astype(jnp.bfloat16)
    flux_pick_ref[...] = spread.T[:n_slots, :n_tiles].astype(jnp.bfloat16)
    scatter_ref[...] = one_hot(iota(scatter_ref.shape, 0) == ocean_place_ref[...])
    for copy in copies:
        copy.wait()
    for k in range(columns // LANES):
        at = slice(k * LANES, (k + 1) * LANES)
        rate_ref[k * rows : (k + 1) * rows, :] = piston[:, at]
        for t in range(tracers):
            air_ref[t, k * rows : (k + 1) * rows, :] = surface[t, :, at]


def fold_tables(last, fold_hbm, fold, table_ref, sem):
    @pl.when(last)
    def _():
        copy = pltpu.make_async_copy(fold_hbm, fold, sem)
        copy.start()
        copy.wait()
        inner = iota((table_ref.shape[0], LANES), 0) & (LANES - 1)
        for start, width in widths(fold.shape[1]):
            at = slice(start, start + width)
            found = one_hot(inner[:, :width] == (fold[:, at] & (LANES - 1)))
            table_ref[:, at] = found


def fold_row(state, table_ref, fold, cuts):
    tiles = len(cuts)
    rest = cuts[-1][1]
    rows = [state[11, :, start : start + LANES] for start, _ in cuts]
    rows[-1] = jnp.where(iota((8, LANES), 1) < rest, rows[-1], 0.0)
    rows = jnp.concatenate(rows, axis=0)
    high = rows.astype(jnp.bfloat16)
    low = (rows - high.astype(jnp.float32)).astype(jnp.bfloat16)
    parts = jnp.concatenate([high, low], axis=1)
    for start, width in cuts:
        at = slice(start, start + width)
        table = table_ref[:, start : start + LANES]
        found = jnp.dot(parts, table, preferred_element_type=jnp.float32)
        outer = jnp.broadcast_to(fold[:, at] >> 7, (8, width))
        value = found[0:8, :width]
        for k in range(1, tiles):
            value = jnp.where(outer == k, found[k * 8 : (k + 1) * 8, :width], value)
        state[12, :, at] = value


def sweep_rows(state, kap, cuts, levels, low, high, write):
    full = len(cuts) - 1
    rest = cuts[-1][1]
    lane = iota((8, LANES), 1)
    level = iota((8, LANES), 0) & (levels - 1)

    def body(r, carry):
        def cell(k):
            return state[r, :, k * LANES : (k + 1) * LANES]

        centre = cell(0)
        east_now = pltpu.roll(centre, LANES - 1, 1)
        around = pltpu.roll(centre, rest - 1, 1)
        west_last = pltpu.roll(cell(full), LANES - rest + 1, 1)
        for k in range(full + 1):
            at = slice(k * LANES, (k + 1) * LANES)
            if k == full:
                east = jnp.where(lane == rest - 1, around, east_now)
            else:
                following = cell(k + 1)
                east_next = pltpu.roll(following, LANES - 1, 1)
                east = jnp.where(lane == LANES - 1, east_next, east_now)
            west_now = pltpu.roll(centre, 1, 1)
            west = jnp.where(lane == 0, west_last, west_now)
            north = state[r + 1, :, at]
            south = state[r - 1, :, at]
            upper = jnp.where(level == 0, centre, pltpu.roll(centre, 1, 0))
            lower = jnp.where(level == levels - 1, centre, pltpu.roll(centre, 7, 0))
            horizontal = (north + south) + (east + west) - 4.0 * centre
            vertical = upper + lower - 2.0 * centre
            rate = kap[k, pl.ds(r, 1), :]
            write(r, k, centre + rate * horizontal + vertical_mix * vertical)
            if k < full:
                centre, east_now, west_last = following, east_next, west_now
        return carry

    lax.fori_loop(low, high, body, 0)


def keep(target):
    def write(r, k, value):
        target[r, :, k * LANES : (k + 1) * LANES] = value

    return write


def first_sweep_kernel(
    me_ref,
    after,
    ocean_hbm,
    kappa_hbm,
    even_hbm,
    odd_hbm,
    fold_hbm,
    out_ref,
    kap_ref,
    token,
    state,
    ocean,
    kappa,
    above,
    below,
    grouped,
    table,
    fold,
    sems,
    levels,
    peers,
):
    me = me_ref[0]
    last = me == peers - 1
    odd = lax.rem(me, 2)
    token[...] = jnp.zeros_like(token)
    planes = state.shape[1]
    cuts = widths(kappa.shape[1])
    copies = [
        pltpu.make_async_copy(ocean_hbm, ocean, sems.at[0]),
        pltpu.make_async_copy(kappa_hbm, kappa, sems.at[1]),
    ]
    for copy in copies:
        copy.start()

    @pl.when(odd == 1)
    def _():
        pltpu.make_async_copy(odd_hbm, above, sems.at[2]).start()
        pltpu.make_async_copy(even_hbm, below, sems.at[3]).start()

    @pl.when(odd == 0)
    def _():
        pltpu.make_async_copy(even_hbm, above, sems.at[2]).start()
        pltpu.make_async_copy(odd_hbm, below, sems.at[3]).start()

    fold_tables(last, fold_hbm, fold, table, sems.at[4])
    for copy in copies:
        copy.wait()
    for k, (start, width) in enumerate(cuts):
        grouped[k, :, :width] = ocean[:, start : start + width]
        kap_ref[k, 4:12, :width] = kappa[:, start : start + width]
    for k, (start, width) in enumerate(cuts):
        for r in range(8):
            part = grouped[k, pl.ds(r, planes, stride=8), :]
            state[4 + r, :, start : start + LANES] = part

    @pl.when(last)
    def _():
        fold_row(state, table, fold, cuts)

    pltpu.make_async_copy(even_hbm, above, sems.at[2]).wait()
    pltpu.make_async_copy(odd_hbm, below, sems.at[3]).wait()
    for r in range(4):
        state[r] = below[r * planes : (r + 1) * planes, :]

    @pl.when(jnp.logical_not(last))
    def _():
        for r in range(4):
            state[12 + r] = above[r * planes : (r + 1) * planes, :]

    for k, (start, _) in enumerate(cuts):
        at = slice(start, start + LANES)
        kap_ref[k, 0:4, :] = below[4 * planes : 4 * planes + 4, at]
        kap_ref[k, 12:16, :] = above[4 * planes : 4 * planes + 4, at]
    sweep_rows(state, kap_ref, cuts, levels, 1, 15, keep(out_ref))


def middle_sweeps_kernel(
    me_ref,
    after,
    state_ref,
    kap_ref,
    fold_hbm,
    out_ref,
    token,
    state,
    table,
    fold,
    sem,
    levels,
    peers,
):
    token[...] = jnp.zeros_like(token)
    cuts = widths(fold.shape[1])
    last = me_ref[0] == peers - 1
    fold_tables(last, fold_hbm, fold, table, sem)
    state[1:15] = state_ref[1:15]

    @pl.when(last)
    def _():
        fold_row(state, table, fold, cuts)

    sweep_rows(state, kap_ref, cuts, levels, 2, 14, keep(out_ref))

    @pl.when(last)
    def _():
        fold_row(out_ref, table, fold, cuts)

    sweep_rows(out_ref, kap_ref, cuts, levels, 3, 13, keep(state))
    out_ref[3:13] = state[3:13]


def last_sweep_kernel(
    me_ref,
    after,
    state_ref,
    kap_ref,
    fold_hbm,
    out_ref,
    state,
    grouped,
    table,
    fold,
    sem,
    levels,
    peers,
):
    columns = out_ref.shape[1]
    cuts = widths(columns)
    planes = state_ref.shape[1]
    last = me_ref[0] == peers - 1
    fold_tables(last, fold_hbm, fold, table, sem)
    state[3:13] = state_ref[3:13]

    @pl.when(last)
    def _():
        fold_row(state, table, fold, cuts)

    def write(r, k, value):
        grouped[k, pl.ds(r - 4, planes, stride=8), :] = value

    sweep_rows(state, kap_ref, cuts, levels, 4, 12, write)
    for k, (start, width) in enumerate(cuts):
        out_ref[:, start : start + width] = grouped[k, :, :width]


def weight_copies(w_hbm, w_ref, sems, slots):
    copies = []
    for d in range(w_ref.shape[0] // slots):
        part = pl.ds(d * slots, slots)
        copies.append(pltpu.make_async_copy(w_hbm.at[part], w_ref.at[part], sems.at[d]))
        copies[-1].start()
    return copies


def forward_kernel(me_ref, recv_ref, sum_ref, w_hbm, out_ref, token, sums, w_ref, sems):
    token[...] = jnp.zeros_like(token)
    me = me_ref[0]
    peers = recv_ref.shape[0]
    tracers, blocks, _ = sums.shape
    n_slots = sum_ref.shape[0]
    window = n_slots // 8
    slots = blocks // window
    copies = weight_copies(w_hbm, w_ref, sems, slots)
    row = iota((8, LANES), 0)
    out_ref[...] = jnp.zeros_like(out_ref)
    for d in range(window):
        copies[d].wait()
        cells = recv_ref[jnp.clip(me - d + window // 2, 0, peers - 1)]
        weights = w_ref[d * slots : (d + 1) * slots].reshape(slots * LANES, LANES)
        product = lax.dot_general(
            cells, weights, (((1,), (1,)), ((), ())), preferred_element_type=jnp.float32
        )
        for t in range(tracers):
            for half in range(0, slots, 8):
                top = t * slots + half
                found = product[top : top + 8, half * LANES : (half + 1) * LANES]
                for k in range(1, 8):
                    at = slice((half + k) * LANES, (half + k + 1) * LANES)
                    found = jnp.where(row == k, product[top : top + 8, at], found)
                sums[t, d * slots + half : d * slots + half + 8, :] = found
    partial_sums = [split_dot(sum_ref[...], sums[t], ((1,), (0,))) for t in range(tracers)]
    for g in range(window):
        peer = me + g - window // 2

        @pl.when((peer >= 0) & (peer < peers))
        def _():
            for t in range(tracers):
                out_ref[peer, t * 8 : (t + 1) * 8, :] = partial_sums[t][g * 8 : (g + 1) * 8]


def flux_kernel(
    me_ref, after, parts_ref, spread_ref, pick_ref, air_ref, rate_ref, send_ref, flux_ref, token
):
    token[...] = jnp.zeros_like(token)
    me = me_ref[0]
    peers = parts_ref.shape[0]
    tracers, rows, columns = flux_ref.shape
    n_slots = spread_ref.shape[1]
    window = n_slots // 8
    send_ref[...] = jnp.zeros_like(send_ref)
    sent = []
    for t in range(tracers):
        parts = []
        for g in range(window):
            coupler = me - g + window // 2
            valid = (coupler >= 0) & (coupler < peers)
            block = parts_ref[jnp.clip(coupler, 0, peers - 1), t * 8 : (t + 1) * 8, :]
            parts.append(jnp.where(valid, block, 0.0))
        remapped = split_dot(spread_ref[...], jnp.concatenate(parts, axis=0), ((1,), (0,)))
        flux = rate_ref[...] * (solubility * air_ref[t] - remapped)
        for k in range(columns // LANES):
            flux_ref[t, :, k * LANES : (k + 1) * LANES] = flux[k * rows : (k + 1) * rows]
        sent.append(
            jnp.dot(pick_ref[...], flux.astype(jnp.bfloat16), preferred_element_type=jnp.float32)
        )
    for g in range(window):
        peer = me - g + window // 2

        @pl.when((peer >= 0) & (peer < peers))
        def _():
            block = jnp.concatenate([s[g * 8 : (g + 1) * 8] for s in sent], axis=0)
            send_ref[peer] = block.astype(jnp.bfloat16)


def backward_kernel(me_ref, after, recv_ref, pick_ref, w_hbm, out_ref, token, w_ref, sems):
    token[...] = jnp.zeros_like(token)
    me = me_ref[0]
    peers, width, _ = recv_ref.shape
    tracers = width // 8
    blocks, n_slots = pick_ref.shape
    window = n_slots // 8
    slots = blocks // window
    copies = weight_copies(w_hbm, w_ref, sems, slots)
    parts = [[] for _ in range(tracers)]
    for g in range(window):
        owner = me + g - window // 2
        valid = (owner >= 0) & (owner < peers)
        block = recv_ref[jnp.clip(owner, 0, peers - 1)].astype(jnp.float32)
        block = jnp.where(valid, block, 0.0)
        for t in range(tracers):
            parts[t].append(block[t * 8 : (t + 1) * 8])
    picked = [
        jnp.dot(
            pick_ref[...],
            jnp.concatenate(parts[t], axis=0).astype(jnp.bfloat16),
            preferred_element_type=jnp.float32,
        )
        for t in range(tracers)
    ]
    out_ref[...] = jnp.zeros_like(out_ref)
    row = iota((slots, LANES), 0)
    for d in range(window):
        part = slice(d * slots, (d + 1) * slots)
        mine = [p[part] for p in picked]
        cells = jnp.concatenate(
            [
                jnp.concatenate([jnp.where(row == k, m, 0.0) for m in mine], axis=0).astype(
                    jnp.bfloat16
                )
                for k in range(slots)
            ],
            axis=1,
        )
        copies[d].wait()
        weights = w_ref[part].reshape(slots * LANES, LANES)
        product = jnp.dot(cells, weights, preferred_element_type=jnp.float32)
        peer = me - d + window // 2

        @pl.when((peer >= 0) & (peer < peers))
        def _():
            out_ref[peer] = product


def add_kernel(me_ref, returned_ref, table_ref, swept, out, buffer, surface, sems):
    me = me_ref[0]
    peers = returned_ref.shape[0]
    tracers, _, columns = surface.shape
    loads = []
    for t in range(tracers):
        loads.append(pltpu.make_async_copy(swept.at[t, 0], surface.at[t], sems.at[tracers + t]))
        loads[-1].start()
    slots = returned_ref.shape[1] // tracers
    window = table_ref.shape[1] // slots
    cuts = widths(columns)
    full = len(cuts) - 1
    rest = cuts[-1][1]
    lane = iota((8, LANES), 1)
    row = iota((8, LANES), 0)
    stays = lane < LANES - rest * row
    copies = []
    for t in range(tracers):
        parts = []
        for d in range(window):
            coupler = me + d - window // 2
            valid = (coupler >= 0) & (coupler < peers)
            block = returned_ref[jnp.clip(coupler, 0, peers - 1), t * slots : (t + 1) * slots, :]
            parts.append(jnp.where(valid, block, 0.0))
        tiles = split_dot(table_ref[...], jnp.concatenate(parts, axis=0), ((1,), (0,)))
        rows = [tiles[k * 8 : (k + 1) * 8] for k in range(full + 1)]
        rows[full] = jnp.where(row == 7, rows[full], pltpu.roll(rows[0], 7, 0))
        turned = [shear(value, -1, rest) for value in rows]
        loads[t].wait()
        for k, (start, width) in enumerate(cuts):
            value = turned[k]
            if k < full:
                value = jnp.where(stays, value, turned[k + 1])
            at = slice(start, start + width)
            buffer[t, :, at] = surface[t, :, at] + ocean_rate * value[:, :width]
        copies.append(pltpu.make_async_copy(buffer.at[t], out.at[t, 0], sems.at[t]))
        copies[-1].start()
    for copy in copies:
        copy.wait()


def atmos_kernel(atmos_ref, flux_ref, mix_ref, out_ref):
    tracers, levels, rows, columns = atmos_ref.shape
    for t in range(tracers):
        for r in range(0, rows, 8):
            for c in range(0, columns, LANES):
                at = (slice(r, r + 8), slice(c, c + LANES))
                mixing = mix_ref[at]
                field = [atmos_ref[(t, v) + at] for v in range(levels)]
                field[0] = field[0] - atmos_rate * flux_ref[(t,) + at]
                for _ in range(ASTEPS):
                    field = [
                        field[v]
                        + mixing
                        * (field[max(v - 1, 0)] + field[min(v + 1, levels - 1)] - 2.0 * field[v])
                        for v in range(levels)
                    ]
                for v in range(levels):
                    out_ref[(t, v) + at] = field[v]


def local(
    ocean,
    kappa,
    atmos,
    piston,
    atmos_mix,
    fold_map,
    send_tile,
    slot_counts,
    out_slot,
    out_tile,
    remap_w,
):
    count = lax.axis_size("tile")
    me = lax.axis_index("tile").astype(jnp.int32).reshape(1)
    tracers, levels, ocean_rows, columns = ocean.shape
    planes = tracers * levels
    window, slots_in = send_tile.shape[1:]
    slots_out = out_tile.shape[2]
    blocks = window * slots_in
    n_slots = window * slots_out
    tiles = -(-columns // LANES)
    full = columns // LANES
    padded = -(-columns // (2 * LANES)) * 2 * LANES
    atmos_rows, atmos_columns = atmos.shape[2:]
    across = atmos_columns // LANES
    n_tiles = atmos_rows * across
    f32, bf16, i32 = jnp.float32, jnp.bfloat16, jnp.int32
    shape = jax.ShapeDtypeStruct
    dma = pltpu.SemaphoreType.DMA
    exchange = functools.partial(
        lax.all_to_all, axis_name="tile", split_axis=0, concat_axis=0, tiled=True
    )

    def cost(us):
        return pl.CostEstimate(
            flops=0, bytes_accessed=int(us * 3.0e6), transcendentals=0
        )

    token_shape = shape((8, LANES), f32)
    sent, token = pl.pallas_call(
        pack_kernel,
        out_shape=(pltpu.HBM((count, tracers * slots_in, LANES), bf16), token_shape),
        in_specs=[smem(), hbm(), hbm()],
        out_specs=(vmem(), vmem()),
        scratch_shapes=[
            pltpu.SMEM(send_tile.shape, i32),
            pltpu.VMEM((tracers, ocean_rows, columns), f32),
            pltpu.VMEM((tracers, tiles * 8, LANES), f32),
            pltpu.VMEM((window, tracers * slots_in, LANES), f32),
            dma((tracers + 1,)),
        ],
        compiler_params=params(),
        name="pack",
    )(me, in_hbm(send_tile), in_hbm(ocean))
    received = exchange(sent)

    halo_rows = 4 * planes + 8
    flat = in_hbm(ocean.reshape(planes * ocean_rows, columns))
    even, odd = pl.pallas_call(
        halo_kernel,
        out_shape=(shape((halo_rows, padded), f32), shape((halo_rows, padded), f32)),
        in_specs=[smem(), vmem(), hbm(), hbm()],
        out_specs=(vmem(),) * 2,
        scratch_shapes=[
            pltpu.VMEM((planes * ocean_rows, columns), f32),
            pltpu.VMEM((ocean_rows, columns), f32),
            pltpu.VMEM((tiles, planes * ocean_rows, LANES), f32),
            dma((2,)),
        ],
        compiler_params=params(),
        cost_estimate=cost(2),
        name="halo",
    )(me, token, flat, in_hbm(kappa))
    even_pairs = [(i, i ^ 1) for i in range(count) if i ^ 1 < count]
    odd_pairs = [(i, i + 1) for i in range(1, count - 1, 2)]
    odd_pairs += [(b, a) for a, b in odd_pairs]
    even = lax.ppermute(even, "tile", even_pairs)
    odd = lax.ppermute(odd, "tile", odd_pairs)

    tile_place = (out_tile % across) * atmos_rows + out_tile // across
    tile_place = jnp.pad(tile_place.reshape(1, n_slots), ((0, 0), (0, LANES - n_slots)))
    over = send_tile // full
    ocean_place = jnp.where(
        send_tile == 8 * full, 8 * full + 7, (send_tile - over * full) * 8 + over
    ).reshape(1, blocks)
    sum_table, slot_pick, spread, flux_pick, scatter, air, rate = pl.pallas_call(
        prepare_kernel,
        out_shape=(
            shape((n_slots, blocks), bf16),
            shape((blocks, n_slots), bf16),
            shape((n_tiles, n_slots), bf16),
            shape((n_slots, n_tiles), bf16),
            shape((tiles * 8, blocks), bf16),
            shape((tracers, n_tiles, LANES), f32),
            shape((n_tiles, LANES), f32),
        ),
        in_specs=[smem(), smem()] + [vmem()] * 4 + [hbm()] * 2,
        out_specs=(vmem(),) * 7,
        scratch_shapes=[
            pltpu.VMEM((tracers, atmos_rows, atmos_columns), f32),
            pltpu.VMEM((atmos_rows, atmos_columns), f32),
            dma((tracers + 1,)),
        ],
        compiler_params=params(),
        cost_estimate=cost(1.5),
        name="prepare",
    )(
        me,
        slot_counts,
        token,
        out_slot,
        tile_place,
        ocean_place,
        in_hbm(atmos),
        in_hbm(piston),
    )

    weights = in_hbm(remap_w[0])
    weight_scratch = [pltpu.VMEM(remap_w.shape[1:], bf16), dma((window,))]
    partial_sums, token = pl.pallas_call(
        forward_kernel,
        out_shape=(pltpu.HBM((count, tracers * slots_out, LANES), f32), token_shape),
        in_specs=[smem(), vmem(), vmem(), hbm()],
        out_specs=(vmem(), vmem()),
        scratch_shapes=[pltpu.VMEM((tracers, blocks, LANES), f32)] + weight_scratch,
        compiler_params=params(),
        name="forward",
    )(me, received, sum_table, weights)
    owner_parts = exchange(partial_sums)

    state_shape = (16, planes, padded)
    fold = in_hbm(fold_map.reshape(1, columns))
    fold_scratch = [pltpu.VMEM((2 * LANES, padded), bf16), pltpu.VMEM((1, columns), i32)]
    state, kap, token = pl.pallas_call(
        functools.partial(first_sweep_kernel, levels=levels, peers=count),
        out_shape=(shape(state_shape, f32), shape((tiles, 16, LANES), f32), token_shape),
        in_specs=[smem(), vmem()] + [hbm()] * 5,
        out_specs=(vmem(),) * 3,
        scratch_shapes=[
            pltpu.VMEM(state_shape, f32),
            pltpu.VMEM((planes * ocean_rows, columns), f32),
            pltpu.VMEM((ocean_rows, columns), f32),
            pltpu.VMEM((halo_rows, padded), f32),
            pltpu.VMEM((halo_rows, padded), f32),
            pltpu.VMEM((tiles, planes * ocean_rows, LANES), f32),
        ]
        + fold_scratch
        + [dma((5,))],
        compiler_params=params(),
        cost_estimate=cost(5),
        name="first_sweep",
    )(me, token, flat, in_hbm(kappa), in_hbm(even), in_hbm(odd), fold)

    flux_sent, flux, token = pl.pallas_call(
        flux_kernel,
        out_shape=(
            pltpu.HBM((count, tracers * slots_out, LANES), bf16),
            shape((tracers, atmos_rows, atmos_columns), f32),
            token_shape,
        ),
        in_specs=[smem()] + [vmem()] * 6,
        out_specs=(vmem(),) * 3,
        compiler_params=params(),
        name="flux",
    )(me, token, owner_parts, spread, flux_pick, air, rate)
    at_coupler = exchange(flux_sent)

    state, token = pl.pallas_call(
        functools.partial(middle_sweeps_kernel, levels=levels, peers=count),
        out_shape=(shape(state_shape, f32), token_shape),
        in_specs=[smem()] + [vmem()] * 3 + [hbm()],
        out_specs=(vmem(), vmem()),
        scratch_shapes=[pltpu.VMEM(state_shape, f32)] + fold_scratch + [dma(())],
        compiler_params=params(),
        cost_estimate=cost(6),
        name="middle_sweeps",
    )(me, token, state, kap, fold)

    back_sums, token = pl.pallas_call(
        backward_kernel,
        out_shape=(pltpu.HBM((count, tracers * slots_in, LANES), f32), token_shape),
        in_specs=[smem()] + [vmem()] * 3 + [hbm()],
        out_specs=(vmem(), vmem()),
        scratch_shapes=weight_scratch,
        compiler_params=params(),
        name="backward",
    )(me, token, at_coupler, slot_pick, weights)
    returned = exchange(back_sums)

    swept = pl.pallas_call(
        functools.partial(last_sweep_kernel, levels=levels, peers=count),
        out_shape=shape((planes * ocean_rows, columns), f32),
        in_specs=[smem()] + [vmem()] * 3 + [hbm()],
        out_specs=vmem(),
        scratch_shapes=[
            pltpu.VMEM(state_shape, f32),
            pltpu.VMEM((tiles, planes * ocean_rows, LANES), f32),
        ]
        + fold_scratch
        + [dma(())],
        compiler_params=params(),
        cost_estimate=cost(4),
        name="last_sweep",
    )(me, token, state, kap, fold)
    atmos_next = pl.pallas_call(
        atmos_kernel,
        out_shape=shape(atmos.shape, f32),
        in_specs=[vmem()] * 3,
        out_specs=vmem(),
        compiler_params=params(),
        cost_estimate=cost(1),
        name="atmos",
    )(atmos, flux, atmos_mix)

    ocean_next = pl.pallas_call(
        add_kernel,
        out_shape=shape(ocean.shape, f32),
        in_specs=[smem()] + [vmem()] * 2 + [hbm()],
        out_specs=hbm(),
        scratch_shapes=[
            pltpu.VMEM((tracers, ocean_rows, columns), f32),
            pltpu.VMEM((tracers, ocean_rows, columns), f32),
            dma((2 * tracers,)),
        ],
        input_output_aliases={3: 0},
        compiler_params=params(),
        name="add",
    )(me, returned, scatter, in_hbm(swept.reshape(ocean.shape)))
    return (ocean_next, atmos_next)


def solution(mesh):
    placed = (
        P("member", None, "tile", None),
        P("tile", None),
        P("member", None, "tile", None),
        P("tile", None),
        P("tile", None),
        P(),
        P("tile", None, None),
        P("tile", None),
        P("tile", None),
        P("tile", None, None),
        P("tile", None, None, None),
    )
    return jax.shard_map(
        local,
        mesh=mesh,
        in_specs=placed,
        out_specs=(P("member", None, "tile", None), P("member", None, "tile", None)),
        check_vma=False,
    )
```

```python
import functools

import jax
import jax.numpy as jnp
from jax import lax
from jax.experimental import pallas as pl
from jax.experimental.pallas import tpu as pltpu
from jax.sharding import PartitionSpec as P

OSTEPS = 4
ASTEPS = 4
LANES = 128
HELD = 5

vertical_mix = 0.1
ocean_rate = 4.0
atmos_rate = 0.5
solubility = 1.2

MIB = 1024 * 1024


def params(mib=16):
    return pltpu.CompilerParams(vmem_limit_bytes=36 * MIB)


def vmem():
    return pl.BlockSpec(memory_space=pltpu.VMEM)


def smem():
    return pl.BlockSpec(memory_space=pltpu.SMEM)


def hbm():
    return pl.BlockSpec(memory_space=pltpu.HBM)


def anywhere():
    return pl.BlockSpec(memory_space=pl.ANY)


def iota(shape, dim):
    return lax.broadcasted_iota(jnp.int32, shape, dim)


def split_dot(table, values, dims):
    high = values.astype(jnp.bfloat16)
    low = (values - high.astype(jnp.float32)).astype(jnp.bfloat16)
    dot = functools.partial(
        lax.dot_general, dimension_numbers=(dims, ((), ())), preferred_element_type=jnp.float32
    )
    return dot(table, high) + dot(table, low)


def shear(tile, sign, shift):
    lane = iota(tile.shape, 1)
    row = iota(tile.shape, 0)
    source = (lane - sign * shift * row) & (LANES - 1)
    return jnp.take_along_axis(tile, source, axis=1, mode="promise_in_bounds")


def widths(columns):
    return [(c, min(LANES, columns - c)) for c in range(0, columns, LANES)]


def in_hbm(x):
    return pltpu.with_memory_space_constraint(x, pltpu.HBM)


def one_hot(mask):
    return jnp.where(mask, 1.0, 0.0).astype(jnp.bfloat16)


def pack_kernel(me_ref, send_hbm, ocean_hbm, out_ref, token, send, surface, tiles, rows, sems):
    me = me_ref[0]
    peers = out_ref.shape[0]
    _, window, slots = send.shape
    tracers, _, columns = surface.shape
    copies = [pltpu.make_async_copy(send_hbm, send, sems.at[tracers])]
    for t in range(tracers):
        copies.append(pltpu.make_async_copy(ocean_hbm.at[t, 0], surface.at[t], sems.at[t]))
    for copy in copies:
        copy.start()
    out_ref[...] = jnp.zeros_like(out_ref)
    token[...] = jnp.zeros_like(token)
    cuts = widths(columns)
    full = len(cuts) - 1
    rest = cuts[-1][1]
    lane = iota((8, LANES), 1)
    row = iota((8, LANES), 0)
    wraps = lane < rest * row
    for t in range(tracers):
        copies[1 + t].wait()
        before = jnp.zeros((8, LANES), jnp.float32)
        first = None
        for k, (start, width) in enumerate(cuts):
            part = surface[t, :, start : start + width]
            if width < LANES:
                part = jnp.concatenate(
                    [part, jnp.zeros((8, LANES - width), jnp.float32)], axis=1
                )
            turned = shear(part, 1, rest)
            value = jnp.where(wraps, before, turned)
            before = turned
            if k == 0:
                first = value
            else:
                tiles[t, k * 8 : (k + 1) * 8] = value
        tiles[t, 0:8] = jnp.where(wraps, pltpu.roll(value, 1, 0), first)
    copies[0].wait()
    for d in range(window):
        for k in range(slots):
            index = send[0, d, k]
            over = index // full
            place = jnp.where(index == 8 * full, 8 * full + 7, (index - over * full) * 8 + over)
            for t in range(tracers):
                rows[d, pl.ds(t * slots + k, 1), :] = tiles[t, pl.ds(place, 1), :]
    for d in range(window):
        peer = me + d - window // 2

        @pl.when((peer >= 0) & (peer < peers))
        def _():
            out_ref[peer] = rows[d].astype(jnp.bfloat16)


def halo_kernel(
    me_ref, after, ocean_hbm, kappa_hbm, even_ref, odd_ref, ocean, kappa, grouped, sems
):
    odd = lax.rem(me_ref[0], 2)
    planes = ocean.shape[0] // 8
    cuts = widths(ocean.shape[1])
    copies = [
        pltpu.make_async_copy(ocean_hbm, ocean, sems.at[0]),
        pltpu.make_async_copy(kappa_hbm, kappa, sems.at[1]),
    ]
    for copy in copies:
        copy.start()
    for copy in copies:
        copy.wait()
    for k, (start, width) in enumerate(cuts):
        grouped[k, 0 : planes * 8, :width] = ocean[:, start : start + width]
        grouped[k, planes * 8 :, :width] = kappa[:, start : start + width]
    for target, upper in ((even_ref, odd == 0), (odd_ref, odd == 1)):
        base = jnp.where(upper, 4, 0)
        near = jnp.where(upper, 7, 0)
        for k, (start, width) in enumerate(cuts):
            rows = [grouped[k, pl.ds(base + r, planes, stride=8), :] for r in range(4)]
            rates = grouped[k, planes * 8 :, :]
            rates = jnp.where(upper, pltpu.roll(rates, 4, 0), rates)
            nearest = grouped[k, pl.ds(near, planes, stride=8), :]
            low = nearest - nearest.astype(jnp.bfloat16).astype(jnp.float32)
            block = jnp.concatenate(rows + [rates, low], axis=0)
            target[:, start : start + LANES] = block.astype(jnp.bfloat16)


def prepare_kernel(
    me_ref,
    counts_ref,
    after,
    slot_ref,
    tile_place_ref,
    ocean_place_ref,
    atmos_hbm,
    piston_hbm,
    w_hbm,
    *refs,
):
    pieces = len(refs) - 10
    w_refs = refs[:pieces]
    sum_ref, pick_ref, spread_ref, flux_pick_ref, scatter_ref, air_ref, rate_ref = refs[pieces:-3]
    surface, piston, sems = refs[-3:]
    tracers, rows, columns = surface.shape
    copies = [pltpu.make_async_copy(piston_hbm, piston, sems.at[tracers])]
    for t in range(tracers):
        copies.append(pltpu.make_async_copy(atmos_hbm.at[t, 0], surface.at[t], sems.at[t]))
    size = w_refs[0].shape[0]
    for i, w_ref in enumerate(w_refs):
        part = w_hbm.at[pl.ds(i * size, size)]
        copies.append(pltpu.make_async_copy(part, w_ref, sems.at[tracers + 1 + i]))
    for copy in copies:
        copy.start()
    n_slots, blocks = sum_ref.shape
    window = counts_ref.shape[1]
    slots = blocks // window
    at = iota((1, blocks), 1)
    live = at < 0
    for d in range(window):
        live = live | ((at >= d * slots) & (at < d * slots + counts_ref[0, d]))
    table = jnp.where((iota((LANES, blocks), 0) == slot_ref[...]) & live, 1.0, 0.0)
    sum_ref[...] = table[:n_slots].astype(jnp.bfloat16)
    pick_ref[...] = table.T[:, :n_slots].astype(jnp.bfloat16)
    spread = jnp.where(iota((LANES, LANES), 0) == tile_place_ref[...], 1.0, 0.0)
    n_tiles = spread_ref.shape[0]
    spread_ref[...] = spread[:n_tiles, :n_slots].astype(jnp.bfloat16)
    flux_pick_ref[...] = spread.T[:n_slots, :n_tiles].astype(jnp.bfloat16)
    scatter_ref[...] = one_hot(iota(scatter_ref.shape, 0) == ocean_place_ref[...])
    for copy in copies:
        copy.wait()
    for k in range(columns // LANES):
        at = slice(k * LANES, (k + 1) * LANES)
        rate_ref[k * rows : (k + 1) * rows, :] = piston[:, at]
        for t in range(tracers):
            air_ref[t, k * rows : (k + 1) * rows, :] = surface[t, :, at]


def fold_tables(last, fold_ref, table_ref):
    @pl.when(last)
    def _():
        inner = iota((LANES, LANES), 0)
        for start, width in widths(fold_ref.shape[1]):
            at = slice(start, start + width)
            found = one_hot(inner[:, :width] == (fold_ref[:, at] & (LANES - 1)))
            table_ref[0:LANES, at] = found
            table_ref[LANES : 2 * LANES, at] = found


def fold_row(state, table_ref, fold_ref):
    columns = fold_ref.shape[1]
    cuts = widths(columns)
    tiles = len(cuts)
    rest = cuts[-1][1]
    rows = [state[11, :, start : start + LANES] for start, _ in cuts]
    rows[-1] = jnp.where(iota((8, LANES), 1) < rest, rows[-1], 0.0)
    rows = jnp.concatenate(rows, axis=0)
    high = rows.astype(jnp.bfloat16)
    low = (rows - high.astype(jnp.float32)).astype(jnp.bfloat16)
    parts = jnp.concatenate([high, low], axis=1)
    for start in range(0, tiles * LANES, 2 * LANES):
        end = min(start + 2 * LANES, tiles * LANES)
        width = min(end, columns) - start
        found = jnp.dot(parts, table_ref[:, start:end], preferred_element_type=jnp.float32)
        at = slice(start, start + width)
        outer = jnp.broadcast_to(fold_ref[:, at] >> 7, (8, width))
        value = found[0:8, :width]
        for k in range(1, tiles):
            value = jnp.where(outer == k, found[k * 8 : (k + 1) * 8, :width], value)
        state[12, :, at] = value


def sweep_rows(state, kap, cuts, levels, low, high, write):
    full = len(cuts) - 1
    rest = cuts[-1][1]
    lane = iota((8, LANES), 1)
    level = iota((8, LANES), 0) & (levels - 1)

    def body(r, carry):
        def cell(k):
            return state[r, :, k * LANES : (k + 1) * LANES]

        centre = cell(0)
        east_now = pltpu.roll(centre, LANES - 1, 1)
        around = pltpu.roll(centre, rest - 1, 1)
        west_last = pltpu.roll(cell(full), LANES - rest + 1, 1)
        for k in range(full + 1):
            at = slice(k * LANES, (k + 1) * LANES)
            if k == full:
                east = jnp.where(lane == rest - 1, around, east_now)
            else:
                following = cell(k + 1)
                east_next = pltpu.roll(following, LANES - 1, 1)
                east = jnp.where(lane == LANES - 1, east_next, east_now)
            west_now = pltpu.roll(centre, 1, 1)
            west = jnp.where(lane == 0, west_last, west_now)
            north = state[r + 1, :, at]
            south = state[r - 1, :, at]
            upper = jnp.where(level == 0, centre, pltpu.roll(centre, 1, 0))
            lower = jnp.where(level == levels - 1, centre, pltpu.roll(centre, 7, 0))
            horizontal = (north + south) + (east + west) - 4.0 * centre
            vertical = upper + lower - 2.0 * centre
            rate = kap[k, pl.ds(r, 1), :]
            write(r, k, centre + rate * horizontal + vertical_mix * vertical)
            if k < full:
                centre, east_now, west_last = following, east_next, west_now
        return carry

    lax.fori_loop(low, high, body, 0)


def keep(target):
    def write(r, k, value):
        target[r, :, k * LANES : (k + 1) * LANES] = value

    return write


def first_sweep_kernel(
    me_ref,
    after,
    ocean_hbm,
    kappa_hbm,
    even_hbm,
    odd_hbm,
    fold_ref,
    out_ref,
    kap_ref,
    token,
    state,
    ocean,
    kappa,
    above,
    below,
    grouped,
    table,
    sems,
    levels,
    peers,
):
    me = me_ref[0]
    last = me == peers - 1
    odd = lax.rem(me, 2)
    token[...] = jnp.zeros_like(token)
    planes = state.shape[1]
    cuts = widths(kappa.shape[1])
    copies = [
        pltpu.make_async_copy(ocean_hbm, ocean, sems.at[0]),
        pltpu.make_async_copy(kappa_hbm, kappa, sems.at[1]),
    ]
    for copy in copies:
        copy.start()

    @pl.when(odd == 1)
    def _():
        pltpu.make_async_copy(odd_hbm, above, sems.at[2]).start()
        pltpu.make_async_copy(even_hbm, below, sems.at[3]).start()

    @pl.when(odd == 0)
    def _():
        pltpu.make_async_copy(even_hbm, above, sems.at[2]).start()
        pltpu.make_async_copy(odd_hbm, below, sems.at[3]).start()

    fold_tables(last, fold_ref, table)
    for copy in copies:
        copy.wait()
    for k, (start, width) in enumerate(cuts):
        grouped[k, :, :width] = ocean[:, start : start + width]
        kap_ref[k, 4:12, :width] = kappa[:, start : start + width]
    for k, (start, width) in enumerate(cuts):
        for r in range(8):
            part = grouped[k, pl.ds(r, planes, stride=8), :]
            state[4 + r, :, start : start + LANES] = part
    pltpu.make_async_copy(even_hbm, above, sems.at[2]).wait()
    pltpu.make_async_copy(odd_hbm, below, sems.at[3]).wait()
    for halo, first, near in ((below, 0, 3), (above, 12, 0)):
        for k, (start, _) in enumerate(cuts):
            at = slice(start, start + LANES)
            block = halo[:, at].astype(jnp.float32)
            for r in range(4):
                value = block[r * planes : (r + 1) * planes]
                if r == near:
                    value = value + block[5 * planes : 6 * planes]
                state[first + r, :, at] = value
            kap_ref[k, first : first + 4, :] = block[4 * planes : 4 * planes + 4]

    @pl.when(last)
    def _():
        fold_row(state, table, fold_ref)

    sweep_rows(state, kap_ref, cuts, levels, 1, 15, keep(out_ref))

    @pl.when(last)
    def _():
        fold_row(out_ref, table, fold_ref)


def second_sweep_kernel(
    me_ref, after, state_ref, kap_ref, fold_ref, out_ref, token, table, levels, peers
):
    token[...] = jnp.zeros_like(token)
    last = me_ref[0] == peers - 1
    fold_tables(last, fold_ref, table)
    sweep_rows(state_ref, kap_ref, widths(fold_ref.shape[1]), levels, 2, 14, keep(out_ref))

    @pl.when(last)
    def _():
        fold_row(out_ref, table, fold_ref)


def last_sweeps_kernel(
    me_ref, after, state_ref, kap_ref, fold_ref, out_ref, state, grouped, table, levels, peers
):
    cuts = widths(out_ref.shape[1])
    planes = state_ref.shape[1]
    last = me_ref[0] == peers - 1
    fold_tables(last, fold_ref, table)
    sweep_rows(state_ref, kap_ref, cuts, levels, 3, 13, keep(state))

    @pl.when(last)
    def _():
        fold_row(state, table, fold_ref)

    def write(r, k, value):
        grouped[k, pl.ds(r - 4, planes, stride=8), :] = value

    sweep_rows(state, kap_ref, cuts, levels, 4, 12, write)
    for k, (start, width) in enumerate(cuts):
        out_ref[:, start : start + width] = grouped[k, :, :width]


def all_weights(held, w_hbm, w_rest, sems):
    size = held[0].shape[0]
    first = len(held) * size
    copies = []
    for i in range(w_rest.shape[0] // size):
        part = pl.ds(i * size, size)
        source = w_hbm.at[pl.ds(first + i * size, size)]
        copies.append(pltpu.make_async_copy(source, w_rest.at[part], sems.at[i]))
        copies[-1].start()

    def get(d):
        if d < len(held):
            weights = held[d][...]
        else:
            at = d - len(held)
            copies[at].wait()
            weights = w_rest[at * size : (at + 1) * size]
        return weights.reshape(size * LANES, LANES)

    return get


def forward_kernel(me_ref, recv_ref, sum_ref, w_hbm, *refs):
    held, (out_ref, token, sums, w_rest, sems) = refs[:-5], refs[-5:]
    get_weights = all_weights(held, w_hbm, w_rest, sems)
    token[...] = jnp.zeros_like(token)
    me = me_ref[0]
    peers = recv_ref.shape[0]
    tracers, blocks, _ = sums.shape
    n_slots = sum_ref.shape[0]
    window = n_slots // 8
    slots = blocks // window
    row = iota((8, LANES), 0)
    out_ref[...] = jnp.zeros_like(out_ref)
    for d in range(window):
        cells = recv_ref[jnp.clip(me - d + window // 2, 0, peers - 1)]
        weights = get_weights(d)
        product = lax.dot_general(
            cells, weights, (((1,), (1,)), ((), ())), preferred_element_type=jnp.float32
        )
        for t in range(tracers):
            for half in range(0, slots, 8):
                top = t * slots + half
                found = product[top : top + 8, half * LANES : (half + 1) * LANES]
                for k in range(1, 8):
                    at = slice((half + k) * LANES, (half + k + 1) * LANES)
                    found = jnp.where(row == k, product[top : top + 8, at], found)
                sums[t, d * slots + half : d * slots + half + 8, :] = found
    partial_sums = [split_dot(sum_ref[...], sums[t], ((1,), (0,))) for t in range(tracers)]
    for g in range(window):
        peer = me + g - window // 2

        @pl.when((peer >= 0) & (peer < peers))
        def _():
            for t in range(tracers):
                out_ref[peer, t * 8 : (t + 1) * 8, :] = partial_sums[t][g * 8 : (g + 1) * 8]


def flux_kernel(
    me_ref, after, parts_ref, spread_ref, pick_ref, air_ref, rate_ref, send_ref, flux_ref, token
):
    token[...] = jnp.zeros_like(token)
    me = me_ref[0]
    peers = parts_ref.shape[0]
    tracers, rows, columns = flux_ref.shape
    n_slots = spread_ref.shape[1]
    window = n_slots // 8
    send_ref[...] = jnp.zeros_like(send_ref)
    sent = []
    for t in range(tracers):
        parts = []
        for g in range(window):
            coupler = me - g + window // 2
            valid = (coupler >= 0) & (coupler < peers)
            block = parts_ref[jnp.clip(coupler, 0, peers - 1), t * 8 : (t + 1) * 8, :]
            parts.append(jnp.where(valid, block, 0.0))
        remapped = split_dot(spread_ref[...], jnp.concatenate(parts, axis=0), ((1,), (0,)))
        flux = rate_ref[...] * (solubility * air_ref[t] - remapped)
        for k in range(columns // LANES):
            flux_ref[t, :, k * LANES : (k + 1) * LANES] = flux[k * rows : (k + 1) * rows]
        sent.append(
            jnp.dot(pick_ref[...], flux.astype(jnp.bfloat16), preferred_element_type=jnp.float32)
        )
    for g in range(window):
        peer = me - g + window // 2

        @pl.when((peer >= 0) & (peer < peers))
        def _():
            block = jnp.concatenate([s[g * 8 : (g + 1) * 8] for s in sent], axis=0)
            send_ref[peer] = block.astype(jnp.bfloat16)


def backward_kernel(me_ref, after, recv_ref, pick_ref, w_hbm, *refs):
    held, (out_ref, token, w_rest, sems) = refs[:-4], refs[-4:]
    get_weights = all_weights(held, w_hbm, w_rest, sems)
    token[...] = jnp.zeros_like(token)
    me = me_ref[0]
    peers, width, _ = recv_ref.shape
    tracers = width // 8
    blocks, n_slots = pick_ref.shape
    window = n_slots // 8
    slots = blocks // window
    parts = [[] for _ in range(tracers)]
    for g in range(window):
        owner = me + g - window // 2
        valid = (owner >= 0) & (owner < peers)
        block = recv_ref[jnp.clip(owner, 0, peers - 1)].astype(jnp.float32)
        block = jnp.where(valid, block, 0.0)
        for t in range(tracers):
            parts[t].append(block[t * 8 : (t + 1) * 8])
    picked = [
        jnp.dot(
            pick_ref[...],
            jnp.concatenate(parts[t], axis=0).astype(jnp.bfloat16),
            preferred_element_type=jnp.float32,
        )
        for t in range(tracers)
    ]
    out_ref[...] = jnp.zeros_like(out_ref)
    row = iota((slots, LANES), 0)
    for d in range(window):
        part = slice(d * slots, (d + 1) * slots)
        mine = [p[part] for p in picked]
        cells = jnp.concatenate(
            [
                jnp.concatenate([jnp.where(row == k, m, 0.0) for m in mine], axis=0).astype(
                    jnp.bfloat16
                )
                for k in range(slots)
            ],
            axis=1,
        )
        weights = get_weights(d)
        product = jnp.dot(cells, weights, preferred_element_type=jnp.float32)
        peer = me - d + window // 2

        @pl.when((peer >= 0) & (peer < peers))
        def _():
            out_ref[peer] = product


def add_kernel(me_ref, returned_ref, table_ref, swept, out, buffer, surface, sems):
    me = me_ref[0]
    peers = returned_ref.shape[0]
    tracers, _, columns = surface.shape
    loads = []
    for t in range(tracers):
        loads.append(pltpu.make_async_copy(swept.at[t, 0], surface.at[t], sems.at[tracers + t]))
        loads[-1].start()
    slots = returned_ref.shape[1] // tracers
    window = table_ref.shape[1] // slots
    cuts = widths(columns)
    full = len(cuts) - 1
    rest = cuts[-1][1]
    lane = iota((8, LANES), 1)
    row = iota((8, LANES), 0)
    stays = lane < LANES - rest * row
    copies = []
    for t in range(tracers):
        parts = []
        for d in range(window):
            coupler = me + d - window // 2
            valid = (coupler >= 0) & (coupler < peers)
            block = returned_ref[jnp.clip(coupler, 0, peers - 1), t * slots : (t + 1) * slots, :]
            parts.append(jnp.where(valid, block, 0.0))
        tiles = split_dot(table_ref[...], jnp.concatenate(parts, axis=0), ((1,), (0,)))
        rows = [tiles[k * 8 : (k + 1) * 8] for k in range(full + 1)]
        rows[full] = jnp.where(row == 7, rows[full], pltpu.roll(rows[0], 7, 0))
        turned = [shear(value, -1, rest) for value in rows]
        loads[t].wait()
        for k, (start, width) in enumerate(cuts):
            value = turned[k]
            if k < full:
                value = jnp.where(stays, value, turned[k + 1])
            at = slice(start, start + width)
            buffer[t, :, at] = surface[t, :, at] + ocean_rate * value[:, :width]
        copies.append(pltpu.make_async_copy(buffer.at[t], out.at[t, 0], sems.at[t]))
        copies[-1].start()
    for copy in copies:
        copy.wait()


def atmos_kernel(atmos_ref, flux_ref, mix_ref, out_ref):
    tracers, levels, rows, columns = atmos_ref.shape
    for t in range(tracers):
        for r in range(0, rows, 8):
            for c in range(0, columns, LANES):
                at = (slice(r, r + 8), slice(c, c + LANES))
                mixing = mix_ref[at]
                field = [atmos_ref[(t, v) + at] for v in range(levels)]
                field[0] = field[0] - atmos_rate * flux_ref[(t,) + at]
                for _ in range(ASTEPS):
                    field = [
                        field[v]
                        + mixing
                        * (field[max(v - 1, 0)] + field[min(v + 1, levels - 1)] - 2.0 * field[v])
                        for v in range(levels)
                    ]
                for v in range(levels):
                    out_ref[(t, v) + at] = field[v]


def local(
    ocean,
    kappa,
    atmos,
    piston,
    atmos_mix,
    fold_map,
    send_tile,
    slot_counts,
    out_slot,
    out_tile,
    remap_w,
):
    count = lax.axis_size("tile")
    me = lax.axis_index("tile").astype(jnp.int32).reshape(1)
    tracers, levels, ocean_rows, columns = ocean.shape
    planes = tracers * levels
    window, slots_in = send_tile.shape[1:]
    slots_out = out_tile.shape[2]
    blocks = window * slots_in
    n_slots = window * slots_out
    tiles = -(-columns // LANES)
    full = columns // LANES
    padded = tiles * LANES
    atmos_rows, atmos_columns = atmos.shape[2:]
    across = atmos_columns // LANES
    n_tiles = atmos_rows * across
    f32, bf16, i32 = jnp.float32, jnp.bfloat16, jnp.int32
    shape = jax.ShapeDtypeStruct
    dma = pltpu.SemaphoreType.DMA
    exchange = functools.partial(
        lax.all_to_all, axis_name="tile", split_axis=0, concat_axis=0, tiled=True
    )

    def cost(us):
        return pl.CostEstimate(
            flops=0, bytes_accessed=int(us * 1.0e4), transcendentals=0
        )

    token_shape = shape((8, LANES), f32)
    sent, token = pl.pallas_call(
        pack_kernel,
        out_shape=(pltpu.HBM((count, tracers * slots_in, LANES), bf16), token_shape),
        in_specs=[smem(), hbm(), hbm()],
        out_specs=(vmem(), vmem()),
        scratch_shapes=[
            pltpu.SMEM(send_tile.shape, i32),
            pltpu.VMEM((tracers, ocean_rows, columns), f32),
            pltpu.VMEM((tracers, tiles * 8, LANES), f32),
            pltpu.VMEM((window, tracers * slots_in, LANES), f32),
            dma((tracers + 1,)),
        ],
        compiler_params=params(),
        name="pack",
    )(me, in_hbm(send_tile), in_hbm(ocean))
    received = exchange(sent)

    halo_rows = 6 * planes
    flat = in_hbm(ocean.reshape(planes * ocean_rows, columns))
    even, odd = pl.pallas_call(
        halo_kernel,
        out_shape=(shape((halo_rows, padded), bf16), shape((halo_rows, padded), bf16)),
        in_specs=[smem(), vmem(), hbm(), hbm()],
        out_specs=(vmem(),) * 2,
        scratch_shapes=[
            pltpu.VMEM((planes * ocean_rows, columns), f32),
            pltpu.VMEM((ocean_rows, columns), f32),
            pltpu.VMEM((tiles, (planes + 1) * ocean_rows, LANES), f32),
            dma((2,)),
        ],
        compiler_params=params(),
        cost_estimate=cost(2),
        name="halo",
    )(me, token, flat, in_hbm(kappa))
    even_pairs = [(i, i ^ 1) for i in range(count) if i ^ 1 < count]
    odd_pairs = [(i, i + 1) for i in range(1, count - 1, 2)]
    odd_pairs += [(b, a) for a, b in odd_pairs]
    even = lax.ppermute(even, "tile", even_pairs)
    odd = lax.ppermute(odd, "tile", odd_pairs)

    tile_place = (out_tile % across) * atmos_rows + out_tile // across
    tile_place = jnp.pad(tile_place.reshape(1, n_slots), ((0, 0), (0, LANES - n_slots)))
    over = send_tile // full
    ocean_place = jnp.where(
        send_tile == 8 * full, 8 * full + 7, (send_tile - over * full) * 8 + over
    ).reshape(1, blocks)
    weights = in_hbm(remap_w[0])
    prepared = pl.pallas_call(
        prepare_kernel,
        out_shape=(
            *[shape((slots_in,) + remap_w.shape[2:], bf16)] * HELD,
            shape((n_slots, blocks), bf16),
            shape((blocks, n_slots), bf16),
            shape((n_tiles, n_slots), bf16),
            shape((n_slots, n_tiles), bf16),
            shape((tiles * 8, blocks), bf16),
            shape((tracers, n_tiles, LANES), f32),
            shape((n_tiles, LANES), f32),
        ),
        in_specs=[smem(), smem()] + [vmem()] * 4 + [hbm()] * 3,
        out_specs=(vmem(),) * (7 + HELD),
        scratch_shapes=[
            pltpu.VMEM((tracers, atmos_rows, atmos_columns), f32),
            pltpu.VMEM((atmos_rows, atmos_columns), f32),
            dma((tracers + 1 + HELD,)),
        ],
        compiler_params=params(),
        cost_estimate=cost(1.5),
        name="prepare",
    )(
        me,
        slot_counts,
        token,
        out_slot,
        tile_place,
        ocean_place,
        in_hbm(atmos),
        in_hbm(piston),
        weights,
    )
    held = prepared[:HELD]
    sum_table, slot_pick, spread, flux_pick, scatter, air, rate = prepared[HELD:]
    weight_scratch = [
        pltpu.VMEM((blocks - HELD * slots_in,) + remap_w.shape[2:], bf16),
        dma((window - HELD,)),
    ]

    partial_sums, token = pl.pallas_call(
        forward_kernel,
        out_shape=(pltpu.HBM((count, tracers * slots_out, LANES), f32), token_shape),
        in_specs=[smem(), vmem(), vmem(), hbm()] + [vmem()] * HELD,
        out_specs=(vmem(), vmem()),
        scratch_shapes=[pltpu.VMEM((tracers, blocks, LANES), f32)] + weight_scratch,
        compiler_params=params(),
        name="forward",
    )(me, received, sum_table, weights, *held)
    owner_parts = exchange(partial_sums)

    state_shape = (16, planes, padded)
    fold = fold_map.reshape(1, columns)
    fold_scratch = [pltpu.VMEM((2 * LANES, padded), bf16)]
    state, kap, token = pl.pallas_call(
        functools.partial(first_sweep_kernel, levels=levels, peers=count),
        out_shape=(pltpu.HBM(state_shape, f32), pltpu.HBM((tiles, 16, LANES), f32), token_shape),
        in_specs=[smem(), vmem()] + [hbm()] * 4 + [vmem()],
        out_specs=(vmem(),) * 3,
        scratch_shapes=[
            pltpu.VMEM(state_shape, f32),
            pltpu.VMEM((planes * ocean_rows, columns), f32),
            pltpu.VMEM((ocean_rows, columns), f32),
            pltpu.VMEM((halo_rows, padded), bf16),
            pltpu.VMEM((halo_rows, padded), bf16),
            pltpu.VMEM((tiles, planes * ocean_rows, LANES), f32),
        ]
        + fold_scratch
        + [dma((4,))],
        compiler_params=params(),
        cost_estimate=cost(5),
        name="first_sweep",
    )(me, token, flat, in_hbm(kappa), in_hbm(even), in_hbm(odd), fold)

    flux_sent, flux, token = pl.pallas_call(
        flux_kernel,
        out_shape=(
            pltpu.HBM((count, tracers * slots_out, LANES), bf16),
            shape((tracers, atmos_rows, atmos_columns), f32),
            token_shape,
        ),
        in_specs=[smem()] + [vmem()] * 6,
        out_specs=(vmem(),) * 3,
        compiler_params=params(),
        name="flux",
    )(me, token, owner_parts, spread, flux_pick, air, rate)
    at_coupler = exchange(flux_sent)

    state, token = pl.pallas_call(
        functools.partial(second_sweep_kernel, levels=levels, peers=count),
        out_shape=(pltpu.HBM(state_shape, f32), token_shape),
        in_specs=[smem()] + [vmem()] * 4,
        out_specs=(vmem(), vmem()),
        scratch_shapes=fold_scratch,
        compiler_params=params(),
        cost_estimate=cost(3),
        name="second_sweep",
    )(me, token, in_hbm(state), in_hbm(kap), fold)

    back_sums, token = pl.pallas_call(
        backward_kernel,
        out_shape=(pltpu.HBM((count, tracers * slots_in, LANES), f32), token_shape),
        in_specs=[smem()] + [vmem()] * 3 + [hbm()] + [vmem()] * HELD,
        out_specs=(vmem(), vmem()),
        scratch_shapes=weight_scratch,
        compiler_params=params(),
        name="backward",
    )(me, token, at_coupler, slot_pick, weights, *held)
    returned = exchange(back_sums)

    swept = pl.pallas_call(
        functools.partial(last_sweeps_kernel, levels=levels, peers=count),
        out_shape=shape((planes * ocean_rows, columns), f32),
        in_specs=[smem()] + [vmem()] * 4,
        out_specs=vmem(),
        scratch_shapes=[
            pltpu.VMEM(state_shape, f32),
            pltpu.VMEM((tiles, planes * ocean_rows, LANES), f32),
        ]
        + fold_scratch,
        compiler_params=params(),
        cost_estimate=cost(4),
        name="last_sweeps",
    )(me, token, in_hbm(state), in_hbm(kap), fold)
    atmos_next = pl.pallas_call(
        atmos_kernel,
        out_shape=shape(atmos.shape, f32),
        in_specs=[vmem()] * 3,
        out_specs=vmem(),
        compiler_params=params(),
        cost_estimate=cost(1),
        name="atmos",
    )(atmos, flux, atmos_mix)

    ocean_next = pl.pallas_call(
        add_kernel,
        out_shape=shape(ocean.shape, f32),
        in_specs=[smem()] + [vmem()] * 2 + [hbm()],
        out_specs=hbm(),
        scratch_shapes=[
            pltpu.VMEM((tracers, ocean_rows, columns), f32),
            pltpu.VMEM((tracers, ocean_rows, columns), f32),
            dma((2 * tracers,)),
        ],
        input_output_aliases={3: 0},
        compiler_params=params(),
        name="add",
    )(me, returned, scatter, in_hbm(swept.reshape(ocean.shape)))
    return (ocean_next, atmos_next)


def solution(mesh):
    placed = (
        P("member", None, "tile", None),
        P("tile", None),
        P("member", None, "tile", None),
        P("tile", None),
        P("tile", None),
        P(),
        P("tile", None, None),
        P("tile", None),
        P("tile", None),
        P("tile", None, None),
        P("tile", None, None, None),
    )
    return jax.shard_map(
        local,
        mesh=mesh,
        in_specs=placed,
        out_specs=(P("member", None, "tile", None), P("member", None, "tile", None)),
        check_vma=False,
    )
```

```python
import functools

import jax
import jax.numpy as jnp
from jax import lax
from jax.experimental import pallas as pl
from jax.experimental.pallas import tpu as pltpu
from jax.sharding import PartitionSpec as P

OSTEPS = 4
ASTEPS = 4
LANES = 128
HELD = 5

vertical_mix = 0.1
ocean_rate = 4.0
atmos_rate = 0.5
solubility = 1.2

MIB = 1024 * 1024


def params(mib=16):
    return pltpu.CompilerParams(vmem_limit_bytes=36 * MIB)


def vmem():
    return pl.BlockSpec(memory_space=pltpu.VMEM)


def smem():
    return pl.BlockSpec(memory_space=pltpu.SMEM)


def hbm():
    return pl.BlockSpec(memory_space=pltpu.HBM)


def anywhere():
    return pl.BlockSpec(memory_space=pl.ANY)


def iota(shape, dim):
    return lax.broadcasted_iota(jnp.int32, shape, dim)


def split_dot(table, values, dims):
    high = values.astype(jnp.bfloat16)
    low = (values - high.astype(jnp.float32)).astype(jnp.bfloat16)
    dot = functools.partial(
        lax.dot_general, dimension_numbers=(dims, ((), ())), preferred_element_type=jnp.float32
    )
    return dot(table, high) + dot(table, low)


def shear(tile, sign, shift):
    lane = iota(tile.shape, 1)
    row = iota(tile.shape, 0)
    source = (lane - sign * shift * row) & (LANES - 1)
    return jnp.take_along_axis(tile, source, axis=1, mode="promise_in_bounds")


def widths(columns):
    return [(c, min(LANES, columns - c)) for c in range(0, columns, LANES)]


def in_hbm(x):
    return pltpu.with_memory_space_constraint(x, pltpu.HBM)


def row_of(tracer, slot, tracers):
    return (slot // 8) * 8 * tracers + tracer * 8 + slot % 8


def magic(divisor, count):
    scale = -(-65536 // divisor)
    assert all((i * scale) >> 16 == i // divisor for i in range(count))
    return scale


def tile_row(index, full, scale):
    over = (index * scale) >> 16
    return jnp.where(index == 8 * full, 8 * full + 7, (index - over * full) * 8 + over)


def one_hot(mask):
    return jnp.where(mask, 1.0, 0.0).astype(jnp.bfloat16)


def pack_kernel(me_ref, send_hbm, ocean_hbm, out_ref, token, send, surface, tiles, rows, sems):
    me = me_ref[0]
    peers = out_ref.shape[0]
    _, window, slots = send.shape
    tracers, _, columns = surface.shape
    copies = [pltpu.make_async_copy(send_hbm, send, sems.at[tracers])]
    for t in range(tracers):
        copies.append(pltpu.make_async_copy(ocean_hbm.at[t, 0], surface.at[t], sems.at[t]))
    for copy in copies:
        copy.start()
    out_ref[...] = jnp.zeros_like(out_ref)
    token[...] = jnp.zeros_like(token)
    cuts = widths(columns)
    full = len(cuts) - 1
    rest = cuts[-1][1]
    lane = iota((8, LANES), 1)
    row = iota((8, LANES), 0)
    wraps = lane < rest * row
    for t in range(tracers):
        copies[1 + t].wait()
        before = jnp.zeros((8, LANES), jnp.float32)
        first = None
        for k, (start, width) in enumerate(cuts):
            part = surface[t, :, start : start + width]
            if width < LANES:
                part = jnp.concatenate(
                    [part, jnp.zeros((8, LANES - width), jnp.float32)], axis=1
                )
            turned = shear(part, 1, rest)
            value = jnp.where(wraps, before, turned)
            before = turned
            if k == 0:
                first = value
            else:
                tiles[t, k * 8 : (k + 1) * 8] = value
        tiles[t, 0:8] = jnp.where(wraps, pltpu.roll(value, 1, 0), first)
    copies[0].wait()
    scale = magic(full, 8 * full + 1)
    for d in range(window):
        for k in range(slots):
            index = send[0, d, k]
            place = tile_row(index, full, scale)
            for t in range(tracers):
                at = row_of(t, k, tracers)
                rows[d, at : at + 1, :] = tiles[t, pl.ds(place, 1), :]
    for d in range(window):
        peer = me + d - window // 2

        @pl.when((peer >= 0) & (peer < peers))
        def _():
            out_ref[peer] = rows[d].astype(jnp.bfloat16)


def pack_halo(odd, ocean, kappa, grouped, even_ref, odd_ref):
    planes = ocean.shape[0] // 8
    cuts = widths(ocean.shape[1])
    for k, (start, width) in enumerate(cuts):
        grouped[k, 0 : planes * 8, :width] = ocean[:, start : start + width]
        grouped[k, planes * 8 :, :width] = kappa[:, start : start + width]
    for target, upper in ((even_ref, odd == 0), (odd_ref, odd == 1)):
        base = jnp.where(upper, 4, 0)
        near = jnp.where(upper, 7, 0)
        for k, (start, width) in enumerate(cuts):
            rows = [grouped[k, pl.ds(base + r, planes, stride=8), :] for r in range(4)]
            rates = grouped[k, planes * 8 :, :]
            rates = jnp.where(upper, pltpu.roll(rates, 4, 0), rates)
            nearest = grouped[k, pl.ds(near, planes, stride=8), :]
            low = nearest - nearest.astype(jnp.bfloat16).astype(jnp.float32)
            block = jnp.concatenate(rows + [rates, low], axis=0)
            target[:, start : start + LANES] = block.astype(jnp.bfloat16)


def prepare_kernel(
    me_ref,
    after,
    counts_hbm,
    slot_hbm,
    out_tile_hbm,
    send_hbm,
    ocean_hbm,
    kappa_hbm,
    atmos_hbm,
    piston_hbm,
    w_hbm,
    *refs,
):
    held = len(refs) - 21
    w_refs = refs[:held]
    even_hbm, odd_hbm = refs[held : held + 2]
    sum_ref, pick_ref, spread_ref, flux_pick_ref, scatter_ref, air_ref, rate_ref = refs[
        held + 2 : held + 9
    ]
    ocean, kappa, grouped, even, odd, surface, piston = refs[held + 9 : -5]
    counts, slot, out_tile, send, sems = refs[-5:]
    tracers, rows, columns = surface.shape
    size = w_refs[0].shape[0]
    pairs = [(counts_hbm, counts), (slot_hbm, slot), (out_tile_hbm, out_tile), (send_hbm, send)]
    pairs += [(ocean_hbm, ocean), (kappa_hbm, kappa), (piston_hbm, piston)]
    pairs += [(atmos_hbm.at[t, 0], surface.at[t]) for t in range(tracers)]
    pairs += [(w_hbm.at[pl.ds(i * size, size)], w_refs[i]) for i in range(held)]
    copies = [pltpu.make_async_copy(a, b, sems.at[i]) for i, (a, b) in enumerate(pairs)]
    for copy in copies:
        copy.start()
    n_slots, blocks = sum_ref.shape
    window, slots = send.shape[1:]
    slots_out = out_tile.shape[2]
    across = columns // LANES
    n_tiles = spread_ref.shape[0]
    full = ocean.shape[1] // LANES
    scale, scale_tile = magic(full, 8 * full + 1), magic(across, n_tiles)
    for copy in copies[:4]:
        copy.wait()
    at = iota((1, blocks), 1)
    live = at < 0
    place = jnp.zeros((1, blocks), jnp.int32)
    tile_place = jnp.zeros((1, blocks), jnp.int32)
    for d in range(window):
        live = live | ((at >= d * slots) & (at < d * slots + counts[0, d]))
        for k in range(slots):
            place = jnp.where(at == d * slots + k, tile_row(send[0, d, k], full, scale), place)
        for j in range(slots_out):
            tile = out_tile[0, d, j]
            down = (tile * scale_tile) >> 16
            value = (tile - down * across) * rows + down
            tile_place = jnp.where(at == d * slots_out + j, value, tile_place)
    table = jnp.where((iota((LANES, blocks), 0) == slot[...]) & live, 1.0, 0.0)
    sum_ref[...] = table[:n_slots].astype(jnp.bfloat16)
    pick_ref[...] = table.T[:, :n_slots].astype(jnp.bfloat16)
    spread = jnp.where(iota((LANES, LANES), 0) == tile_place, 1.0, 0.0)
    spread_ref[...] = spread[:n_tiles, :n_slots].astype(jnp.bfloat16)
    flux_pick_ref[...] = spread.T[:n_slots, :n_tiles].astype(jnp.bfloat16)
    scatter_ref[...] = one_hot(iota(scatter_ref.shape, 0) == place)
    for copy in copies[4:6]:
        copy.wait()
    pack_halo(lax.rem(me_ref[0], 2), ocean, kappa, grouped, even, odd)
    copies += [
        pltpu.make_async_copy(even, even_hbm, sems.at[len(copies)]),
        pltpu.make_async_copy(odd, odd_hbm, sems.at[len(copies) + 1]),
    ]
    for copy in copies[-2:]:
        copy.start()
    for copy in copies[6:]:
        copy.wait()
    for k in range(columns // LANES):
        at = slice(k * LANES, (k + 1) * LANES)
        rate_ref[k * rows : (k + 1) * rows, :] = piston[:, at]
        for t in range(tracers):
            air_ref[t, k * rows : (k + 1) * rows, :] = surface[t, :, at]


def fold_tables(last, fold_ref, table_ref):
    @pl.when(last)
    def _():
        inner = iota((LANES, LANES), 0)
        for start, width in widths(fold_ref.shape[1]):
            at = slice(start, start + width)
            found = one_hot(inner[:, :width] == (fold_ref[:, at] & (LANES - 1)))
            table_ref[0:LANES, at] = found
            table_ref[LANES : 2 * LANES, at] = found


def fold_row(state, table_ref, fold_ref):
    columns = fold_ref.shape[1]
    cuts = widths(columns)
    tiles = len(cuts)
    rest = cuts[-1][1]
    rows = [state[11, :, start : start + LANES] for start, _ in cuts]
    rows[-1] = jnp.where(iota((8, LANES), 1) < rest, rows[-1], 0.0)
    rows = jnp.concatenate(rows, axis=0)
    high = rows.astype(jnp.bfloat16)
    low = (rows - high.astype(jnp.float32)).astype(jnp.bfloat16)
    parts = jnp.concatenate([high, low], axis=1)
    for start in range(0, tiles * LANES, 2 * LANES):
        end = min(start + 2 * LANES, tiles * LANES)
        width = min(end, columns) - start
        found = jnp.dot(parts, table_ref[:, start:end], preferred_element_type=jnp.float32)
        at = slice(start, start + width)
        outer = jnp.broadcast_to(fold_ref[:, at] >> 7, (8, width))
        value = found[0:8, :width]
        for k in range(1, tiles):
            value = jnp.where(outer == k, found[k * 8 : (k + 1) * 8, :width], value)
        state[12, :, at] = value


def sweep_rows(state, kap, cuts, levels, low, high, write):
    full = len(cuts) - 1
    rest = cuts[-1][1]
    lane = iota((8, LANES), 1)
    level = iota((8, LANES), 0) & (levels - 1)

    def body(r, carry):
        def cell(k):
            return state[r, :, k * LANES : (k + 1) * LANES]

        centre = cell(0)
        east_now = pltpu.roll(centre, LANES - 1, 1)
        around = pltpu.roll(centre, rest - 1, 1)
        west_last = pltpu.roll(cell(full), LANES - rest + 1, 1)
        for k in range(full + 1):
            at = slice(k * LANES, (k + 1) * LANES)
            if k == full:
                east = jnp.where(lane == rest - 1, around, east_now)
            else:
                following = cell(k + 1)
                east_next = pltpu.roll(following, LANES - 1, 1)
                east = jnp.where(lane == LANES - 1, east_next, east_now)
            west_now = pltpu.roll(centre, 1, 1)
            west = jnp.where(lane == 0, west_last, west_now)
            north = state[r + 1, :, at]
            south = state[r - 1, :, at]
            upper = jnp.where(level == 0, centre, pltpu.roll(centre, 1, 0))
            lower = jnp.where(level == levels - 1, centre, pltpu.roll(centre, 7, 0))
            horizontal = (north + south) + (east + west) - 4.0 * centre
            vertical = upper + lower - 2.0 * centre
            rate = kap[k, pl.ds(r, 1), :]
            write(r, k, centre + rate * horizontal + vertical_mix * vertical)
            if k < full:
                centre, east_now, west_last = following, east_next, west_now
        return carry

    lax.fori_loop(low, high, body, 0)


def keep(target):
    def write(r, k, value):
        target[r, :, k * LANES : (k + 1) * LANES] = value

    return write


def first_sweep_kernel(
    me_ref,
    after,
    ocean_hbm,
    kappa_hbm,
    even_hbm,
    odd_hbm,
    fold_ref,
    out_ref,
    kap_ref,
    token,
    state,
    ocean,
    kappa,
    above,
    below,
    grouped,
    table,
    sems,
    levels,
    peers,
):
    me = me_ref[0]
    last = me == peers - 1
    odd = lax.rem(me, 2)
    token[...] = jnp.zeros_like(token)
    planes = state.shape[1]
    cuts = widths(kappa.shape[1])
    copies = [
        pltpu.make_async_copy(ocean_hbm, ocean, sems.at[0]),
        pltpu.make_async_copy(kappa_hbm, kappa, sems.at[1]),
    ]
    for copy in copies:
        copy.start()

    @pl.when(odd == 1)
    def _():
        pltpu.make_async_copy(odd_hbm, above, sems.at[2]).start()
        pltpu.make_async_copy(even_hbm, below, sems.at[3]).start()

    @pl.when(odd == 0)
    def _():
        pltpu.make_async_copy(even_hbm, above, sems.at[2]).start()
        pltpu.make_async_copy(odd_hbm, below, sems.at[3]).start()

    fold_tables(last, fold_ref, table)
    for copy in copies:
        copy.wait()
    for k, (start, width) in enumerate(cuts):
        grouped[k, :, :width] = ocean[:, start : start + width]
        kap_ref[k, 4:12, :width] = kappa[:, start : start + width]
    for k, (start, width) in enumerate(cuts):
        for r in range(8):
            part = grouped[k, pl.ds(r, planes, stride=8), :]
            state[4 + r, :, start : start + LANES] = part
    pltpu.make_async_copy(even_hbm, above, sems.at[2]).wait()
    pltpu.make_async_copy(odd_hbm, below, sems.at[3]).wait()
    for halo, first, near in ((below, 0, 3), (above, 12, 0)):
        for k, (start, _) in enumerate(cuts):
            at = slice(start, start + LANES)
            block = halo[:, at].astype(jnp.float32)
            for r in range(4):
                value = block[r * planes : (r + 1) * planes]
                if r == near:
                    value = value + block[5 * planes : 6 * planes]
                state[first + r, :, at] = value
            kap_ref[k, first : first + 4, :] = block[4 * planes : 4 * planes + 4]

    @pl.when(last)
    def _():
        fold_row(state, table, fold_ref)

    sweep_rows(state, kap_ref, cuts, levels, 1, 15, keep(out_ref))

    @pl.when(last)
    def _():
        fold_row(out_ref, table, fold_ref)


def second_sweep_kernel(
    me_ref, after, state_ref, kap_ref, fold_ref, out_ref, token, table, levels, peers
):
    token[...] = jnp.zeros_like(token)
    last = me_ref[0] == peers - 1
    fold_tables(last, fold_ref, table)
    sweep_rows(state_ref, kap_ref, widths(fold_ref.shape[1]), levels, 2, 14, keep(out_ref))

    @pl.when(last)
    def _():
        fold_row(out_ref, table, fold_ref)


def last_sweeps_kernel(
    me_ref, after, state_ref, kap_ref, fold_ref, out_ref, state, grouped, table, levels, peers
):
    cuts = widths(out_ref.shape[1])
    planes = state_ref.shape[1]
    last = me_ref[0] == peers - 1
    fold_tables(last, fold_ref, table)
    sweep_rows(state_ref, kap_ref, cuts, levels, 3, 13, keep(state))

    @pl.when(last)
    def _():
        fold_row(state, table, fold_ref)

    def write(r, k, value):
        grouped[k, pl.ds(r - 4, planes, stride=8), :] = value

    sweep_rows(state, kap_ref, cuts, levels, 4, 12, write)
    for k, (start, width) in enumerate(cuts):
        out_ref[:, start : start + width] = grouped[k, :, :width]


def all_weights(held, w_hbm, w_rest, sems):
    size = held[0].shape[0]
    first = len(held) * size
    copies = []
    for i in range(w_rest.shape[0] // size):
        part = pl.ds(i * size, size)
        source = w_hbm.at[pl.ds(first + i * size, size)]
        copies.append(pltpu.make_async_copy(source, w_rest.at[part], sems.at[i]))
        copies[-1].start()

    def get(d):
        if d < len(held):
            weights = held[d][...]
        else:
            at = d - len(held)
            copies[at].wait()
            weights = w_rest[at * size : (at + 1) * size]
        return weights.reshape(size * LANES, LANES)

    return get


def forward_kernel(me_ref, recv_ref, sum_ref, w_hbm, *refs):
    held, (out_ref, token, sums, w_rest, sems) = refs[:-5], refs[-5:]
    get_weights = all_weights(held, w_hbm, w_rest, sems)
    token[...] = jnp.zeros_like(token)
    me = me_ref[0]
    peers = recv_ref.shape[0]
    tracers, blocks, _ = sums.shape
    n_slots = sum_ref.shape[0]
    window = n_slots // 8
    slots = blocks // window
    row = iota((8, LANES), 0)
    out_ref[...] = jnp.zeros_like(out_ref)
    for d in range(window):
        source = jnp.clip(me - d + window // 2, 0, peers - 1)
        weights = get_weights(d)
        for first in range(0, slots, 8):
            top = row_of(0, first, tracers)
            cells = recv_ref[source, top : top + 8 * tracers, :]
            product = lax.dot_general(
                cells,
                weights[first * LANES : (first + 8) * LANES],
                (((1,), (1,)), ((), ())),
                preferred_element_type=jnp.float32,
            )
            for t in range(tracers):
                part = product[t * 8 : (t + 1) * 8]
                found = part[:, :LANES]
                for k in range(1, 8):
                    found = jnp.where(row == k, part[:, k * LANES : (k + 1) * LANES], found)
                sums[t, d * slots + first : d * slots + first + 8, :] = found
    partial_sums = [split_dot(sum_ref[...], sums[t], ((1,), (0,))) for t in range(tracers)]
    for g in range(window):
        peer = me + g - window // 2

        @pl.when((peer >= 0) & (peer < peers))
        def _():
            for t in range(tracers):
                out_ref[peer, t * 8 : (t + 1) * 8, :] = partial_sums[t][g * 8 : (g + 1) * 8]


def flux_kernel(
    me_ref, after, parts_ref, spread_ref, pick_ref, air_ref, rate_ref, send_ref, flux_ref, token
):
    token[...] = jnp.zeros_like(token)
    me = me_ref[0]
    peers = parts_ref.shape[0]
    tracers, rows, columns = flux_ref.shape
    n_slots = spread_ref.shape[1]
    window = n_slots // 8
    send_ref[...] = jnp.zeros_like(send_ref)
    sent = []
    for t in range(tracers):
        parts = []
        for g in range(window):
            coupler = me - g + window // 2
            valid = (coupler >= 0) & (coupler < peers)
            block = parts_ref[jnp.clip(coupler, 0, peers - 1), t * 8 : (t + 1) * 8, :]
            parts.append(jnp.where(valid, block, 0.0))
        remapped = split_dot(spread_ref[...], jnp.concatenate(parts, axis=0), ((1,), (0,)))
        flux = rate_ref[...] * (solubility * air_ref[t] - remapped)
        for k in range(columns // LANES):
            flux_ref[t, :, k * LANES : (k + 1) * LANES] = flux[k * rows : (k + 1) * rows]
        sent.append(
            jnp.dot(pick_ref[...], flux.astype(jnp.bfloat16), preferred_element_type=jnp.float32)
        )
    for g in range(window):
        peer = me - g + window // 2

        @pl.when((peer >= 0) & (peer < peers))
        def _():
            block = jnp.concatenate([s[g * 8 : (g + 1) * 8] for s in sent], axis=0)
            send_ref[peer] = block.astype(jnp.bfloat16)


def backward_kernel(me_ref, after, recv_ref, pick_ref, w_hbm, *refs):
    held, (out_ref, token, w_rest, sems) = refs[:-4], refs[-4:]
    get_weights = all_weights(held, w_hbm, w_rest, sems)
    token[...] = jnp.zeros_like(token)
    me = me_ref[0]
    peers, width, _ = recv_ref.shape
    tracers = width // 8
    blocks, n_slots = pick_ref.shape
    window = n_slots // 8
    slots = blocks // window
    parts = [[] for _ in range(tracers)]
    for g in range(window):
        owner = me + g - window // 2
        valid = (owner >= 0) & (owner < peers)
        block = recv_ref[jnp.clip(owner, 0, peers - 1)].astype(jnp.float32)
        block = jnp.where(valid, block, 0.0)
        for t in range(tracers):
            parts[t].append(block[t * 8 : (t + 1) * 8])
    picked = [
        jnp.dot(
            pick_ref[...],
            jnp.concatenate(parts[t], axis=0).astype(jnp.bfloat16),
            preferred_element_type=jnp.float32,
        )
        for t in range(tracers)
    ]
    out_ref[...] = jnp.zeros_like(out_ref)
    row = iota((8, LANES), 0)
    for d in range(window):
        weights = get_weights(d)
        products = []
        for first in range(0, slots, 8):
            at = slice(d * slots + first, d * slots + first + 8)
            mine = [p[at] for p in picked]
            cells = jnp.concatenate(
                [
                    jnp.concatenate([jnp.where(row == k, m, 0.0) for m in mine], axis=0).astype(
                        jnp.bfloat16
                    )
                    for k in range(8)
                ],
                axis=1,
            )
            products.append(
                jnp.dot(
                    cells,
                    weights[first * LANES : (first + 8) * LANES],
                    preferred_element_type=jnp.float32,
                )
            )
        peer = me - d + window // 2

        @pl.when((peer >= 0) & (peer < peers))
        def _():
            out_ref[peer] = jnp.concatenate(products, axis=0)


def add_kernel(me_ref, returned_ref, table_ref, swept, out, buffer, surface, sems):
    me = me_ref[0]
    peers = returned_ref.shape[0]
    tracers, _, columns = surface.shape
    loads = []
    for t in range(tracers):
        loads.append(pltpu.make_async_copy(swept.at[t, 0], surface.at[t], sems.at[tracers + t]))
        loads[-1].start()
    slots = returned_ref.shape[1] // tracers
    window = table_ref.shape[1] // slots
    cuts = widths(columns)
    full = len(cuts) - 1
    rest = cuts[-1][1]
    lane = iota((8, LANES), 1)
    row = iota((8, LANES), 0)
    stays = lane < LANES - rest * row
    copies = []
    for t in range(tracers):
        parts = []
        for d in range(window):
            coupler = me + d - window // 2
            valid = (coupler >= 0) & (coupler < peers)
            for first in range(0, slots, 8):
                top = row_of(t, first, tracers)
                block = returned_ref[jnp.clip(coupler, 0, peers - 1), top : top + 8, :]
                parts.append(jnp.where(valid, block, 0.0))
        tiles = split_dot(table_ref[...], jnp.concatenate(parts, axis=0), ((1,), (0,)))
        rows = [tiles[k * 8 : (k + 1) * 8] for k in range(full + 1)]
        rows[full] = jnp.where(row == 7, rows[full], pltpu.roll(rows[0], 7, 0))
        turned = [shear(value, -1, rest) for value in rows]
        loads[t].wait()
        for k, (start, width) in enumerate(cuts):
            value = turned[k]
            if k < full:
                value = jnp.where(stays, value, turned[k + 1])
            at = slice(start, start + width)
            buffer[t, :, at] = surface[t, :, at] + ocean_rate * value[:, :width]
        copies.append(pltpu.make_async_copy(buffer.at[t], out.at[t, 0], sems.at[t]))
        copies[-1].start()
    for copy in copies:
        copy.wait()


def atmos_kernel(atmos_ref, flux_ref, mix_ref, out_ref):
    tracers, levels, rows, columns = atmos_ref.shape
    for t in range(tracers):
        for r in range(0, rows, 8):
            for c in range(0, columns, LANES):
                at = (slice(r, r + 8), slice(c, c + LANES))
                mixing = mix_ref[at]
                field = [atmos_ref[(t, v) + at] for v in range(levels)]
                field[0] = field[0] - atmos_rate * flux_ref[(t,) + at]
                for _ in range(ASTEPS):
                    field = [
                        field[v]
                        + mixing
                        * (field[max(v - 1, 0)] + field[min(v + 1, levels - 1)] - 2.0 * field[v])
                        for v in range(levels)
                    ]
                for v in range(levels):
                    out_ref[(t, v) + at] = field[v]


def local(
    ocean,
    kappa,
    atmos,
    piston,
    atmos_mix,
    fold_map,
    send_tile,
    slot_counts,
    out_slot,
    out_tile,
    remap_w,
):
    count = lax.axis_size("tile")
    me = lax.axis_index("tile").astype(jnp.int32).reshape(1)
    tracers, levels, ocean_rows, columns = ocean.shape
    planes = tracers * levels
    window, slots_in = send_tile.shape[1:]
    slots_out = out_tile.shape[2]
    blocks = window * slots_in
    n_slots = window * slots_out
    tiles = -(-columns // LANES)
    padded = tiles * LANES
    atmos_rows, atmos_columns = atmos.shape[2:]
    across = atmos_columns // LANES
    n_tiles = atmos_rows * across
    f32, bf16, i32 = jnp.float32, jnp.bfloat16, jnp.int32
    shape = jax.ShapeDtypeStruct
    dma = pltpu.SemaphoreType.DMA
    exchange = functools.partial(
        lax.all_to_all, axis_name="tile", split_axis=0, concat_axis=0, tiled=True
    )

    def cost(us):
        return pl.CostEstimate(
            flops=0, bytes_accessed=int(us * 1.0e4), transcendentals=0
        )

    token_shape = shape((8, LANES), f32)
    sent, token = pl.pallas_call(
        pack_kernel,
        out_shape=(pltpu.HBM((count, tracers * slots_in, LANES), bf16), token_shape),
        in_specs=[smem(), hbm(), hbm()],
        out_specs=(vmem(), vmem()),
        scratch_shapes=[
            pltpu.SMEM(send_tile.shape, i32),
            pltpu.VMEM((tracers, ocean_rows, columns), f32),
            pltpu.VMEM((tracers, tiles * 8, LANES), f32),
            pltpu.VMEM((window, tracers * slots_in, LANES), f32),
            dma((tracers + 1,)),
        ],
        compiler_params=params(),
        name="pack",
    )(me, in_hbm(send_tile), in_hbm(ocean))
    received = exchange(sent)

    halo_rows = 6 * planes
    flat = in_hbm(ocean.reshape(planes * ocean_rows, columns))
    weights = in_hbm(remap_w[0])
    prepared = pl.pallas_call(
        prepare_kernel,
        out_shape=(
            *[shape((slots_in,) + remap_w.shape[2:], bf16)] * HELD,
            pltpu.HBM((halo_rows, padded), bf16),
            pltpu.HBM((halo_rows, padded), bf16),
            shape((n_slots, blocks), bf16),
            shape((blocks, n_slots), bf16),
            shape((n_tiles, n_slots), bf16),
            shape((n_slots, n_tiles), bf16),
            shape((tiles * 8, blocks), bf16),
            shape((tracers, n_tiles, LANES), f32),
            shape((n_tiles, LANES), f32),
        ),
        in_specs=[smem(), vmem()] + [hbm()] * 9,
        out_specs=(vmem(),) * HELD + (hbm(),) * 2 + (vmem(),) * 7,
        scratch_shapes=[
            pltpu.VMEM((planes * ocean_rows, columns), f32),
            pltpu.VMEM((ocean_rows, columns), f32),
            pltpu.VMEM((tiles, (planes + 1) * ocean_rows, LANES), f32),
            pltpu.VMEM((halo_rows, padded), bf16),
            pltpu.VMEM((halo_rows, padded), bf16),
            pltpu.VMEM((tracers, atmos_rows, atmos_columns), f32),
            pltpu.VMEM((atmos_rows, atmos_columns), f32),
            pltpu.SMEM(slot_counts.shape, i32),
            pltpu.VMEM(out_slot.shape, i32),
            pltpu.SMEM(out_tile.shape, i32),
            pltpu.SMEM(send_tile.shape, i32),
            dma((tracers + 9 + HELD,)),
        ],
        compiler_params=params(),
        cost_estimate=cost(3),
        name="prepare",
    )(
        me,
        token,
        in_hbm(slot_counts),
        in_hbm(out_slot),
        in_hbm(out_tile),
        in_hbm(send_tile),
        flat,
        in_hbm(kappa),
        in_hbm(atmos),
        in_hbm(piston),
        weights,
    )
    held = prepared[:HELD]
    even, odd = prepared[HELD : HELD + 2]
    sum_table, slot_pick, spread, flux_pick, scatter, air, rate = prepared[HELD + 2 :]
    even_pairs = [(i, i ^ 1) for i in range(count) if i ^ 1 < count]
    odd_pairs = [(i, i + 1) for i in range(1, count - 1, 2)]
    odd_pairs += [(b, a) for a, b in odd_pairs]
    even = lax.ppermute(even, "tile", even_pairs)
    odd = lax.ppermute(odd, "tile", odd_pairs)
    weight_scratch = [
        pltpu.VMEM((blocks - HELD * slots_in,) + remap_w.shape[2:], bf16),
        dma((window - HELD,)),
    ]

    partial_sums, token = pl.pallas_call(
        forward_kernel,
        out_shape=(pltpu.HBM((count, tracers * slots_out, LANES), f32), token_shape),
        in_specs=[smem(), vmem(), vmem(), hbm()] + [vmem()] * HELD,
        out_specs=(vmem(), vmem()),
        scratch_shapes=[pltpu.VMEM((tracers, blocks, LANES), f32)] + weight_scratch,
        compiler_params=params(),
        name="forward",
    )(me, received, sum_table, weights, *held)
    owner_parts = exchange(partial_sums)

    state_shape = (16, planes, padded)
    fold = fold_map.reshape(1, columns)
    fold_scratch = [pltpu.VMEM((2 * LANES, padded), bf16)]
    state, kap, token = pl.pallas_call(
        functools.partial(first_sweep_kernel, levels=levels, peers=count),
        out_shape=(pltpu.HBM(state_shape, f32), pltpu.HBM((tiles, 16, LANES), f32), token_shape),
        in_specs=[smem(), vmem()] + [hbm()] * 4 + [vmem()],
        out_specs=(vmem(),) * 3,
        scratch_shapes=[
            pltpu.VMEM(state_shape, f32),
            pltpu.VMEM((planes * ocean_rows, columns), f32),
            pltpu.VMEM((ocean_rows, columns), f32),
            pltpu.VMEM((halo_rows, padded), bf16),
            pltpu.VMEM((halo_rows, padded), bf16),
            pltpu.VMEM((tiles, planes * ocean_rows, LANES), f32),
        ]
        + fold_scratch
        + [dma((4,))],
        compiler_params=params(),
        cost_estimate=cost(5),
        name="first_sweep",
    )(me, token, flat, in_hbm(kappa), in_hbm(even), in_hbm(odd), fold)

    flux_sent, flux, token = pl.pallas_call(
        flux_kernel,
        out_shape=(
            pltpu.HBM((count, tracers * slots_out, LANES), bf16),
            shape((tracers, atmos_rows, atmos_columns), f32),
            token_shape,
        ),
        in_specs=[smem()] + [vmem()] * 6,
        out_specs=(vmem(),) * 3,
        compiler_params=params(),
        name="flux",
    )(me, token, owner_parts, spread, flux_pick, air, rate)
    at_coupler = exchange(flux_sent)

    state, token = pl.pallas_call(
        functools.partial(second_sweep_kernel, levels=levels, peers=count),
        out_shape=(pltpu.HBM(state_shape, f32), token_shape),
        in_specs=[smem()] + [vmem()] * 4,
        out_specs=(vmem(), vmem()),
        scratch_shapes=fold_scratch,
        compiler_params=params(),
        cost_estimate=cost(3),
        name="second_sweep",
    )(me, token, in_hbm(state), in_hbm(kap), fold)

    back_sums, token = pl.pallas_call(
        backward_kernel,
        out_shape=(pltpu.HBM((count, tracers * slots_in, LANES), f32), token_shape),
        in_specs=[smem()] + [vmem()] * 3 + [hbm()] + [vmem()] * HELD,
        out_specs=(vmem(), vmem()),
        scratch_shapes=weight_scratch,
        compiler_params=params(),
        name="backward",
    )(me, token, at_coupler, slot_pick, weights, *held)
    returned = exchange(back_sums)

    swept = pl.pallas_call(
        functools.partial(last_sweeps_kernel, levels=levels, peers=count),
        out_shape=shape((planes * ocean_rows, columns), f32),
        in_specs=[smem()] + [vmem()] * 4,
        out_specs=vmem(),
        scratch_shapes=[
            pltpu.VMEM(state_shape, f32),
            pltpu.VMEM((tiles, planes * ocean_rows, LANES), f32),
        ]
        + fold_scratch,
        compiler_params=params(),
        cost_estimate=cost(4),
        name="last_sweeps",
    )(me, token, in_hbm(state), in_hbm(kap), fold)
    atmos_next = pl.pallas_call(
        atmos_kernel,
        out_shape=shape(atmos.shape, f32),
        in_specs=[vmem()] * 3,
        out_specs=vmem(),
        compiler_params=params(),
        cost_estimate=cost(1),
        name="atmos",
    )(atmos, flux, atmos_mix)

    ocean_next = pl.pallas_call(
        add_kernel,
        out_shape=shape(ocean.shape, f32),
        in_specs=[smem()] + [vmem()] * 2 + [hbm()],
        out_specs=hbm(),
        scratch_shapes=[
            pltpu.VMEM((tracers, ocean_rows, columns), f32),
            pltpu.VMEM((tracers, ocean_rows, columns), f32),
            dma((2 * tracers,)),
        ],
        input_output_aliases={3: 0},
        compiler_params=params(),
        name="add",
    )(me, returned, scatter, in_hbm(swept.reshape(ocean.shape)))
    return (ocean_next, atmos_next)


def solution(mesh):
    placed = (
        P("member", None, "tile", None),
        P("tile", None),
        P("member", None, "tile", None),
        P("tile", None),
        P("tile", None),
        P(),
        P("tile", None, None),
        P("tile", None),
        P("tile", None),
        P("tile", None, None),
        P("tile", None, None, None),
    )
    return jax.shard_map(
        local,
        mesh=mesh,
        in_specs=placed,
        out_specs=(P("member", None, "tile", None), P("member", None, "tile", None)),
        check_vma=False,
    )
```

```python
import functools

import jax
import jax.numpy as jnp
from jax import lax
from jax.experimental import pallas as pl
from jax.experimental.pallas import tpu as pltpu
from jax.sharding import PartitionSpec as P

OSTEPS = 4
ASTEPS = 4
LANES = 128
HELD = 5

vertical_mix = 0.1
ocean_rate = 4.0
atmos_rate = 0.5
solubility = 1.2

MIB = 1024 * 1024


def params(mib=16):
    return pltpu.CompilerParams(vmem_limit_bytes=36 * MIB)


def vmem():
    return pl.BlockSpec(memory_space=pltpu.VMEM)


def smem():
    return pl.BlockSpec(memory_space=pltpu.SMEM)


def hbm():
    return pl.BlockSpec(memory_space=pltpu.HBM)


def anywhere():
    return pl.BlockSpec(memory_space=pl.ANY)


def iota(shape, dim):
    return lax.broadcasted_iota(jnp.int32, shape, dim)


def split_dot(table, values, dims):
    high = values.astype(jnp.bfloat16)
    low = (values - high.astype(jnp.float32)).astype(jnp.bfloat16)
    dot = functools.partial(
        lax.dot_general, dimension_numbers=(dims, ((), ())), preferred_element_type=jnp.float32
    )
    return dot(table, high) + dot(table, low)


def shear(tile, sign, shift):
    lane = iota(tile.shape, 1)
    row = iota(tile.shape, 0)
    source = (lane - sign * shift * row) & (LANES - 1)
    return jnp.take_along_axis(tile, source, axis=1, mode="promise_in_bounds")


def widths(columns):
    return [(c, min(LANES, columns - c)) for c in range(0, columns, LANES)]


def in_hbm(x):
    return pltpu.with_memory_space_constraint(x, pltpu.HBM)


def row_of(tracer, slot, tracers):
    return (slot // 8) * 8 * tracers + tracer * 8 + slot % 8


def magic(divisor, count):
    scale = -(-65536 // divisor)
    assert all((i * scale) >> 16 == i // divisor for i in range(count))
    return scale


def tile_row(index, full, scale):
    over = (index * scale) >> 16
    return jnp.where(index == 8 * full, 8 * full + 7, (index - over * full) * 8 + over)


def one_hot(mask):
    return jnp.where(mask, 1.0, 0.0).astype(jnp.bfloat16)


def pack_kernel(me_ref, send_hbm, ocean_hbm, out_ref, token, send, surface, tiles, rows, sems):
    me = me_ref[0]
    peers = out_ref.shape[0]
    _, window, slots = send.shape
    tracers, _, columns = surface.shape
    copies = [pltpu.make_async_copy(send_hbm, send, sems.at[tracers])]
    for t in range(tracers):
        copies.append(pltpu.make_async_copy(ocean_hbm.at[t, 0], surface.at[t], sems.at[t]))
    for copy in copies:
        copy.start()
    out_ref[...] = jnp.zeros_like(out_ref)
    token[...] = jnp.zeros_like(token)
    cuts = widths(columns)
    full = len(cuts) - 1
    rest = cuts[-1][1]
    lane = iota((8, LANES), 1)
    row = iota((8, LANES), 0)
    wraps = lane < rest * row
    for t in range(tracers):
        copies[1 + t].wait()
        before = jnp.zeros((8, LANES), jnp.float32)
        first = None
        for k, (start, width) in enumerate(cuts):
            part = surface[t, :, start : start + width]
            if width < LANES:
                part = jnp.concatenate(
                    [part, jnp.zeros((8, LANES - width), jnp.float32)], axis=1
                )
            turned = shear(part, 1, rest)
            value = jnp.where(wraps, before, turned)
            before = turned
            if k == 0:
                first = value
            else:
                tiles[t, k * 8 : (k + 1) * 8] = value
        tiles[t, 0:8] = jnp.where(wraps, pltpu.roll(value, 1, 0), first)
    copies[0].wait()
    scale = magic(full, 8 * full + 1)
    for d in range(window):
        for k in range(slots):
            index = send[0, d, k]
            place = tile_row(index, full, scale)
            for t in range(tracers):
                at = row_of(t, k, tracers)
                rows[d, at : at + 1, :] = tiles[t, pl.ds(place, 1), :]
    for d in range(window):
        peer = me + d - window // 2

        @pl.when((peer >= 0) & (peer < peers))
        def _():
            out_ref[peer] = rows[d].astype(jnp.bfloat16)


def pack_halo(odd, ocean, kappa, grouped, even_ref, odd_ref):
    planes = ocean.shape[0] // 8
    cuts = widths(ocean.shape[1])
    for k, (start, width) in enumerate(cuts):
        grouped[k, 0 : planes * 8, :width] = ocean[:, start : start + width]
        grouped[k, planes * 8 :, :width] = kappa[:, start : start + width]
    for target, upper in ((even_ref, odd == 0), (odd_ref, odd == 1)):
        base = jnp.where(upper, 4, 0)
        near = jnp.where(upper, 7, 0)
        for k, (start, width) in enumerate(cuts):
            rows = [grouped[k, pl.ds(base + r, planes, stride=8), :] for r in range(4)]
            rates = grouped[k, planes * 8 :, :]
            rates = jnp.where(upper, pltpu.roll(rates, 4, 0), rates)
            nearest = grouped[k, pl.ds(near, planes, stride=8), :]
            low = nearest - nearest.astype(jnp.bfloat16).astype(jnp.float32)
            block = jnp.concatenate(rows + [rates, low], axis=0)
            target[:, start : start + LANES] = block.astype(jnp.bfloat16)


def prepare_kernel(
    me_ref,
    after,
    counts_hbm,
    slot_hbm,
    out_tile_hbm,
    send_hbm,
    ocean_hbm,
    kappa_hbm,
    atmos_hbm,
    piston_hbm,
    w_hbm,
    *refs,
):
    held = len(refs) - 21
    w_refs = refs[:held]
    even_hbm, odd_hbm = refs[held : held + 2]
    sum_ref, pick_ref, spread_ref, flux_pick_ref, scatter_ref, air_ref, rate_ref = refs[
        held + 2 : held + 9
    ]
    ocean, kappa, grouped, even, odd, surface, piston = refs[held + 9 : -5]
    counts, slot, out_tile, send, sems = refs[-5:]
    tracers, rows, columns = surface.shape
    size = w_refs[0].shape[0]
    pairs = [(counts_hbm, counts), (slot_hbm, slot), (out_tile_hbm, out_tile), (send_hbm, send)]
    pairs += [(ocean_hbm, ocean), (kappa_hbm, kappa), (piston_hbm, piston)]
    pairs += [(atmos_hbm.at[t, 0], surface.at[t]) for t in range(tracers)]
    pairs += [(w_hbm.at[pl.ds(i * size, size)], w_refs[i]) for i in range(held)]
    copies = [pltpu.make_async_copy(a, b, sems.at[i]) for i, (a, b) in enumerate(pairs)]
    for copy in copies:
        copy.start()
    n_slots, blocks = sum_ref.shape
    window, slots = send.shape[1:]
    slots_out = out_tile.shape[2]
    across = columns // LANES
    n_tiles = spread_ref.shape[0]
    full = ocean.shape[1] // LANES
    scale, scale_tile = magic(full, 8 * full + 1), magic(across, n_tiles)
    for copy in copies[:4]:
        copy.wait()
    at = iota((1, blocks), 1)
    live = at < 0
    place = jnp.zeros((1, blocks), jnp.int32)
    tile_place = jnp.zeros((1, blocks), jnp.int32)
    for d in range(window):
        live = live | ((at >= d * slots) & (at < d * slots + counts[0, d]))
        for k in range(slots):
            place = jnp.where(at == d * slots + k, tile_row(send[0, d, k], full, scale), place)
        for j in range(slots_out):
            tile = out_tile[0, d, j]
            down = (tile * scale_tile) >> 16
            value = (tile - down * across) * rows + down
            tile_place = jnp.where(at == d * slots_out + j, value, tile_place)
    table = jnp.where((iota((LANES, blocks), 0) == slot[...]) & live, 1.0, 0.0)
    sum_ref[...] = table[:n_slots].astype(jnp.bfloat16)
    pick_ref[...] = table.T[:, :n_slots].astype(jnp.bfloat16)
    spread = jnp.where(iota((LANES, LANES), 0) == tile_place, 1.0, 0.0)
    spread_ref[...] = spread[:n_tiles, :n_slots].astype(jnp.bfloat16)
    flux_pick_ref[...] = spread.T[:n_slots, :n_tiles].astype(jnp.bfloat16)
    scatter_ref[...] = one_hot(iota(scatter_ref.shape, 0) == place)
    for copy in copies[4:6]:
        copy.wait()
    pack_halo(lax.rem(me_ref[0], 2), ocean, kappa, grouped, even, odd)
    copies += [
        pltpu.make_async_copy(even, even_hbm, sems.at[len(copies)]),
        pltpu.make_async_copy(odd, odd_hbm, sems.at[len(copies) + 1]),
    ]
    for copy in copies[-2:]:
        copy.start()
    for copy in copies[6:]:
        copy.wait()
    for k in range(columns // LANES):
        at = slice(k * LANES, (k + 1) * LANES)
        rate_ref[k * rows : (k + 1) * rows, :] = piston[:, at]
        for t in range(tracers):
            air_ref[t, k * rows : (k + 1) * rows, :] = surface[t, :, at]


def fold_tables(last, fold_ref, table_ref):
    @pl.when(last)
    def _():
        inner = iota((LANES, LANES), 0)
        for start, width in widths(fold_ref.shape[1]):
            at = slice(start, start + width)
            found = one_hot(inner[:, :width] == (fold_ref[:, at] & (LANES - 1)))
            table_ref[0:LANES, at] = found
            table_ref[LANES : 2 * LANES, at] = found


def fold_row(state, table_ref, fold_ref):
    columns = fold_ref.shape[1]
    cuts = widths(columns)
    tiles = len(cuts)
    rest = cuts[-1][1]
    rows = [state[11, :, start : start + LANES] for start, _ in cuts]
    rows[-1] = jnp.where(iota((8, LANES), 1) < rest, rows[-1], 0.0)
    rows = jnp.concatenate(rows, axis=0)
    high = rows.astype(jnp.bfloat16)
    low = (rows - high.astype(jnp.float32)).astype(jnp.bfloat16)
    parts = jnp.concatenate([high, low], axis=1)
    for start in range(0, tiles * LANES, 2 * LANES):
        end = min(start + 2 * LANES, tiles * LANES)
        width = min(end, columns) - start
        found = jnp.dot(parts, table_ref[:, start:end], preferred_element_type=jnp.float32)
        at = slice(start, start + width)
        outer = jnp.broadcast_to(fold_ref[:, at] >> 7, (8, width))
        value = found[0:8, :width]
        for k in range(1, tiles):
            value = jnp.where(outer == k, found[k * 8 : (k + 1) * 8, :width], value)
        state[12, :, at] = value


def sweep_rows(state, kap, cuts, levels, low, high, write, before=None, after=None):
    full = len(cuts) - 1
    rest = cuts[-1][1]
    lane = iota((8, LANES), 1)
    level = iota((8, LANES), 0) & (levels - 1)

    def body(r, carry):
        if before is not None:
            before(r)

        def cell(k):
            return state[r, :, k * LANES : (k + 1) * LANES]

        centre = cell(0)
        east_now = pltpu.roll(centre, LANES - 1, 1)
        around = pltpu.roll(centre, rest - 1, 1)
        west_last = pltpu.roll(cell(full), LANES - rest + 1, 1)
        for k in range(full + 1):
            at = slice(k * LANES, (k + 1) * LANES)
            if k == full:
                east = jnp.where(lane == rest - 1, around, east_now)
            else:
                following = cell(k + 1)
                east_next = pltpu.roll(following, LANES - 1, 1)
                east = jnp.where(lane == LANES - 1, east_next, east_now)
            west_now = pltpu.roll(centre, 1, 1)
            west = jnp.where(lane == 0, west_last, west_now)
            north = state[r + 1, :, at]
            south = state[r - 1, :, at]
            upper = jnp.where(level == 0, centre, pltpu.roll(centre, 1, 0))
            lower = jnp.where(level == levels - 1, centre, pltpu.roll(centre, 7, 0))
            horizontal = (north + south) + (east + west) - 4.0 * centre
            vertical = upper + lower - 2.0 * centre
            rate = kap[k, pl.ds(r, 1), :]
            write(r, k, centre + rate * horizontal + vertical_mix * vertical)
            if k < full:
                centre, east_now, west_last = following, east_next, west_now
        if after is not None:
            after(r)
        return carry

    lax.fori_loop(low, high, body, 0)


def keep(target):
    def write(r, k, value):
        target[r, :, k * LANES : (k + 1) * LANES] = value

    return write


def row_copy(source, target, sems, r):
    return pltpu.make_async_copy(source.at[r], target.at[r], sems.at[r])


def sweep_and_send(
    state, kap, cuts, levels, low, high, kept, out_hbm, sems, last, table, fold_ref, before=None
):
    def after(r):
        @pl.when(jnp.logical_not(last & (r == 12)))
        def _():
            row_copy(kept, out_hbm, sems, r).start()

    sweep_rows(state, kap, cuts, levels, low, high, keep(kept), before, after)

    @pl.when(last)
    def _():
        fold_row(kept, table, fold_ref)
        row_copy(kept, out_hbm, sems, 12).start()

    for r in range(low, high):
        row_copy(kept, out_hbm, sems, r).wait()


def fetch_rows(state_hbm, state, kap_hbm, kap, sems, low, high):
    kap_copy = pltpu.make_async_copy(kap_hbm, kap, sems.at[0])
    kap_copy.start()
    for r in range(low, high):
        row_copy(state_hbm, state, sems, r).start()
    kap_copy.wait()
    row_copy(state_hbm, state, sems, low).wait()
    row_copy(state_hbm, state, sems, low + 1).wait()

    def before(r):
        row_copy(state_hbm, state, sems, r + 1).wait()

    return before


def first_sweep_kernel(
    me_ref,
    after,
    ocean_hbm,
    kappa_hbm,
    even_hbm,
    odd_hbm,
    fold_ref,
    out_hbm,
    kap_hbm,
    token,
    state,
    kept,
    kap_ref,
    ocean,
    kappa,
    above,
    below,
    grouped,
    table,
    sems,
    row_sems,
    levels,
    peers,
):
    me = me_ref[0]
    last = me == peers - 1
    odd = lax.rem(me, 2)
    token[...] = jnp.zeros_like(token)
    planes = state.shape[1]
    cuts = widths(kappa.shape[1])
    copies = [
        pltpu.make_async_copy(ocean_hbm, ocean, sems.at[0]),
        pltpu.make_async_copy(kappa_hbm, kappa, sems.at[1]),
    ]
    for copy in copies:
        copy.start()

    @pl.when(odd == 1)
    def _():
        pltpu.make_async_copy(odd_hbm, above, sems.at[2]).start()
        pltpu.make_async_copy(even_hbm, below, sems.at[3]).start()

    @pl.when(odd == 0)
    def _():
        pltpu.make_async_copy(even_hbm, above, sems.at[2]).start()
        pltpu.make_async_copy(odd_hbm, below, sems.at[3]).start()

    fold_tables(last, fold_ref, table)
    for copy in copies:
        copy.wait()
    for k, (start, width) in enumerate(cuts):
        grouped[k, :, :width] = ocean[:, start : start + width]
        kap_ref[k, 4:12, :width] = kappa[:, start : start + width]
    for k, (start, width) in enumerate(cuts):
        for r in range(8):
            part = grouped[k, pl.ds(r, planes, stride=8), :]
            state[4 + r, :, start : start + LANES] = part
    pltpu.make_async_copy(even_hbm, above, sems.at[2]).wait()
    pltpu.make_async_copy(odd_hbm, below, sems.at[3]).wait()
    for halo, first, near in ((below, 0, 3), (above, 12, 0)):
        for k, (start, _) in enumerate(cuts):
            at = slice(start, start + LANES)
            block = halo[:, at].astype(jnp.float32)
            for r in range(4):
                value = block[r * planes : (r + 1) * planes]
                if r == near:
                    value = value + block[5 * planes : 6 * planes]
                state[first + r, :, at] = value
            kap_ref[k, first : first + 4, :] = block[4 * planes : 4 * planes + 4]

    @pl.when(last)
    def _():
        fold_row(state, table, fold_ref)

    kap_copy = pltpu.make_async_copy(kap_ref, kap_hbm, row_sems.at[0])
    kap_copy.start()
    sweep_and_send(
        state, kap_ref, cuts, levels, 1, 15, kept, out_hbm, row_sems, last, table, fold_ref
    )
    kap_copy.wait()


def second_sweep_kernel(
    me_ref,
    after,
    state_hbm,
    kap_hbm,
    fold_ref,
    out_hbm,
    token,
    state,
    kap,
    kept,
    table,
    sems,
    out_sems,
    levels,
    peers,
):
    token[...] = jnp.zeros_like(token)
    last = me_ref[0] == peers - 1
    before = fetch_rows(state_hbm, state, kap_hbm, kap, sems, 1, 15)
    fold_tables(last, fold_ref, table)
    cuts = widths(fold_ref.shape[1])
    sweep_and_send(
        state, kap, cuts, levels, 2, 14, kept, out_hbm, out_sems, last, table, fold_ref, before
    )


def last_sweeps_kernel(
    me_ref,
    after,
    state_hbm,
    kap_hbm,
    fold_ref,
    out_ref,
    came,
    kap_ref,
    state,
    grouped,
    table,
    sems,
    levels,
    peers,
):
    cuts = widths(out_ref.shape[1])
    planes = came.shape[1]
    last = me_ref[0] == peers - 1
    before = fetch_rows(state_hbm, came, kap_hbm, kap_ref, sems, 2, 14)
    fold_tables(last, fold_ref, table)
    sweep_rows(came, kap_ref, cuts, levels, 3, 13, keep(state), before)

    @pl.when(last)
    def _():
        fold_row(state, table, fold_ref)

    def write(r, k, value):
        grouped[k, pl.ds(r - 4, planes, stride=8), :] = value

    sweep_rows(state, kap_ref, cuts, levels, 4, 12, write)
    for k, (start, width) in enumerate(cuts):
        out_ref[:, start : start + width] = grouped[k, :, :width]


def all_weights(held, w_hbm, w_rest, sems):
    size = held[0].shape[0]
    first = len(held) * size
    copies = []
    for i in range(w_rest.shape[0] // size):
        part = pl.ds(i * size, size)
        source = w_hbm.at[pl.ds(first + i * size, size)]
        copies.append(pltpu.make_async_copy(source, w_rest.at[part], sems.at[i]))
        copies[-1].start()

    def get(d):
        if d < len(held):
            weights = held[d][...]
        else:
            at = d - len(held)
            copies[at].wait()
            weights = w_rest[at * size : (at + 1) * size]
        return weights.reshape(size * LANES, LANES)

    return get


def forward_kernel(me_ref, recv_ref, sum_ref, w_hbm, *refs):
    held, (out_ref, token, sums, w_rest, sems) = refs[:-5], refs[-5:]
    get_weights = all_weights(held, w_hbm, w_rest, sems)
    token[...] = jnp.zeros_like(token)
    me = me_ref[0]
    peers = recv_ref.shape[0]
    tracers, blocks, _ = sums.shape
    n_slots = sum_ref.shape[0]
    window = n_slots // 8
    slots = blocks // window
    row = iota((8, LANES), 0)
    out_ref[...] = jnp.zeros_like(out_ref)
    for d in range(window):
        source = jnp.clip(me - d + window // 2, 0, peers - 1)
        weights = get_weights(d)
        for first in range(0, slots, 8):
            top = row_of(0, first, tracers)
            cells = recv_ref[source, top : top + 8 * tracers, :]
            product = lax.dot_general(
                cells,
                weights[first * LANES : (first + 8) * LANES],
                (((1,), (1,)), ((), ())),
                preferred_element_type=jnp.float32,
            )
            for t in range(tracers):
                part = product[t * 8 : (t + 1) * 8]
                found = part[:, :LANES]
                for k in range(1, 8):
                    found = jnp.where(row == k, part[:, k * LANES : (k + 1) * LANES], found)
                sums[t, d * slots + first : d * slots + first + 8, :] = found
    partial_sums = [split_dot(sum_ref[...], sums[t], ((1,), (0,))) for t in range(tracers)]
    for g in range(window):
        peer = me + g - window // 2

        @pl.when((peer >= 0) & (peer < peers))
        def _():
            for t in range(tracers):
                out_ref[peer, t * 8 : (t + 1) * 8, :] = partial_sums[t][g * 8 : (g + 1) * 8]


def flux_kernel(
    me_ref, after, parts_ref, spread_ref, pick_ref, air_ref, rate_ref, send_ref, flux_ref, token
):
    token[...] = jnp.zeros_like(token)
    me = me_ref[0]
    peers = parts_ref.shape[0]
    tracers, rows, columns = flux_ref.shape
    n_slots = spread_ref.shape[1]
    window = n_slots // 8
    send_ref[...] = jnp.zeros_like(send_ref)
    sent = []
    for t in range(tracers):
        parts = []
        for g in range(window):
            coupler = me - g + window // 2
            valid = (coupler >= 0) & (coupler < peers)
            block = parts_ref[jnp.clip(coupler, 0, peers - 1), t * 8 : (t + 1) * 8, :]
            parts.append(jnp.where(valid, block, 0.0))
        remapped = split_dot(spread_ref[...], jnp.concatenate(parts, axis=0), ((1,), (0,)))
        flux = rate_ref[...] * (solubility * air_ref[t] - remapped)
        for k in range(columns // LANES):
            flux_ref[t, :, k * LANES : (k + 1) * LANES] = flux[k * rows : (k + 1) * rows]
        sent.append(
            jnp.dot(pick_ref[...], flux.astype(jnp.bfloat16), preferred_element_type=jnp.float32)
        )
    for g in range(window):
        peer = me - g + window // 2

        @pl.when((peer >= 0) & (peer < peers))
        def _():
            block = jnp.concatenate([s[g * 8 : (g + 1) * 8] for s in sent], axis=0)
            send_ref[peer] = block.astype(jnp.bfloat16)


def backward_kernel(me_ref, after, after_too, recv_ref, pick_ref, w_hbm, *refs):
    held, (out_ref, token, w_rest, sems) = refs[:-4], refs[-4:]
    get_weights = all_weights(held, w_hbm, w_rest, sems)
    token[...] = jnp.zeros_like(token)
    me = me_ref[0]
    peers, width, _ = recv_ref.shape
    tracers = width // 8
    blocks, n_slots = pick_ref.shape
    window = n_slots // 8
    slots = blocks // window
    parts = [[] for _ in range(tracers)]
    for g in range(window):
        owner = me + g - window // 2
        valid = (owner >= 0) & (owner < peers)
        block = recv_ref[jnp.clip(owner, 0, peers - 1)].astype(jnp.float32)
        block = jnp.where(valid, block, 0.0)
        for t in range(tracers):
            parts[t].append(block[t * 8 : (t + 1) * 8])
    picked = [
        jnp.dot(
            pick_ref[...],
            jnp.concatenate(parts[t], axis=0).astype(jnp.bfloat16),
            preferred_element_type=jnp.float32,
        )
        for t in range(tracers)
    ]
    out_ref[...] = jnp.zeros_like(out_ref)
    row = iota((8, LANES), 0)
    for d in range(window):
        weights = get_weights(d)
        products = []
        for first in range(0, slots, 8):
            at = slice(d * slots + first, d * slots + first + 8)
            mine = [p[at] for p in picked]
            cells = jnp.concatenate(
                [
                    jnp.concatenate([jnp.where(row == k, m, 0.0) for m in mine], axis=0).astype(
                        jnp.bfloat16
                    )
                    for k in range(8)
                ],
                axis=1,
            )
            products.append(
                jnp.dot(
                    cells,
                    weights[first * LANES : (first + 8) * LANES],
                    preferred_element_type=jnp.float32,
                )
            )
        peer = me - d + window // 2

        @pl.when((peer >= 0) & (peer < peers))
        def _():
            out_ref[peer] = jnp.concatenate(products, axis=0)


def add_kernel(me_ref, returned_ref, table_ref, swept, out, buffer, surface, sems):
    me = me_ref[0]
    peers = returned_ref.shape[0]
    tracers, _, columns = surface.shape
    loads = []
    for t in range(tracers):
        loads.append(pltpu.make_async_copy(swept.at[t, 0], surface.at[t], sems.at[tracers + t]))
        loads[-1].start()
    slots = returned_ref.shape[1] // tracers
    window = table_ref.shape[1] // slots
    cuts = widths(columns)
    full = len(cuts) - 1
    rest = cuts[-1][1]
    lane = iota((8, LANES), 1)
    row = iota((8, LANES), 0)
    stays = lane < LANES - rest * row
    copies = []
    for t in range(tracers):
        parts = []
        for d in range(window):
            coupler = me + d - window // 2
            valid = (coupler >= 0) & (coupler < peers)
            for first in range(0, slots, 8):
                top = row_of(t, first, tracers)
                block = returned_ref[jnp.clip(coupler, 0, peers - 1), top : top + 8, :]
                parts.append(jnp.where(valid, block, 0.0))
        tiles = split_dot(table_ref[...], jnp.concatenate(parts, axis=0), ((1,), (0,)))
        rows = [tiles[k * 8 : (k + 1) * 8] for k in range(full + 1)]
        rows[full] = jnp.where(row == 7, rows[full], pltpu.roll(rows[0], 7, 0))
        turned = [shear(value, -1, rest) for value in rows]
        loads[t].wait()
        for k, (start, width) in enumerate(cuts):
            value = turned[k]
            if k < full:
                value = jnp.where(stays, value, turned[k + 1])
            at = slice(start, start + width)
            buffer[t, :, at] = surface[t, :, at] + ocean_rate * value[:, :width]
        copies.append(pltpu.make_async_copy(buffer.at[t], out.at[t, 0], sems.at[t]))
        copies[-1].start()
    for copy in copies:
        copy.wait()


def atmos_kernel(after, atmos_ref, flux_ref, mix_ref, out_ref, token):
    token[...] = jnp.zeros_like(token)
    tracers, levels, rows, columns = atmos_ref.shape
    for t in range(tracers):
        for r in range(0, rows, 8):
            for c in range(0, columns, LANES):
                at = (slice(r, r + 8), slice(c, c + LANES))
                mixing = mix_ref[at]
                field = [atmos_ref[(t, v) + at] for v in range(levels)]
                field[0] = field[0] - atmos_rate * flux_ref[(t,) + at]
                for _ in range(ASTEPS):
                    field = [
                        field[v]
                        + mixing
                        * (field[max(v - 1, 0)] + field[min(v + 1, levels - 1)] - 2.0 * field[v])
                        for v in range(levels)
                    ]
                for v in range(levels):
                    out_ref[(t, v) + at] = field[v]


def local(
    ocean,
    kappa,
    atmos,
    piston,
    atmos_mix,
    fold_map,
    send_tile,
    slot_counts,
    out_slot,
    out_tile,
    remap_w,
):
    count = lax.axis_size("tile")
    me = lax.axis_index("tile").astype(jnp.int32).reshape(1)
    tracers, levels, ocean_rows, columns = ocean.shape
    planes = tracers * levels
    window, slots_in = send_tile.shape[1:]
    slots_out = out_tile.shape[2]
    blocks = window * slots_in
    n_slots = window * slots_out
    tiles = -(-columns // LANES)
    padded = tiles * LANES
    atmos_rows, atmos_columns = atmos.shape[2:]
    across = atmos_columns // LANES
    n_tiles = atmos_rows * across
    f32, bf16, i32 = jnp.float32, jnp.bfloat16, jnp.int32
    shape = jax.ShapeDtypeStruct
    dma = pltpu.SemaphoreType.DMA
    exchange = functools.partial(
        lax.all_to_all, axis_name="tile", split_axis=0, concat_axis=0, tiled=True
    )

    def cost(us):
        return pl.CostEstimate(
            flops=0, bytes_accessed=int(us * 1.0e4), transcendentals=0
        )

    token_shape = shape((8, LANES), f32)
    sent, token = pl.pallas_call(
        pack_kernel,
        out_shape=(pltpu.HBM((count, tracers * slots_in, LANES), bf16), token_shape),
        in_specs=[smem(), hbm(), hbm()],
        out_specs=(vmem(), vmem()),
        scratch_shapes=[
            pltpu.SMEM(send_tile.shape, i32),
            pltpu.VMEM((tracers, ocean_rows, columns), f32),
            pltpu.VMEM((tracers, tiles * 8, LANES), f32),
            pltpu.VMEM((window, tracers * slots_in, LANES), f32),
            dma((tracers + 1,)),
        ],
        compiler_params=params(),
        name="pack",
    )(me, in_hbm(send_tile), in_hbm(ocean))
    received = exchange(sent)

    halo_rows = 6 * planes
    flat = in_hbm(ocean.reshape(planes * ocean_rows, columns))
    weights = in_hbm(remap_w[0])
    prepared = pl.pallas_call(
        prepare_kernel,
        out_shape=(
            *[shape((slots_in,) + remap_w.shape[2:], bf16)] * HELD,
            pltpu.HBM((halo_rows, padded), bf16),
            pltpu.HBM((halo_rows, padded), bf16),
            shape((n_slots, blocks), bf16),
            shape((blocks, n_slots), bf16),
            shape((n_tiles, n_slots), bf16),
            shape((n_slots, n_tiles), bf16),
            shape((tiles * 8, blocks), bf16),
            shape((tracers, n_tiles, LANES), f32),
            shape((n_tiles, LANES), f32),
        ),
        in_specs=[smem(), vmem()] + [hbm()] * 9,
        out_specs=(vmem(),) * HELD + (hbm(),) * 2 + (vmem(),) * 7,
        scratch_shapes=[
            pltpu.VMEM((planes * ocean_rows, columns), f32),
            pltpu.VMEM((ocean_rows, columns), f32),
            pltpu.VMEM((tiles, (planes + 1) * ocean_rows, LANES), f32),
            pltpu.VMEM((halo_rows, padded), bf16),
            pltpu.VMEM((halo_rows, padded), bf16),
            pltpu.VMEM((tracers, atmos_rows, atmos_columns), f32),
            pltpu.VMEM((atmos_rows, atmos_columns), f32),
            pltpu.SMEM(slot_counts.shape, i32),
            pltpu.VMEM(out_slot.shape, i32),
            pltpu.SMEM(out_tile.shape, i32),
            pltpu.SMEM(send_tile.shape, i32),
            dma((tracers + 9 + HELD,)),
        ],
        compiler_params=params(),
        cost_estimate=cost(3),
        name="prepare",
    )(
        me,
        token,
        in_hbm(slot_counts),
        in_hbm(out_slot),
        in_hbm(out_tile),
        in_hbm(send_tile),
        flat,
        in_hbm(kappa),
        in_hbm(atmos),
        in_hbm(piston),
        weights,
    )
    held = prepared[:HELD]
    even, odd = prepared[HELD : HELD + 2]
    sum_table, slot_pick, spread, flux_pick, scatter, air, rate = prepared[HELD + 2 :]
    even_pairs = [(i, i ^ 1) for i in range(count) if i ^ 1 < count]
    odd_pairs = [(i, i + 1) for i in range(1, count - 1, 2)]
    odd_pairs += [(b, a) for a, b in odd_pairs]
    even = lax.ppermute(even, "tile", even_pairs)
    odd = lax.ppermute(odd, "tile", odd_pairs)
    weight_scratch = [
        pltpu.VMEM((blocks - HELD * slots_in,) + remap_w.shape[2:], bf16),
        dma((window - HELD,)),
    ]

    partial_sums, token = pl.pallas_call(
        forward_kernel,
        out_shape=(pltpu.HBM((count, tracers * slots_out, LANES), f32), token_shape),
        in_specs=[smem(), vmem(), vmem(), hbm()] + [vmem()] * HELD,
        out_specs=(vmem(), vmem()),
        scratch_shapes=[pltpu.VMEM((tracers, blocks, LANES), f32)] + weight_scratch,
        compiler_params=params(),
        name="forward",
    )(me, received, sum_table, weights, *held)
    owner_parts = exchange(partial_sums)

    state_shape = (16, planes, padded)
    kap_shape = (tiles, 16, LANES)
    fold = fold_map.reshape(1, columns)
    fold_scratch = [pltpu.VMEM((2 * LANES, padded), bf16)]
    state, kap, token = pl.pallas_call(
        functools.partial(first_sweep_kernel, levels=levels, peers=count),
        out_shape=(pltpu.HBM(state_shape, f32), pltpu.HBM((tiles, 16, LANES), f32), token_shape),
        in_specs=[smem(), vmem()] + [hbm()] * 4 + [vmem()],
        out_specs=(hbm(), hbm(), vmem()),
        scratch_shapes=[
            pltpu.VMEM(state_shape, f32),
            pltpu.VMEM(state_shape, f32),
            pltpu.VMEM(kap_shape, f32),
            pltpu.VMEM((planes * ocean_rows, columns), f32),
            pltpu.VMEM((ocean_rows, columns), f32),
            pltpu.VMEM((halo_rows, padded), bf16),
            pltpu.VMEM((halo_rows, padded), bf16),
            pltpu.VMEM((tiles, planes * ocean_rows, LANES), f32),
        ]
        + fold_scratch
        + [dma((4,)), dma((16,))],
        compiler_params=params(),
        cost_estimate=cost(5),
        name="first_sweep",
    )(me, token, flat, in_hbm(kappa), in_hbm(even), in_hbm(odd), fold)

    flux_sent, flux, flux_token = pl.pallas_call(
        flux_kernel,
        out_shape=(
            pltpu.HBM((count, tracers * slots_out, LANES), bf16),
            shape((tracers, atmos_rows, atmos_columns), f32),
            token_shape,
        ),
        in_specs=[smem()] + [vmem()] * 6,
        out_specs=(vmem(),) * 3,
        compiler_params=params(),
        name="flux",
    )(me, token, owner_parts, spread, flux_pick, air, rate)
    at_coupler = exchange(flux_sent)

    state, token = pl.pallas_call(
        functools.partial(second_sweep_kernel, levels=levels, peers=count),
        out_shape=(pltpu.HBM(state_shape, f32), token_shape),
        in_specs=[smem(), vmem(), hbm(), hbm(), vmem()],
        out_specs=(hbm(), vmem()),
        scratch_shapes=[
            pltpu.VMEM(state_shape, f32),
            pltpu.VMEM(kap_shape, f32),
            pltpu.VMEM(state_shape, f32),
        ]
        + fold_scratch
        + [dma((16,)), dma((16,))],
        compiler_params=params(),
        cost_estimate=cost(3),
        name="second_sweep",
    )(me, flux_token, in_hbm(state), in_hbm(kap), fold)

    atmos_next, air_token = pl.pallas_call(
        atmos_kernel,
        out_shape=(shape(atmos.shape, f32), token_shape),
        in_specs=[vmem()] * 4,
        out_specs=(vmem(), vmem()),
        compiler_params=params(),
        cost_estimate=cost(1),
        name="atmos",
    )(flux_token, atmos, flux, atmos_mix)

    back_sums, token = pl.pallas_call(
        backward_kernel,
        out_shape=(shape((count, tracers * slots_in, LANES), f32), token_shape),
        in_specs=[smem()] + [vmem()] * 4 + [hbm()] + [vmem()] * HELD,
        out_specs=(vmem(), vmem()),
        scratch_shapes=weight_scratch,
        compiler_params=params(),
        name="backward",
    )(me, token, air_token, at_coupler, slot_pick, weights, *held)
    returned = exchange(back_sums.astype(jnp.float16)).astype(f32)

    swept = pl.pallas_call(
        functools.partial(last_sweeps_kernel, levels=levels, peers=count),
        out_shape=shape((planes * ocean_rows, columns), f32),
        in_specs=[smem(), vmem(), hbm(), hbm(), vmem()],
        out_specs=vmem(),
        scratch_shapes=[
            pltpu.VMEM(state_shape, f32),
            pltpu.VMEM(kap_shape, f32),
            pltpu.VMEM(state_shape, f32),
            pltpu.VMEM((tiles, planes * ocean_rows, LANES), f32),
        ]
        + fold_scratch
        + [dma((16,))],
        compiler_params=params(),
        cost_estimate=cost(4),
        name="last_sweeps",
    )(me, token, in_hbm(state), in_hbm(kap), fold)
    ocean_next = pl.pallas_call(
        add_kernel,
        out_shape=shape(ocean.shape, f32),
        in_specs=[smem()] + [vmem()] * 2 + [hbm()],
        out_specs=hbm(),
        scratch_shapes=[
            pltpu.VMEM((tracers, ocean_rows, columns), f32),
            pltpu.VMEM((tracers, ocean_rows, columns), f32),
            dma((2 * tracers,)),
        ],
        input_output_aliases={3: 0},
        compiler_params=params(),
        name="add",
    )(me, returned, scatter, in_hbm(swept.reshape(ocean.shape)))
    return (ocean_next, atmos_next)


def solution(mesh):
    placed = (
        P("member", None, "tile", None),
        P("tile", None),
        P("member", None, "tile", None),
        P("tile", None),
        P("tile", None),
        P(),
        P("tile", None, None),
        P("tile", None),
        P("tile", None),
        P("tile", None, None),
        P("tile", None, None, None),
    )
    return jax.shard_map(
        local,
        mesh=mesh,
        in_specs=placed,
        out_specs=(P("member", None, "tile", None), P("member", None, "tile", None)),
        check_vma=False,
    )
```

```python
import functools

import jax
import jax.numpy as jnp
from jax import lax
from jax.experimental import pallas as pl
from jax.experimental.pallas import tpu as pltpu
from jax.sharding import PartitionSpec as P

OSTEPS = 4
ASTEPS = 4
LANES = 128
HELD = 6

vertical_mix = 0.1
ocean_rate = 4.0
atmos_rate = 0.5
solubility = 1.2

MIB = 1024 * 1024


def params(mib=16):
    return pltpu.CompilerParams(vmem_limit_bytes=36 * MIB)


def vmem():
    return pl.BlockSpec(memory_space=pltpu.VMEM)


def smem():
    return pl.BlockSpec(memory_space=pltpu.SMEM)


def hbm():
    return pl.BlockSpec(memory_space=pltpu.HBM)


def anywhere():
    return pl.BlockSpec(memory_space=pl.ANY)


def iota(shape, dim):
    return lax.broadcasted_iota(jnp.int32, shape, dim)


def split_dot(table, values, dims):
    high = values.astype(jnp.bfloat16)
    low = (values - high.astype(jnp.float32)).astype(jnp.bfloat16)
    dot = functools.partial(
        lax.dot_general, dimension_numbers=(dims, ((), ())), preferred_element_type=jnp.float32
    )
    return dot(table, high) + dot(table, low)


def shear(tile, sign, shift):
    lane = iota(tile.shape, 1)
    row = iota(tile.shape, 0)
    source = (lane - sign * shift * row) & (LANES - 1)
    return jnp.take_along_axis(tile, source, axis=1, mode="promise_in_bounds")


def widths(columns):
    return [(c, min(LANES, columns - c)) for c in range(0, columns, LANES)]


def in_hbm(x):
    return pltpu.with_memory_space_constraint(x, pltpu.HBM)


def row_of(tracer, slot, tracers):
    return (slot // 8) * 8 * tracers + tracer * 8 + slot % 8


def magic(divisor, count):
    scale = -(-65536 // divisor)
    assert all((i * scale) >> 16 == i // divisor for i in range(count))
    return scale


def tile_row(index, full, scale):
    over = (index * scale) >> 16
    return jnp.where(index == 8 * full, 8 * full + 7, (index - over * full) * 8 + over)


def one_hot(mask):
    return jnp.where(mask, 1.0, 0.0).astype(jnp.bfloat16)


def pack_kernel(me_ref, send_hbm, ocean_hbm, out_ref, token, send, surface, tiles, rows, sems):
    me = me_ref[0]
    peers = out_ref.shape[0]
    _, window, slots = send.shape
    tracers, _, columns = surface.shape
    copies = [pltpu.make_async_copy(send_hbm, send, sems.at[tracers])]
    for t in range(tracers):
        copies.append(pltpu.make_async_copy(ocean_hbm.at[t, 0], surface.at[t], sems.at[t]))
    for copy in copies:
        copy.start()
    out_ref[...] = jnp.zeros_like(out_ref)
    token[...] = jnp.zeros_like(token)
    cuts = widths(columns)
    full = len(cuts) - 1
    rest = cuts[-1][1]
    lane = iota((8, LANES), 1)
    row = iota((8, LANES), 0)
    wraps = lane < rest * row
    for t in range(tracers):
        copies[1 + t].wait()
        before = jnp.zeros((8, LANES), jnp.float32)
        first = None
        for k, (start, width) in enumerate(cuts):
            part = surface[t, :, start : start + width]
            if width < LANES:
                part = jnp.concatenate(
                    [part, jnp.zeros((8, LANES - width), jnp.float32)], axis=1
                )
            turned = shear(part, 1, rest)
            value = jnp.where(wraps, before, turned)
            before = turned
            if k == 0:
                first = value
            else:
                tiles[t, k * 8 : (k + 1) * 8] = value
        tiles[t, 0:8] = jnp.where(wraps, pltpu.roll(value, 1, 0), first)
    copies[0].wait()
    scale = magic(full, 8 * full + 1)
    for d in range(window):
        for k in range(slots):
            index = send[0, d, k]
            place = tile_row(index, full, scale)
            for t in range(tracers):
                at = row_of(t, k, tracers)
                rows[d, at : at + 1, :] = tiles[t, pl.ds(place, 1), :]
    for d in range(window):
        peer = me + d - window // 2

        @pl.when((peer >= 0) & (peer < peers))
        def _():
            out_ref[peer] = rows[d].astype(jnp.bfloat16)


def pack_halo(odd, ocean, kappa, grouped, even_ref, odd_ref):
    planes = ocean.shape[0] // 8
    cuts = widths(ocean.shape[1])
    for k, (start, width) in enumerate(cuts):
        grouped[k, 0 : planes * 8, :width] = ocean[:, start : start + width]
        grouped[k, planes * 8 :, :width] = kappa[:, start : start + width]
    for target, upper in ((even_ref, odd == 0), (odd_ref, odd == 1)):
        base = jnp.where(upper, 4, 0)
        near = jnp.where(upper, 7, 0)
        for k, (start, width) in enumerate(cuts):
            rows = [grouped[k, pl.ds(base + r, planes, stride=8), :] for r in range(4)]
            rates = grouped[k, planes * 8 :, :]
            rates = jnp.where(upper, pltpu.roll(rates, 4, 0), rates)
            nearest = grouped[k, pl.ds(near, planes, stride=8), :]
            low = nearest - nearest.astype(jnp.bfloat16).astype(jnp.float32)
            block = jnp.concatenate(rows + [rates, low], axis=0)
            target[:, start : start + LANES] = block.astype(jnp.bfloat16)


def prepare_kernel(
    me_ref,
    after,
    counts_hbm,
    slot_hbm,
    out_tile_hbm,
    send_hbm,
    ocean_hbm,
    kappa_hbm,
    atmos_hbm,
    piston_hbm,
    w_hbm,
    *refs,
):
    held = len(refs) - 21
    w_refs = refs[:held]
    even_hbm, odd_hbm = refs[held : held + 2]
    sum_ref, pick_ref, spread_ref, flux_pick_ref, scatter_ref, air_ref, rate_ref = refs[
        held + 2 : held + 9
    ]
    ocean, kappa, grouped, even, odd, surface, piston = refs[held + 9 : -5]
    counts, slot, out_tile, send, sems = refs[-5:]
    tracers, rows, columns = surface.shape
    size = w_refs[0].shape[0]
    pairs = [(counts_hbm, counts), (slot_hbm, slot), (out_tile_hbm, out_tile), (send_hbm, send)]
    pairs += [(ocean_hbm, ocean), (kappa_hbm, kappa), (piston_hbm, piston)]
    pairs += [(atmos_hbm.at[t, 0], surface.at[t]) for t in range(tracers)]
    pairs += [(w_hbm.at[pl.ds(i * size, size)], w_refs[i]) for i in range(held)]
    copies = [pltpu.make_async_copy(a, b, sems.at[i]) for i, (a, b) in enumerate(pairs)]
    for copy in copies:
        copy.start()
    n_slots, blocks = sum_ref.shape
    window, slots = send.shape[1:]
    slots_out = out_tile.shape[2]
    across = columns // LANES
    n_tiles = spread_ref.shape[0]
    full = ocean.shape[1] // LANES
    scale, scale_tile = magic(full, 8 * full + 1), magic(across, n_tiles)
    for copy in copies[:4]:
        copy.wait()
    at = iota((1, blocks), 1)
    live = at < 0
    place = jnp.zeros((1, blocks), jnp.int32)
    tile_place = jnp.zeros((1, blocks), jnp.int32)
    for d in range(window):
        live = live | ((at >= d * slots) & (at < d * slots + counts[0, d]))
        for k in range(slots):
            place = jnp.where(at == d * slots + k, tile_row(send[0, d, k], full, scale), place)
        for j in range(slots_out):
            tile = out_tile[0, d, j]
            down = (tile * scale_tile) >> 16
            value = (tile - down * across) * rows + down
            tile_place = jnp.where(at == d * slots_out + j, value, tile_place)
    table = jnp.where((iota((LANES, blocks), 0) == slot[...]) & live, 1.0, 0.0)
    sum_ref[...] = table[:n_slots].astype(jnp.bfloat16)
    pick_ref[...] = table.T[:, :n_slots].astype(jnp.bfloat16)
    spread = jnp.where(iota((LANES, LANES), 0) == tile_place, 1.0, 0.0)
    spread_ref[...] = spread[:n_tiles, :n_slots].astype(jnp.bfloat16)
    flux_pick_ref[...] = spread.T[:n_slots, :n_tiles].astype(jnp.bfloat16)
    scatter_ref[...] = one_hot(iota(scatter_ref.shape, 0) == place)
    for copy in copies[4:6]:
        copy.wait()
    pack_halo(lax.rem(me_ref[0], 2), ocean, kappa, grouped, even, odd)
    copies += [
        pltpu.make_async_copy(even, even_hbm, sems.at[len(copies)]),
        pltpu.make_async_copy(odd, odd_hbm, sems.at[len(copies) + 1]),
    ]
    for copy in copies[-2:]:
        copy.start()
    for copy in copies[6:]:
        copy.wait()
    for k in range(columns // LANES):
        at = slice(k * LANES, (k + 1) * LANES)
        rate_ref[k * rows : (k + 1) * rows, :] = piston[:, at]
        for t in range(tracers):
            air_ref[t, k * rows : (k + 1) * rows, :] = surface[t, :, at]


def fold_tables(last, fold_ref, table_ref):
    @pl.when(last)
    def _():
        inner = iota((LANES, LANES), 0)
        for start, width in widths(fold_ref.shape[1]):
            at = slice(start, start + width)
            found = one_hot(inner[:, :width] == (fold_ref[:, at] & (LANES - 1)))
            table_ref[0:LANES, at] = found
            table_ref[LANES : 2 * LANES, at] = found


def fold_row(state, table_ref, fold_ref):
    columns = fold_ref.shape[1]
    cuts = widths(columns)
    tiles = len(cuts)
    rest = cuts[-1][1]
    rows = [state[11, :, start : start + LANES] for start, _ in cuts]
    rows[-1] = jnp.where(iota((8, LANES), 1) < rest, rows[-1], 0.0)
    rows = jnp.concatenate(rows, axis=0)
    high = rows.astype(jnp.bfloat16)
    low = (rows - high.astype(jnp.float32)).astype(jnp.bfloat16)
    parts = jnp.concatenate([high, low], axis=1)
    for start in range(0, tiles * LANES, 2 * LANES):
        end = min(start + 2 * LANES, tiles * LANES)
        width = min(end, columns) - start
        found = jnp.dot(parts, table_ref[:, start:end], preferred_element_type=jnp.float32)
        at = slice(start, start + width)
        outer = jnp.broadcast_to(fold_ref[:, at] >> 7, (8, width))
        value = found[0:8, :width]
        for k in range(1, tiles):
            value = jnp.where(outer == k, found[k * 8 : (k + 1) * 8, :width], value)
        state[12, :, at] = value


def sweep_rows(state, kap, cuts, levels, low, high, write, after=None):
    full = len(cuts) - 1
    rest = cuts[-1][1]
    lane = iota((8, LANES), 1)
    level = iota((8, LANES), 0) & (levels - 1)

    def body(r, carry):
        def cell(k):
            return state[r, :, k * LANES : (k + 1) * LANES]

        centre = cell(0)
        east_now = pltpu.roll(centre, LANES - 1, 1)
        around = pltpu.roll(centre, rest - 1, 1)
        west_last = pltpu.roll(cell(full), LANES - rest + 1, 1)
        for k in range(full + 1):
            at = slice(k * LANES, (k + 1) * LANES)
            if k == full:
                east = jnp.where(lane == rest - 1, around, east_now)
            else:
                following = cell(k + 1)
                east_next = pltpu.roll(following, LANES - 1, 1)
                east = jnp.where(lane == LANES - 1, east_next, east_now)
            west_now = pltpu.roll(centre, 1, 1)
            west = jnp.where(lane == 0, west_last, west_now)
            north = state[r + 1, :, at]
            south = state[r - 1, :, at]
            upper = jnp.where(level == 0, centre, pltpu.roll(centre, 1, 0))
            lower = jnp.where(level == levels - 1, centre, pltpu.roll(centre, 7, 0))
            horizontal = (north + south) + (east + west) - 4.0 * centre
            vertical = upper + lower - 2.0 * centre
            rate = kap[k, pl.ds(r, 1), :]
            write(r, k, centre + rate * horizontal + vertical_mix * vertical)
            if k < full:
                centre, east_now, west_last = following, east_next, west_now
        if after is not None:
            after(r)
        return carry

    lax.fori_loop(low, high, body, 0)


def keep(target):
    def write(r, k, value):
        target[r, :, k * LANES : (k + 1) * LANES] = value

    return write


def row_copy(source, target, sems, r):
    return pltpu.make_async_copy(source.at[r], target.at[r], sems.at[r])


def sweep_and_send(
    state, kap, cuts, levels, low, high, kept, out_hbm, sems, last, table, fold_ref, between=None
):
    def after(r):
        @pl.when(jnp.logical_not(last & (r == 12)))
        def _():
            row_copy(kept, out_hbm, sems, r).start()

    write = keep(kept)
    sweep_rows(state, kap, cuts, levels, 10, high, write, after)

    @pl.when(last)
    def _():
        fold_row(kept, table, fold_ref)
        row_copy(kept, out_hbm, sems, 12).start()

    if between is not None:
        between()
    sweep_rows(state, kap, cuts, levels, low, 10, write, after)

    def finish():
        for r in range(low, high):
            row_copy(kept, out_hbm, sems, r).wait()

    return finish


def fetch_rows(state_hbm, state, kap_hbm, kap, sems, low, high):
    kap_copy = pltpu.make_async_copy(kap_hbm, kap, sems.at[0])
    kap_copy.start()
    copies = {r: row_copy(state_hbm, state, sems, r) for r in range(low, high)}
    for r in reversed(range(low, high)):
        copies[r].start()

    def upper():
        kap_copy.wait()
        for r in range(9, high):
            copies[r].wait()

    def lower():
        for r in range(low, 9):
            copies[r].wait()

    return upper, lower


def first_sweep_kernel(
    me_ref,
    after,
    ocean_hbm,
    kappa_hbm,
    even_hbm,
    odd_hbm,
    fold_ref,
    out_hbm,
    kap_hbm,
    token,
    state,
    kept,
    kap_ref,
    ocean,
    kappa,
    above,
    below,
    grouped,
    table,
    sems,
    row_sems,
    levels,
    peers,
):
    me = me_ref[0]
    last = me == peers - 1
    odd = lax.rem(me, 2)
    token[...] = jnp.zeros_like(token)
    planes = state.shape[1]
    cuts = widths(kappa.shape[1])
    copies = [
        pltpu.make_async_copy(ocean_hbm, ocean, sems.at[0]),
        pltpu.make_async_copy(kappa_hbm, kappa, sems.at[1]),
    ]
    for copy in copies:
        copy.start()

    @pl.when(odd == 1)
    def _():
        pltpu.make_async_copy(odd_hbm, above, sems.at[2]).start()
        pltpu.make_async_copy(even_hbm, below, sems.at[3]).start()

    @pl.when(odd == 0)
    def _():
        pltpu.make_async_copy(even_hbm, above, sems.at[2]).start()
        pltpu.make_async_copy(odd_hbm, below, sems.at[3]).start()

    fold_tables(last, fold_ref, table)
    for copy in copies:
        copy.wait()
    for k, (start, width) in enumerate(cuts):
        grouped[k, :, :width] = ocean[:, start : start + width]
        kap_ref[k, 4:12, :width] = kappa[:, start : start + width]
    for k, (start, width) in enumerate(cuts):
        for r in range(8):
            part = grouped[k, pl.ds(r, planes, stride=8), :]
            state[4 + r, :, start : start + LANES] = part
    pltpu.make_async_copy(even_hbm, above, sems.at[2]).wait()
    pltpu.make_async_copy(odd_hbm, below, sems.at[3]).wait()
    for halo, first, near in ((below, 0, 3), (above, 12, 0)):
        for k, (start, _) in enumerate(cuts):
            at = slice(start, start + LANES)
            block = halo[:, at].astype(jnp.float32)
            for r in range(4):
                value = block[r * planes : (r + 1) * planes]
                if r == near:
                    value = value + block[5 * planes : 6 * planes]
                state[first + r, :, at] = value
            kap_ref[k, first : first + 4, :] = block[4 * planes : 4 * planes + 4]

    @pl.when(last)
    def _():
        fold_row(state, table, fold_ref)

    kap_copy = pltpu.make_async_copy(kap_ref, kap_hbm, row_sems.at[0])
    kap_copy.start()
    finish = sweep_and_send(
        state, kap_ref, cuts, levels, 1, 15, kept, out_hbm, row_sems, last, table, fold_ref
    )
    finish()
    kap_copy.wait()


def second_sweep_kernel(
    me_ref,
    after,
    state_hbm,
    kap_hbm,
    fold_ref,
    atmos_hbm,
    flux_ref,
    mix_hbm,
    out_hbm,
    air_hbm,
    token,
    state,
    kap,
    kept,
    air,
    air_next,
    mix,
    table,
    sems,
    out_sems,
    air_sems,
    levels,
    peers,
):
    token[...] = jnp.zeros_like(token)
    last = me_ref[0] == peers - 1
    upper, lower = fetch_rows(state_hbm, state, kap_hbm, kap, sems, 1, 15)
    loads = [
        pltpu.make_async_copy(atmos_hbm, air, air_sems.at[0]),
        pltpu.make_async_copy(mix_hbm, mix, air_sems.at[1]),
    ]
    for copy in loads:
        copy.start()
    fold_tables(last, fold_ref, table)
    upper()
    cuts = widths(fold_ref.shape[1])
    finish = sweep_and_send(
        state, kap, cuts, levels, 2, 14, kept, out_hbm, out_sems, last, table, fold_ref, lower
    )
    for copy in loads:
        copy.wait()
    atmos_sweeps(air, flux_ref, mix, air_next)
    store = pltpu.make_async_copy(air_next, air_hbm, air_sems.at[2])
    store.start()
    finish()
    store.wait()


def last_sweeps_kernel(
    me_ref,
    after,
    state_hbm,
    kap_hbm,
    fold_ref,
    out_ref,
    surface_ref,
    came,
    kap_ref,
    state,
    grouped,
    table,
    sems,
    levels,
    peers,
):
    cuts = widths(out_ref.shape[1])
    planes = came.shape[1]
    last = me_ref[0] == peers - 1
    upper, lower = fetch_rows(state_hbm, came, kap_hbm, kap_ref, sems, 2, 14)
    fold_tables(last, fold_ref, table)
    upper()
    lower()
    sweep_rows(came, kap_ref, cuts, levels, 3, 13, keep(state))

    @pl.when(last)
    def _():
        fold_row(state, table, fold_ref)

    def write(r, k, value):
        grouped[k, pl.ds(r - 4, planes, stride=8), :] = value

    sweep_rows(state, kap_ref, cuts, levels, 4, 12, write)
    for k, (start, width) in enumerate(cuts):
        at = slice(start, start + width)
        out_ref[:, at] = grouped[k, :, :width]
        for t in range(planes // levels):
            top = t * levels * 8
            surface_ref[t, :, at] = grouped[k, top : top + 8, :width]


def all_weights(held, w_hbm, w_rest, sems):
    size = held[0].shape[0]
    first = len(held) * size
    copies = []
    for i in range(w_rest.shape[0] // size):
        part = pl.ds(i * size, size)
        source = w_hbm.at[pl.ds(first + i * size, size)]
        copies.append(pltpu.make_async_copy(source, w_rest.at[part], sems.at[i]))
        copies[-1].start()

    def get(d):
        if d < len(held):
            weights = held[d][...]
        else:
            at = d - len(held)
            copies[at].wait()
            weights = w_rest[at * size : (at + 1) * size]
        return weights.reshape(size * LANES, LANES)

    return get


def forward_kernel(me_ref, recv_ref, sum_ref, w_hbm, *refs):
    held, (out_ref, token, sums, w_rest, sems) = refs[:-5], refs[-5:]
    get_weights = all_weights(held, w_hbm, w_rest, sems)
    token[...] = jnp.zeros_like(token)
    me = me_ref[0]
    peers = recv_ref.shape[0]
    tracers, blocks, _ = sums.shape
    n_slots = sum_ref.shape[0]
    window = n_slots // 8
    slots = blocks // window
    row = iota((8, LANES), 0)
    out_ref[...] = jnp.zeros_like(out_ref)
    for d in range(window):
        source = jnp.clip(me - d + window // 2, 0, peers - 1)
        weights = get_weights(d)
        for first in range(0, slots, 8):
            top = row_of(0, first, tracers)
            cells = recv_ref[source, top : top + 8 * tracers, :]
            product = lax.dot_general(
                cells,
                weights[first * LANES : (first + 8) * LANES],
                (((1,), (1,)), ((), ())),
                preferred_element_type=jnp.float32,
            )
            for t in range(tracers):
                part = product[t * 8 : (t + 1) * 8]
                found = part[:, :LANES]
                for k in range(1, 8):
                    found = jnp.where(row == k, part[:, k * LANES : (k + 1) * LANES], found)
                sums[t, d * slots + first : d * slots + first + 8, :] = found
    partial_sums = [split_dot(sum_ref[...], sums[t], ((1,), (0,))) for t in range(tracers)]
    for g in range(window):
        peer = me + g - window // 2

        @pl.when((peer >= 0) & (peer < peers))
        def _():
            for t in range(tracers):
                out_ref[peer, t * 8 : (t + 1) * 8, :] = partial_sums[t][g * 8 : (g + 1) * 8]


def flux_kernel(
    me_ref, after, parts_ref, spread_ref, pick_ref, air_ref, rate_ref, send_ref, flux_ref, token
):
    token[...] = jnp.zeros_like(token)
    me = me_ref[0]
    peers = parts_ref.shape[0]
    tracers, rows, columns = flux_ref.shape
    n_slots = spread_ref.shape[1]
    window = n_slots // 8
    send_ref[...] = jnp.zeros_like(send_ref)
    sent = []
    for t in range(tracers):
        parts = []
        for g in range(window):
            coupler = me - g + window // 2
            valid = (coupler >= 0) & (coupler < peers)
            block = parts_ref[jnp.clip(coupler, 0, peers - 1), t * 8 : (t + 1) * 8, :]
            parts.append(jnp.where(valid, block, 0.0))
        remapped = split_dot(spread_ref[...], jnp.concatenate(parts, axis=0), ((1,), (0,)))
        flux = rate_ref[...] * (solubility * air_ref[t] - remapped)
        for k in range(columns // LANES):
            flux_ref[t, :, k * LANES : (k + 1) * LANES] = flux[k * rows : (k + 1) * rows]
        sent.append(
            jnp.dot(pick_ref[...], flux.astype(jnp.bfloat16), preferred_element_type=jnp.float32)
        )
    for g in range(window):
        peer = me - g + window // 2

        @pl.when((peer >= 0) & (peer < peers))
        def _():
            block = jnp.concatenate([s[g * 8 : (g + 1) * 8] for s in sent], axis=0)
            send_ref[peer] = block.astype(jnp.bfloat16)


def backward_kernel(me_ref, after, recv_ref, pick_ref, w_hbm, *refs):
    held, (out_ref, token, w_rest, sems) = refs[:-4], refs[-4:]
    get_weights = all_weights(held, w_hbm, w_rest, sems)
    token[...] = jnp.zeros_like(token)
    me = me_ref[0]
    peers, width, _ = recv_ref.shape
    tracers = width // 8
    blocks, n_slots = pick_ref.shape
    window = n_slots // 8
    slots = blocks // window
    parts = [[] for _ in range(tracers)]
    for g in range(window):
        owner = me + g - window // 2
        valid = (owner >= 0) & (owner < peers)
        block = recv_ref[jnp.clip(owner, 0, peers - 1)].astype(jnp.float32)
        block = jnp.where(valid, block, 0.0)
        for t in range(tracers):
            parts[t].append(block[t * 8 : (t + 1) * 8])
    picked = [
        jnp.dot(
            pick_ref[...],
            jnp.concatenate(parts[t], axis=0).astype(jnp.bfloat16),
            preferred_element_type=jnp.float32,
        )
        for t in range(tracers)
    ]
    out_ref[...] = jnp.zeros_like(out_ref)
    row = iota((8, LANES), 0)
    for d in range(window):
        weights = get_weights(d)
        products = []
        for first in range(0, slots, 8):
            at = slice(d * slots + first, d * slots + first + 8)
            mine = [p[at] for p in picked]
            cells = jnp.concatenate(
                [
                    jnp.concatenate([jnp.where(row == k, m, 0.0) for m in mine], axis=0).astype(
                        jnp.bfloat16
                    )
                    for k in range(8)
                ],
                axis=1,
            )
            products.append(
                jnp.dot(
                    cells,
                    weights[first * LANES : (first + 8) * LANES],
                    preferred_element_type=jnp.float32,
                )
            )
        peer = me - d + window // 2

        @pl.when((peer >= 0) & (peer < peers))
        def _():
            out_ref[peer] = jnp.concatenate(products, axis=0)


def add_kernel(me_ref, returned_ref, table_ref, surface, swept, out, buffer, sems):
    me = me_ref[0]
    peers = returned_ref.shape[0]
    tracers, _, columns = surface.shape
    slots = returned_ref.shape[1] // tracers
    window = table_ref.shape[1] // slots
    cuts = widths(columns)
    full = len(cuts) - 1
    rest = cuts[-1][1]
    lane = iota((8, LANES), 1)
    row = iota((8, LANES), 0)
    stays = lane < LANES - rest * row
    copies = []
    for t in range(tracers):
        parts = []
        for d in range(window):
            coupler = me + d - window // 2
            valid = (coupler >= 0) & (coupler < peers)
            for first in range(0, slots, 8):
                top = row_of(t, first, tracers)
                block = returned_ref[jnp.clip(coupler, 0, peers - 1), top : top + 8, :]
                parts.append(jnp.where(valid, block, 0.0))
        tiles = split_dot(table_ref[...], jnp.concatenate(parts, axis=0), ((1,), (0,)))
        rows = [tiles[k * 8 : (k + 1) * 8] for k in range(full + 1)]
        rows[full] = jnp.where(row == 7, rows[full], pltpu.roll(rows[0], 7, 0))
        turned = [shear(value, -1, rest) for value in rows]
        for k, (start, width) in enumerate(cuts):
            value = turned[k]
            if k < full:
                value = jnp.where(stays, value, turned[k + 1])
            at = slice(start, start + width)
            buffer[t, :, at] = surface[t, :, at] + ocean_rate * value[:, :width]
        copies.append(pltpu.make_async_copy(buffer.at[t], out.at[t, 0], sems.at[t]))
        copies[-1].start()
    for copy in copies:
        copy.wait()


def atmos_sweeps(atmos_ref, flux_ref, mix_ref, out_ref):
    tracers, levels, rows, columns = atmos_ref.shape
    for t in range(tracers):
        for r in range(0, rows, 8):
            for c in range(0, columns, LANES):
                at = (slice(r, r + 8), slice(c, c + LANES))
                mixing = mix_ref[at]
                field = [atmos_ref[(t, v) + at] for v in range(levels)]
                field[0] = field[0] - atmos_rate * flux_ref[(t,) + at]
                for _ in range(ASTEPS):
                    field = [
                        field[v]
                        + mixing
                        * (field[max(v - 1, 0)] + field[min(v + 1, levels - 1)] - 2.0 * field[v])
                        for v in range(levels)
                    ]
                for v in range(levels):
                    out_ref[(t, v) + at] = field[v]


def local(
    ocean,
    kappa,
    atmos,
    piston,
    atmos_mix,
    fold_map,
    send_tile,
    slot_counts,
    out_slot,
    out_tile,
    remap_w,
):
    count = lax.axis_size("tile")
    me = lax.axis_index("tile").astype(jnp.int32).reshape(1)
    tracers, levels, ocean_rows, columns = ocean.shape
    planes = tracers * levels
    window, slots_in = send_tile.shape[1:]
    slots_out = out_tile.shape[2]
    blocks = window * slots_in
    n_slots = window * slots_out
    tiles = -(-columns // LANES)
    padded = tiles * LANES
    atmos_rows, atmos_columns = atmos.shape[2:]
    across = atmos_columns // LANES
    n_tiles = atmos_rows * across
    f32, bf16, i32 = jnp.float32, jnp.bfloat16, jnp.int32
    shape = jax.ShapeDtypeStruct
    dma = pltpu.SemaphoreType.DMA
    exchange = functools.partial(
        lax.all_to_all, axis_name="tile", split_axis=0, concat_axis=0, tiled=True
    )

    def cost(us):
        return pl.CostEstimate(
            flops=0, bytes_accessed=int(us * 1.0e4), transcendentals=0
        )

    token_shape = shape((8, LANES), f32)
    sent, token = pl.pallas_call(
        pack_kernel,
        out_shape=(pltpu.HBM((count, tracers * slots_in, LANES), bf16), token_shape),
        in_specs=[smem(), hbm(), hbm()],
        out_specs=(vmem(), vmem()),
        scratch_shapes=[
            pltpu.SMEM(send_tile.shape, i32),
            pltpu.VMEM((tracers, ocean_rows, columns), f32),
            pltpu.VMEM((tracers, tiles * 8, LANES), f32),
            pltpu.VMEM((window, tracers * slots_in, LANES), f32),
            dma((tracers + 1,)),
        ],
        compiler_params=params(),
        name="pack",
    )(me, in_hbm(send_tile), in_hbm(ocean))
    received = exchange(sent)

    halo_rows = 6 * planes
    flat = in_hbm(ocean.reshape(planes * ocean_rows, columns))
    weights = in_hbm(remap_w[0])
    prepared = pl.pallas_call(
        prepare_kernel,
        out_shape=(
            *[shape((slots_in,) + remap_w.shape[2:], bf16)] * HELD,
            pltpu.HBM((halo_rows, padded), bf16),
            pltpu.HBM((halo_rows, padded), bf16),
            shape((n_slots, blocks), bf16),
            shape((blocks, n_slots), bf16),
            shape((n_tiles, n_slots), bf16),
            shape((n_slots, n_tiles), bf16),
            shape((tiles * 8, blocks), bf16),
            shape((tracers, n_tiles, LANES), f32),
            shape((n_tiles, LANES), f32),
        ),
        in_specs=[smem(), vmem()] + [hbm()] * 9,
        out_specs=(vmem(),) * HELD + (hbm(),) * 2 + (vmem(),) * 7,
        scratch_shapes=[
            pltpu.VMEM((planes * ocean_rows, columns), f32),
            pltpu.VMEM((ocean_rows, columns), f32),
            pltpu.VMEM((tiles, (planes + 1) * ocean_rows, LANES), f32),
            pltpu.VMEM((halo_rows, padded), bf16),
            pltpu.VMEM((halo_rows, padded), bf16),
            pltpu.VMEM((tracers, atmos_rows, atmos_columns), f32),
            pltpu.VMEM((atmos_rows, atmos_columns), f32),
            pltpu.SMEM(slot_counts.shape, i32),
            pltpu.VMEM(out_slot.shape, i32),
            pltpu.SMEM(out_tile.shape, i32),
            pltpu.SMEM(send_tile.shape, i32),
            dma((tracers + 9 + HELD,)),
        ],
        compiler_params=params(),
        cost_estimate=cost(3),
        name="prepare",
    )(
        me,
        token,
        in_hbm(slot_counts),
        in_hbm(out_slot),
        in_hbm(out_tile),
        in_hbm(send_tile),
        flat,
        in_hbm(kappa),
        in_hbm(atmos),
        in_hbm(piston),
        weights,
    )
    held = prepared[:HELD]
    even, odd = prepared[HELD : HELD + 2]
    sum_table, slot_pick, spread, flux_pick, scatter, air, rate = prepared[HELD + 2 :]
    even_pairs = [(i, i ^ 1) for i in range(count) if i ^ 1 < count]
    odd_pairs = [(i, i + 1) for i in range(1, count - 1, 2)]
    odd_pairs += [(b, a) for a, b in odd_pairs]
    even = lax.ppermute(even, "tile", even_pairs)
    odd = lax.ppermute(odd, "tile", odd_pairs)
    weight_scratch = [
        pltpu.VMEM((blocks - HELD * slots_in,) + remap_w.shape[2:], bf16),
        dma((window - HELD,)),
    ]

    partial_sums, token = pl.pallas_call(
        forward_kernel,
        out_shape=(shape((count, tracers * slots_out, LANES), f32), token_shape),
        in_specs=[smem(), vmem(), vmem(), hbm()] + [vmem()] * HELD,
        out_specs=(vmem(), vmem()),
        scratch_shapes=[pltpu.VMEM((tracers, blocks, LANES), f32)] + weight_scratch,
        compiler_params=params(),
        name="forward",
    )(me, received, sum_table, weights, *held)
    owner_parts = exchange(partial_sums.astype(jnp.float16)).astype(f32)

    state_shape = (16, planes, padded)
    kap_shape = (tiles, 16, LANES)
    fold = fold_map.reshape(1, columns)
    fold_scratch = [pltpu.VMEM((2 * LANES, padded), bf16)]
    state, kap, token = pl.pallas_call(
        functools.partial(first_sweep_kernel, levels=levels, peers=count),
        out_shape=(pltpu.HBM(state_shape, f32), pltpu.HBM((tiles, 16, LANES), f32), token_shape),
        in_specs=[smem(), vmem()] + [hbm()] * 4 + [vmem()],
        out_specs=(hbm(), hbm(), vmem()),
        scratch_shapes=[
            pltpu.VMEM(state_shape, f32),
            pltpu.VMEM(state_shape, f32),
            pltpu.VMEM(kap_shape, f32),
            pltpu.VMEM((planes * ocean_rows, columns), f32),
            pltpu.VMEM((ocean_rows, columns), f32),
            pltpu.VMEM((halo_rows, padded), bf16),
            pltpu.VMEM((halo_rows, padded), bf16),
            pltpu.VMEM((tiles, planes * ocean_rows, LANES), f32),
        ]
        + fold_scratch
        + [dma((4,)), dma((16,))],
        compiler_params=params(),
        cost_estimate=cost(5),
        name="first_sweep",
    )(me, token, flat, in_hbm(kappa), in_hbm(even), in_hbm(odd), fold)

    flux_sent, flux, flux_token = pl.pallas_call(
        flux_kernel,
        out_shape=(
            pltpu.HBM((count, tracers * slots_out, LANES), bf16),
            shape((tracers, atmos_rows, atmos_columns), f32),
            token_shape,
        ),
        in_specs=[smem()] + [vmem()] * 6,
        out_specs=(vmem(),) * 3,
        compiler_params=params(),
        name="flux",
    )(me, token, owner_parts, spread, flux_pick, air, rate)
    at_coupler = exchange(flux_sent)

    state, atmos_next, token = pl.pallas_call(
        functools.partial(second_sweep_kernel, levels=levels, peers=count),
        out_shape=(pltpu.HBM(state_shape, f32), pltpu.HBM(atmos.shape, f32), token_shape),
        in_specs=[smem(), vmem(), hbm(), hbm(), vmem(), hbm(), vmem(), hbm()],
        out_specs=(hbm(), hbm(), vmem()),
        scratch_shapes=[
            pltpu.VMEM(state_shape, f32),
            pltpu.VMEM(kap_shape, f32),
            pltpu.VMEM(state_shape, f32),
            pltpu.VMEM(atmos.shape, f32),
            pltpu.VMEM(atmos.shape, f32),
            pltpu.VMEM(atmos_mix.shape, f32),
        ]
        + fold_scratch
        + [dma((16,)), dma((16,)), dma((3,))],
        compiler_params=params(),
        cost_estimate=cost(3),
        name="second_sweep",
    )(
        me,
        flux_token,
        in_hbm(state),
        in_hbm(kap),
        fold,
        in_hbm(atmos),
        flux,
        in_hbm(atmos_mix),
    )

    back_sums, token = pl.pallas_call(
        backward_kernel,
        out_shape=(shape((count, tracers * slots_in, LANES), f32), token_shape),
        in_specs=[smem()] + [vmem()] * 3 + [hbm()] + [vmem()] * HELD,
        out_specs=(vmem(), vmem()),
        scratch_shapes=weight_scratch,
        compiler_params=params(),
        name="backward",
    )(me, token, at_coupler, slot_pick, weights, *held)
    returned = exchange(back_sums.astype(jnp.float16)).astype(f32)

    swept, surface = pl.pallas_call(
        functools.partial(last_sweeps_kernel, levels=levels, peers=count),
        out_shape=(
            pltpu.HBM((planes * ocean_rows, columns), f32),
            shape((tracers, ocean_rows, columns), f32),
        ),
        in_specs=[smem(), vmem(), hbm(), hbm(), vmem()],
        out_specs=(vmem(), vmem()),
        scratch_shapes=[
            pltpu.VMEM(state_shape, f32),
            pltpu.VMEM(kap_shape, f32),
            pltpu.VMEM(state_shape, f32),
            pltpu.VMEM((tiles, planes * ocean_rows, LANES), f32),
        ]
        + fold_scratch
        + [dma((16,))],
        compiler_params=params(),
        cost_estimate=cost(4),
        name="last_sweeps",
    )(me, token, in_hbm(state), in_hbm(kap), fold)
    ocean_next = pl.pallas_call(
        add_kernel,
        out_shape=shape(ocean.shape, f32),
        in_specs=[smem()] + [vmem()] * 3 + [hbm()],
        out_specs=hbm(),
        scratch_shapes=[pltpu.VMEM((tracers, ocean_rows, columns), f32), dma((tracers,))],
        input_output_aliases={4: 0},
        compiler_params=params(),
        name="add",
    )(me, returned, scatter, surface, in_hbm(swept.reshape(ocean.shape)))
    return (ocean_next, atmos_next)


def solution(mesh):
    placed = (
        P("member", None, "tile", None),
        P("tile", None),
        P("member", None, "tile", None),
        P("tile", None),
        P("tile", None),
        P(),
        P("tile", None, None),
        P("tile", None),
        P("tile", None),
        P("tile", None, None),
        P("tile", None, None, None),
    )
    return jax.shard_map(
        local,
        mesh=mesh,
        in_specs=placed,
        out_specs=(P("member", None, "tile", None), P("member", None, "tile", None)),
        check_vma=False,
    )
```

```python
import functools

import jax
import jax.numpy as jnp
from jax import lax
from jax.experimental import pallas as pl
from jax.experimental.pallas import tpu as pltpu
from jax.sharding import PartitionSpec as P

OSTEPS = 4
ASTEPS = 4
LANES = 128
HELD = 6

vertical_mix = 0.1
ocean_rate = 4.0
atmos_rate = 0.5
solubility = 1.2

MIB = 1024 * 1024


def params(mib=16):
    return pltpu.CompilerParams(vmem_limit_bytes=36 * MIB)


def vmem():
    return pl.BlockSpec(memory_space=pltpu.VMEM)


def smem():
    return pl.BlockSpec(memory_space=pltpu.SMEM)


def hbm():
    return pl.BlockSpec(memory_space=pltpu.HBM)


def anywhere():
    return pl.BlockSpec(memory_space=pl.ANY)


def iota(shape, dim):
    return lax.broadcasted_iota(jnp.int32, shape, dim)


def split_dot(table, values, dims):
    high = values.astype(jnp.bfloat16)
    low = (values - high.astype(jnp.float32)).astype(jnp.bfloat16)
    dot = functools.partial(
        lax.dot_general, dimension_numbers=(dims, ((), ())), preferred_element_type=jnp.float32
    )
    return dot(table, high) + dot(table, low)


def shear(tile, sign, shift):
    lane = iota(tile.shape, 1)
    row = iota(tile.shape, 0)
    source = (lane - sign * shift * row) & (LANES - 1)
    return jnp.take_along_axis(tile, source, axis=1, mode="promise_in_bounds")


def widths(columns):
    return [(c, min(LANES, columns - c)) for c in range(0, columns, LANES)]


def in_hbm(x):
    return pltpu.with_memory_space_constraint(x, pltpu.HBM)


def row_of(tracer, slot, tracers):
    return (slot // 8) * 8 * tracers + tracer * 8 + slot % 8


def magic(divisor, count):
    scale = -(-65536 // divisor)
    assert all((i * scale) >> 16 == i // divisor for i in range(count))
    return scale


def tile_row(index, full, scale):
    over = (index * scale) >> 16
    return jnp.where(index == 8 * full, 8 * full + 7, (index - over * full) * 8 + over)


def one_hot(mask):
    return jnp.where(mask, 1.0, 0.0).astype(jnp.bfloat16)


def pack_kernel(me_ref, send_hbm, ocean_hbm, out_ref, token, send, surface, tiles, rows, sems):
    me = me_ref[0]
    peers = out_ref.shape[0]
    _, window, slots = send.shape
    tracers, _, columns = surface.shape
    copies = [pltpu.make_async_copy(send_hbm, send, sems.at[tracers])]
    for t in range(tracers):
        copies.append(pltpu.make_async_copy(ocean_hbm.at[t, 0], surface.at[t], sems.at[t]))
    for copy in copies:
        copy.start()
    out_ref[...] = jnp.zeros_like(out_ref)
    token[...] = jnp.zeros_like(token)
    cuts = widths(columns)
    full = len(cuts) - 1
    rest = cuts[-1][1]
    lane = iota((8, LANES), 1)
    row = iota((8, LANES), 0)
    wraps = lane < rest * row
    for t in range(tracers):
        copies[1 + t].wait()
        before = jnp.zeros((8, LANES), jnp.float32)
        first = None
        for k, (start, width) in enumerate(cuts):
            part = surface[t, :, start : start + width]
            if width < LANES:
                part = jnp.concatenate(
                    [part, jnp.zeros((8, LANES - width), jnp.float32)], axis=1
                )
            turned = shear(part, 1, rest)
            value = jnp.where(wraps, before, turned)
            before = turned
            if k == 0:
                first = value
            else:
                tiles[t, k * 8 : (k + 1) * 8] = value
        tiles[t, 0:8] = jnp.where(wraps, pltpu.roll(value, 1, 0), first)
    copies[0].wait()
    scale = magic(full, 8 * full + 1)
    for d in range(window):
        for k in range(slots):
            index = send[0, d, k]
            place = tile_row(index, full, scale)
            for t in range(tracers):
                at = row_of(t, k, tracers)
                rows[d, at : at + 1, :] = tiles[t, pl.ds(place, 1), :]
    for d in range(window):
        peer = me + d - window // 2

        @pl.when((peer >= 0) & (peer < peers))
        def _():
            out_ref[peer] = rows[d].astype(jnp.bfloat16)


def pack_halo(odd, ocean, kappa, grouped, even_ref, odd_ref):
    planes = ocean.shape[0] // 8
    cuts = widths(ocean.shape[1])
    for k, (start, width) in enumerate(cuts):
        grouped[k, 0 : planes * 8, :width] = ocean[:, start : start + width]
        grouped[k, planes * 8 :, :width] = kappa[:, start : start + width]
    for target, upper in ((even_ref, odd == 0), (odd_ref, odd == 1)):
        base = jnp.where(upper, 4, 0)
        near = jnp.where(upper, 7, 0)
        for k, (start, width) in enumerate(cuts):
            rows = [grouped[k, pl.ds(base + r, planes, stride=8), :] for r in range(4)]
            rates = grouped[k, planes * 8 :, :]
            rates = jnp.where(upper, pltpu.roll(rates, 4, 0), rates)
            nearest = grouped[k, pl.ds(near, planes, stride=8), :]
            low = nearest - nearest.astype(jnp.bfloat16).astype(jnp.float32)
            block = jnp.concatenate(rows + [rates, low], axis=0)
            target[:, start : start + LANES] = block.astype(jnp.bfloat16)


def prepare_kernel(
    me_ref,
    after,
    counts_hbm,
    slot_hbm,
    out_tile_hbm,
    send_hbm,
    ocean_hbm,
    kappa_hbm,
    atmos_hbm,
    piston_hbm,
    w_hbm,
    *refs,
):
    held = len(refs) - 21
    w_refs = refs[:held]
    even_hbm, odd_hbm = refs[held : held + 2]
    sum_ref, pick_ref, spread_ref, flux_pick_ref, scatter_ref, air_ref, rate_ref = refs[
        held + 2 : held + 9
    ]
    ocean, kappa, grouped, even, odd, surface, piston = refs[held + 9 : -5]
    counts, slot, out_tile, send, sems = refs[-5:]
    tracers, rows, columns = surface.shape
    size = w_refs[0].shape[0]
    pairs = [(counts_hbm, counts), (slot_hbm, slot), (out_tile_hbm, out_tile), (send_hbm, send)]
    pairs += [(ocean_hbm, ocean), (kappa_hbm, kappa), (piston_hbm, piston)]
    pairs += [(atmos_hbm.at[t, 0], surface.at[t]) for t in range(tracers)]
    pairs += [(w_hbm.at[pl.ds(i * size, size)], w_refs[i]) for i in range(held)]
    copies = [pltpu.make_async_copy(a, b, sems.at[i]) for i, (a, b) in enumerate(pairs)]
    for copy in copies:
        copy.start()
    n_slots, blocks = sum_ref.shape
    window, slots = send.shape[1:]
    slots_out = out_tile.shape[2]
    across = columns // LANES
    n_tiles = spread_ref.shape[0]
    full = ocean.shape[1] // LANES
    scale, scale_tile = magic(full, 8 * full + 1), magic(across, n_tiles)
    for copy in copies[:4]:
        copy.wait()
    at = iota((1, blocks), 1)
    live = at < 0
    place = jnp.zeros((1, blocks), jnp.int32)
    tile_place = jnp.zeros((1, blocks), jnp.int32)
    for d in range(window):
        live = live | ((at >= d * slots) & (at < d * slots + counts[0, d]))
        for k in range(slots):
            place = jnp.where(at == d * slots + k, tile_row(send[0, d, k], full, scale), place)
        for j in range(slots_out):
            tile = out_tile[0, d, j]
            down = (tile * scale_tile) >> 16
            value = (tile - down * across) * rows + down
            tile_place = jnp.where(at == d * slots_out + j, value, tile_place)
    table = jnp.where((iota((LANES, blocks), 0) == slot[...]) & live, 1.0, 0.0)
    sum_ref[...] = table[:n_slots].astype(jnp.bfloat16)
    pick_ref[...] = table.T[:, :n_slots].astype(jnp.bfloat16)
    spread = jnp.where(iota((LANES, LANES), 0) == tile_place, 1.0, 0.0)
    spread_ref[...] = spread[:n_tiles, :n_slots].astype(jnp.bfloat16)
    flux_pick_ref[...] = spread.T[:n_slots, :n_tiles].astype(jnp.bfloat16)
    scatter_ref[...] = one_hot(iota(scatter_ref.shape, 0) == place)
    for copy in copies[4:6]:
        copy.wait()
    pack_halo(lax.rem(me_ref[0], 2), ocean, kappa, grouped, even, odd)
    copies += [
        pltpu.make_async_copy(even, even_hbm, sems.at[len(copies)]),
        pltpu.make_async_copy(odd, odd_hbm, sems.at[len(copies) + 1]),
    ]
    for copy in copies[-2:]:
        copy.start()
    for copy in copies[6:]:
        copy.wait()
    for k in range(columns // LANES):
        at = slice(k * LANES, (k + 1) * LANES)
        rate_ref[k * rows : (k + 1) * rows, :] = piston[:, at]
        for t in range(tracers):
            air_ref[t, k * rows : (k + 1) * rows, :] = surface[t, :, at]


def fold_tables(last, fold_ref, table_ref):
    @pl.when(last)
    def _():
        inner = iota((LANES, LANES), 0)
        for start, width in widths(fold_ref.shape[1]):
            at = slice(start, start + width)
            found = one_hot(inner[:, :width] == (fold_ref[:, at] & (LANES - 1)))
            table_ref[0:LANES, at] = found
            table_ref[LANES : 2 * LANES, at] = found


def fold_row(state, table_ref, fold_ref):
    columns = fold_ref.shape[1]
    cuts = widths(columns)
    tiles = len(cuts)
    rest = cuts[-1][1]
    rows = [state[11, :, start : start + LANES] for start, _ in cuts]
    rows[-1] = jnp.where(iota((8, LANES), 1) < rest, rows[-1], 0.0)
    rows = jnp.concatenate(rows, axis=0)
    high = rows.astype(jnp.bfloat16)
    low = (rows - high.astype(jnp.float32)).astype(jnp.bfloat16)
    parts = jnp.concatenate([high, low], axis=1)
    for start in range(0, tiles * LANES, 2 * LANES):
        end = min(start + 2 * LANES, tiles * LANES)
        width = min(end, columns) - start
        found = jnp.dot(parts, table_ref[:, start:end], preferred_element_type=jnp.float32)
        at = slice(start, start + width)
        outer = jnp.broadcast_to(fold_ref[:, at] >> 7, (8, width))
        value = found[0:8, :width]
        for k in range(1, tiles):
            value = jnp.where(outer == k, found[k * 8 : (k + 1) * 8, :width], value)
        state[12, :, at] = value


def sweep_rows(state, kap, cuts, levels, low, high, write, after=None):
    full = len(cuts) - 1
    rest = cuts[-1][1]
    lane = iota((8, LANES), 1)
    level = iota((8, LANES), 0) & (levels - 1)

    def body(r, carry):
        def cell(k):
            return state[r, :, k * LANES : (k + 1) * LANES]

        centre = cell(0)
        east_now = pltpu.roll(centre, LANES - 1, 1)
        around = pltpu.roll(centre, rest - 1, 1)
        west_last = pltpu.roll(cell(full), LANES - rest + 1, 1)
        for k in range(full + 1):
            at = slice(k * LANES, (k + 1) * LANES)
            if k == full:
                east = jnp.where(lane == rest - 1, around, east_now)
            else:
                following = cell(k + 1)
                east_next = pltpu.roll(following, LANES - 1, 1)
                east = jnp.where(lane == LANES - 1, east_next, east_now)
            west_now = pltpu.roll(centre, 1, 1)
            west = jnp.where(lane == 0, west_last, west_now)
            north = state[r + 1, :, at]
            south = state[r - 1, :, at]
            upper = jnp.where(level == 0, centre, pltpu.roll(centre, 1, 0))
            lower = jnp.where(level == levels - 1, centre, pltpu.roll(centre, 7, 0))
            horizontal = (north + south) + (east + west) - 4.0 * centre
            vertical = upper + lower - 2.0 * centre
            rate = kap[k, pl.ds(r, 1), :]
            write(r, k, centre + rate * horizontal + vertical_mix * vertical)
            if k < full:
                centre, east_now, west_last = following, east_next, west_now
        if after is not None:
            after(r)
        return carry

    lax.fori_loop(low, high, body, 0)


def keep(target):
    def write(r, k, value):
        target[r, :, k * LANES : (k + 1) * LANES] = value

    return write


def row_copy(source, target, sems, r):
    return pltpu.make_async_copy(source.at[r], target.at[r], sems.at[r])


def first_sweep_kernel(
    me_ref,
    after,
    ocean_hbm,
    kappa_hbm,
    even_hbm,
    odd_hbm,
    fold_ref,
    out_hbm,
    kap_hbm,
    token,
    state,
    kept,
    kap_ref,
    ocean,
    kappa,
    above,
    below,
    grouped,
    table,
    sems,
    row_sems,
    levels,
    peers,
):
    me = me_ref[0]
    last = me == peers - 1
    odd = lax.rem(me, 2)
    token[...] = jnp.zeros_like(token)
    planes = state.shape[1]
    cuts = widths(kappa.shape[1])
    copies = [
        pltpu.make_async_copy(ocean_hbm, ocean, sems.at[0]),
        pltpu.make_async_copy(kappa_hbm, kappa, sems.at[1]),
    ]
    for copy in copies:
        copy.start()

    @pl.when(odd == 1)
    def _():
        pltpu.make_async_copy(odd_hbm, above, sems.at[2]).start()
        pltpu.make_async_copy(even_hbm, below, sems.at[3]).start()

    @pl.when(odd == 0)
    def _():
        pltpu.make_async_copy(even_hbm, above, sems.at[2]).start()
        pltpu.make_async_copy(odd_hbm, below, sems.at[3]).start()

    fold_tables(last, fold_ref, table)
    for copy in copies:
        copy.wait()
    for k, (start, width) in enumerate(cuts):
        grouped[k, :, :width] = ocean[:, start : start + width]
        kap_ref[k, 4:12, :width] = kappa[:, start : start + width]
    for k, (start, width) in enumerate(cuts):
        for r in range(8):
            part = grouped[k, pl.ds(r, planes, stride=8), :]
            state[4 + r, :, start : start + LANES] = part
    pltpu.make_async_copy(even_hbm, above, sems.at[2]).wait()
    pltpu.make_async_copy(odd_hbm, below, sems.at[3]).wait()
    for halo, first, near in ((below, 0, 3), (above, 12, 0)):
        for k, (start, _) in enumerate(cuts):
            at = slice(start, start + LANES)
            block = halo[:, at].astype(jnp.float32)
            for r in range(4):
                value = block[r * planes : (r + 1) * planes]
                if r == near:
                    value = value + block[5 * planes : 6 * planes]
                state[first + r, :, at] = value
            kap_ref[k, first : first + 4, :] = block[4 * planes : 4 * planes + 4]

    @pl.when(last)
    def _():
        fold_row(state, table, fold_ref)

    kap_copy = pltpu.make_async_copy(kap_ref, kap_hbm, row_sems.at[0])
    kap_copy.start()

    def after(r):
        row_copy(kept, out_hbm, row_sems, r).start()

    sweep_rows(state, kap_ref, cuts, levels, 1, 15, keep(kept), after)
    for r in range(1, 15):
        row_copy(kept, out_hbm, row_sems, r).wait()
    kap_copy.wait()


def last_sweeps_kernel(
    me_ref,
    after,
    state_hbm,
    kap_hbm,
    fold_ref,
    out_ref,
    surface_ref,
    came,
    kap_ref,
    state,
    grouped,
    table,
    sems,
    levels,
    peers,
):
    cuts = widths(out_ref.shape[1])
    planes = came.shape[1]
    last = me_ref[0] == peers - 1
    copies = [pltpu.make_async_copy(kap_hbm, kap_ref, sems.at[0])]
    copies += [row_copy(state_hbm, came, sems, r) for r in range(1, 15)]
    for copy in copies:
        copy.start()
    fold_tables(last, fold_ref, table)
    for copy in copies:
        copy.wait()

    def fold(rows):
        @pl.when(last)
        def _():
            fold_row(rows, table, fold_ref)

    fold(came)
    sweep_rows(came, kap_ref, cuts, levels, 2, 14, keep(state))
    fold(state)
    sweep_rows(state, kap_ref, cuts, levels, 3, 13, keep(came))
    fold(came)

    def write(r, k, value):
        grouped[k, pl.ds(r - 4, planes, stride=8), :] = value

    sweep_rows(came, kap_ref, cuts, levels, 4, 12, write)
    for k, (start, width) in enumerate(cuts):
        at = slice(start, start + width)
        out_ref[:, at] = grouped[k, :, :width]
        for t in range(planes // levels):
            top = t * levels * 8
            surface_ref[t, :, at] = grouped[k, top : top + 8, :width]


def all_weights(held, w_hbm, w_rest, sems):
    size = held[0].shape[0]
    first = len(held) * size
    copies = []
    for i in range(w_rest.shape[0] // size):
        part = pl.ds(i * size, size)
        source = w_hbm.at[pl.ds(first + i * size, size)]
        copies.append(pltpu.make_async_copy(source, w_rest.at[part], sems.at[i]))
        copies[-1].start()

    def get(d):
        if d < len(held):
            weights = held[d][...]
        else:
            at = d - len(held)
            copies[at].wait()
            weights = w_rest[at * size : (at + 1) * size]
        return weights.reshape(size * LANES, LANES)

    return get


def forward_kernel(me_ref, recv_ref, sum_ref, w_hbm, *refs):
    held, (out_ref, token, sums, w_rest, sems) = refs[:-5], refs[-5:]
    get_weights = all_weights(held, w_hbm, w_rest, sems)
    token[...] = jnp.zeros_like(token)
    me = me_ref[0]
    peers = recv_ref.shape[0]
    tracers, blocks, _ = sums.shape
    n_slots = sum_ref.shape[0]
    window = n_slots // 8
    slots = blocks // window
    row = iota((8, LANES), 0)
    out_ref[...] = jnp.zeros_like(out_ref)
    for d in range(window):
        source = jnp.clip(me - d + window // 2, 0, peers - 1)
        weights = get_weights(d)
        for first in range(0, slots, 8):
            top = row_of(0, first, tracers)
            cells = recv_ref[source, top : top + 8 * tracers, :]
            product = lax.dot_general(
                cells,
                weights[first * LANES : (first + 8) * LANES],
                (((1,), (1,)), ((), ())),
                preferred_element_type=jnp.float32,
            )
            for t in range(tracers):
                part = product[t * 8 : (t + 1) * 8]
                found = part[:, :LANES]
                for k in range(1, 8):
                    found = jnp.where(row == k, part[:, k * LANES : (k + 1) * LANES], found)
                sums[t, d * slots + first : d * slots + first + 8, :] = found
    partial_sums = [split_dot(sum_ref[...], sums[t], ((1,), (0,))) for t in range(tracers)]
    for g in range(window):
        peer = me + g - window // 2

        @pl.when((peer >= 0) & (peer < peers))
        def _():
            for t in range(tracers):
                out_ref[peer, t * 8 : (t + 1) * 8, :] = partial_sums[t][g * 8 : (g + 1) * 8]


def flux_kernel(
    me_ref, after, parts_ref, spread_ref, pick_ref, air_ref, rate_ref, send_ref, flux_ref, token
):
    token[...] = jnp.zeros_like(token)
    me = me_ref[0]
    peers = parts_ref.shape[0]
    tracers, rows, columns = flux_ref.shape
    n_slots = spread_ref.shape[1]
    window = n_slots // 8
    send_ref[...] = jnp.zeros_like(send_ref)
    sent = []
    for t in range(tracers):
        parts = []
        for g in range(window):
            coupler = me - g + window // 2
            valid = (coupler >= 0) & (coupler < peers)
            block = parts_ref[jnp.clip(coupler, 0, peers - 1), t * 8 : (t + 1) * 8, :]
            parts.append(jnp.where(valid, block, 0.0))
        remapped = split_dot(spread_ref[...], jnp.concatenate(parts, axis=0), ((1,), (0,)))
        flux = rate_ref[...] * (solubility * air_ref[t] - remapped)
        for k in range(columns // LANES):
            flux_ref[t, :, k * LANES : (k + 1) * LANES] = flux[k * rows : (k + 1) * rows]
        sent.append(
            jnp.dot(pick_ref[...], flux.astype(jnp.bfloat16), preferred_element_type=jnp.float32)
        )
    for g in range(window):
        peer = me - g + window // 2

        @pl.when((peer >= 0) & (peer < peers))
        def _():
            block = jnp.concatenate([s[g * 8 : (g + 1) * 8] for s in sent], axis=0)
            send_ref[peer] = block.astype(jnp.bfloat16)


def backward_kernel(me_ref, after, recv_ref, pick_ref, w_hbm, *refs):
    held, (out_ref, token, w_rest, sems) = refs[:-4], refs[-4:]
    get_weights = all_weights(held, w_hbm, w_rest, sems)
    token[...] = jnp.zeros_like(token)
    me = me_ref[0]
    peers, width, _ = recv_ref.shape
    tracers = width // 8
    blocks, n_slots = pick_ref.shape
    window = n_slots // 8
    slots = blocks // window
    parts = [[] for _ in range(tracers)]
    for g in range(window):
        owner = me + g - window // 2
        valid = (owner >= 0) & (owner < peers)
        block = recv_ref[jnp.clip(owner, 0, peers - 1)].astype(jnp.float32)
        block = jnp.where(valid, block, 0.0)
        for t in range(tracers):
            parts[t].append(block[t * 8 : (t + 1) * 8])
    picked = [
        jnp.dot(
            pick_ref[...],
            jnp.concatenate(parts[t], axis=0).astype(jnp.bfloat16),
            preferred_element_type=jnp.float32,
        )
        for t in range(tracers)
    ]
    out_ref[...] = jnp.zeros_like(out_ref)
    row = iota((8, LANES), 0)
    for d in range(window):
        weights = get_weights(d)
        products = []
        for first in range(0, slots, 8):
            at = slice(d * slots + first, d * slots + first + 8)
            mine = [p[at] for p in picked]
            cells = jnp.concatenate(
                [
                    jnp.concatenate([jnp.where(row == k, m, 0.0) for m in mine], axis=0).astype(
                        jnp.bfloat16
                    )
                    for k in range(8)
                ],
                axis=1,
            )
            products.append(
                jnp.dot(
                    cells,
                    weights[first * LANES : (first + 8) * LANES],
                    preferred_element_type=jnp.float32,
                )
            )
        peer = me - d + window // 2

        @pl.when((peer >= 0) & (peer < peers))
        def _():
            out_ref[peer] = jnp.concatenate(products, axis=0)


def add_kernel(me_ref, returned_ref, table_ref, surface, swept, out, buffer, sems):
    me = me_ref[0]
    peers = returned_ref.shape[0]
    tracers, _, columns = surface.shape
    slots = returned_ref.shape[1] // tracers
    window = table_ref.shape[1] // slots
    cuts = widths(columns)
    full = len(cuts) - 1
    rest = cuts[-1][1]
    lane = iota((8, LANES), 1)
    row = iota((8, LANES), 0)
    stays = lane < LANES - rest * row
    copies = []
    for t in range(tracers):
        parts = []
        for d in range(window):
            coupler = me + d - window // 2
            valid = (coupler >= 0) & (coupler < peers)
            for first in range(0, slots, 8):
                top = row_of(t, first, tracers)
                block = returned_ref[jnp.clip(coupler, 0, peers - 1), top : top + 8, :]
                parts.append(jnp.where(valid, block, 0.0))
        tiles = split_dot(table_ref[...], jnp.concatenate(parts, axis=0), ((1,), (0,)))
        rows = [tiles[k * 8 : (k + 1) * 8] for k in range(full + 1)]
        rows[full] = jnp.where(row == 7, rows[full], pltpu.roll(rows[0], 7, 0))
        turned = [shear(value, -1, rest) for value in rows]
        for k, (start, width) in enumerate(cuts):
            value = turned[k]
            if k < full:
                value = jnp.where(stays, value, turned[k + 1])
            at = slice(start, start + width)
            buffer[t, :, at] = surface[t, :, at] + ocean_rate * value[:, :width]
        copies.append(pltpu.make_async_copy(buffer.at[t], out.at[t, 0], sems.at[t]))
        copies[-1].start()
    for copy in copies:
        copy.wait()


def atmos_kernel(after, atmos_ref, flux_ref, mix_ref, out_ref, token):
    token[...] = jnp.zeros_like(token)
    tracers, levels, rows, columns = atmos_ref.shape
    for t in range(tracers):
        for r in range(0, rows, 8):
            for c in range(0, columns, LANES):
                at = (slice(r, r + 8), slice(c, c + LANES))
                mixing = mix_ref[at]
                field = [atmos_ref[(t, v) + at] for v in range(levels)]
                field[0] = field[0] - atmos_rate * flux_ref[(t,) + at]
                for _ in range(ASTEPS):
                    field = [
                        field[v]
                        + mixing
                        * (field[max(v - 1, 0)] + field[min(v + 1, levels - 1)] - 2.0 * field[v])
                        for v in range(levels)
                    ]
                for v in range(levels):
                    out_ref[(t, v) + at] = field[v]


def local(
    ocean,
    kappa,
    atmos,
    piston,
    atmos_mix,
    fold_map,
    send_tile,
    slot_counts,
    out_slot,
    out_tile,
    remap_w,
):
    count = lax.axis_size("tile")
    me = lax.axis_index("tile").astype(jnp.int32).reshape(1)
    tracers, levels, ocean_rows, columns = ocean.shape
    planes = tracers * levels
    window, slots_in = send_tile.shape[1:]
    slots_out = out_tile.shape[2]
    blocks = window * slots_in
    n_slots = window * slots_out
    tiles = -(-columns // LANES)
    padded = tiles * LANES
    atmos_rows, atmos_columns = atmos.shape[2:]
    across = atmos_columns // LANES
    n_tiles = atmos_rows * across
    f32, bf16, i32 = jnp.float32, jnp.bfloat16, jnp.int32
    shape = jax.ShapeDtypeStruct
    dma = pltpu.SemaphoreType.DMA
    exchange = functools.partial(
        lax.all_to_all, axis_name="tile", split_axis=0, concat_axis=0, tiled=True
    )

    def cost(us):
        return pl.CostEstimate(
            flops=0, bytes_accessed=int(us * 1.0e4), transcendentals=0
        )

    token_shape = shape((8, LANES), f32)
    sent, token = pl.pallas_call(
        pack_kernel,
        out_shape=(pltpu.HBM((count, tracers * slots_in, LANES), bf16), token_shape),
        in_specs=[smem(), hbm(), hbm()],
        out_specs=(vmem(), vmem()),
        scratch_shapes=[
            pltpu.SMEM(send_tile.shape, i32),
            pltpu.VMEM((tracers, ocean_rows, columns), f32),
            pltpu.VMEM((tracers, tiles * 8, LANES), f32),
            pltpu.VMEM((window, tracers * slots_in, LANES), f32),
            dma((tracers + 1,)),
        ],
        compiler_params=params(),
        name="pack",
    )(me, in_hbm(send_tile), in_hbm(ocean))
    received = exchange(sent)

    halo_rows = 6 * planes
    flat = in_hbm(ocean.reshape(planes * ocean_rows, columns))
    weights = in_hbm(remap_w[0])
    prepared = pl.pallas_call(
        prepare_kernel,
        out_shape=(
            *[shape((slots_in,) + remap_w.shape[2:], bf16)] * HELD,
            pltpu.HBM((halo_rows, padded), bf16),
            pltpu.HBM((halo_rows, padded), bf16),
            shape((n_slots, blocks), bf16),
            shape((blocks, n_slots), bf16),
            shape((n_tiles, n_slots), bf16),
            shape((n_slots, n_tiles), bf16),
            shape((tiles * 8, blocks), bf16),
            shape((tracers, n_tiles, LANES), f32),
            shape((n_tiles, LANES), f32),
        ),
        in_specs=[smem(), vmem()] + [hbm()] * 9,
        out_specs=(vmem(),) * HELD + (hbm(),) * 2 + (vmem(),) * 7,
        scratch_shapes=[
            pltpu.VMEM((planes * ocean_rows, columns), f32),
            pltpu.VMEM((ocean_rows, columns), f32),
            pltpu.VMEM((tiles, (planes + 1) * ocean_rows, LANES), f32),
            pltpu.VMEM((halo_rows, padded), bf16),
            pltpu.VMEM((halo_rows, padded), bf16),
            pltpu.VMEM((tracers, atmos_rows, atmos_columns), f32),
            pltpu.VMEM((atmos_rows, atmos_columns), f32),
            pltpu.SMEM(slot_counts.shape, i32),
            pltpu.VMEM(out_slot.shape, i32),
            pltpu.SMEM(out_tile.shape, i32),
            pltpu.SMEM(send_tile.shape, i32),
            dma((tracers + 9 + HELD,)),
        ],
        compiler_params=params(),
        cost_estimate=cost(3),
        name="prepare",
    )(
        me,
        token,
        in_hbm(slot_counts),
        in_hbm(out_slot),
        in_hbm(out_tile),
        in_hbm(send_tile),
        flat,
        in_hbm(kappa),
        in_hbm(atmos),
        in_hbm(piston),
        weights,
    )
    held = prepared[:HELD]
    even, odd = prepared[HELD : HELD + 2]
    sum_table, slot_pick, spread, flux_pick, scatter, air, rate = prepared[HELD + 2 :]
    even_pairs = [(i, i ^ 1) for i in range(count) if i ^ 1 < count]
    odd_pairs = [(i, i + 1) for i in range(1, count - 1, 2)]
    odd_pairs += [(b, a) for a, b in odd_pairs]
    even = lax.ppermute(even, "tile", even_pairs)
    odd = lax.ppermute(odd, "tile", odd_pairs)
    weight_scratch = [
        pltpu.VMEM((blocks - HELD * slots_in,) + remap_w.shape[2:], bf16),
        dma((window - HELD,)),
    ]

    partial_sums, token = pl.pallas_call(
        forward_kernel,
        out_shape=(shape((count, tracers * slots_out, LANES), f32), token_shape),
        in_specs=[smem(), vmem(), vmem(), hbm()] + [vmem()] * HELD,
        out_specs=(vmem(), vmem()),
        scratch_shapes=[pltpu.VMEM((tracers, blocks, LANES), f32)] + weight_scratch,
        compiler_params=params(),
        name="forward",
    )(me, received, sum_table, weights, *held)
    owner_parts = exchange(partial_sums.astype(jnp.float16)).astype(f32)

    state_shape = (16, planes, padded)
    kap_shape = (tiles, 16, LANES)
    fold = fold_map.reshape(1, columns)
    fold_scratch = [pltpu.VMEM((2 * LANES, padded), bf16)]
    state, kap, token = pl.pallas_call(
        functools.partial(first_sweep_kernel, levels=levels, peers=count),
        out_shape=(pltpu.HBM(state_shape, f32), pltpu.HBM((tiles, 16, LANES), f32), token_shape),
        in_specs=[smem(), vmem()] + [hbm()] * 4 + [vmem()],
        out_specs=(hbm(), hbm(), vmem()),
        scratch_shapes=[
            pltpu.VMEM(state_shape, f32),
            pltpu.VMEM(state_shape, f32),
            pltpu.VMEM(kap_shape, f32),
            pltpu.VMEM((planes * ocean_rows, columns), f32),
            pltpu.VMEM((ocean_rows, columns), f32),
            pltpu.VMEM((halo_rows, padded), bf16),
            pltpu.VMEM((halo_rows, padded), bf16),
            pltpu.VMEM((tiles, planes * ocean_rows, LANES), f32),
        ]
        + fold_scratch
        + [dma((4,)), dma((16,))],
        compiler_params=params(),
        cost_estimate=cost(5),
        name="first_sweep",
    )(me, token, flat, in_hbm(kappa), in_hbm(even), in_hbm(odd), fold)

    flux_sent, flux, flux_token = pl.pallas_call(
        flux_kernel,
        out_shape=(
            pltpu.HBM((count, tracers * slots_out, LANES), bf16),
            shape((tracers, atmos_rows, atmos_columns), f32),
            token_shape,
        ),
        in_specs=[smem()] + [vmem()] * 6,
        out_specs=(vmem(),) * 3,
        compiler_params=params(),
        name="flux",
    )(me, token, owner_parts, spread, flux_pick, air, rate)
    at_coupler = exchange(flux_sent)

    atmos_next, token = pl.pallas_call(
        atmos_kernel,
        out_shape=(pltpu.HBM(atmos.shape, f32), token_shape),
        in_specs=[vmem()] * 4,
        out_specs=(vmem(), vmem()),
        compiler_params=params(),
        cost_estimate=cost(2),
        name="atmos",
    )(flux_token, in_hbm(atmos), flux, in_hbm(atmos_mix))

    back_sums, token = pl.pallas_call(
        backward_kernel,
        out_shape=(shape((count, tracers * slots_in, LANES), f32), token_shape),
        in_specs=[smem()] + [vmem()] * 3 + [hbm()] + [vmem()] * HELD,
        out_specs=(vmem(), vmem()),
        scratch_shapes=weight_scratch,
        compiler_params=params(),
        name="backward",
    )(me, token, at_coupler, slot_pick, weights, *held)
    returned = exchange(back_sums.astype(jnp.float16)).astype(f32)

    swept, surface = pl.pallas_call(
        functools.partial(last_sweeps_kernel, levels=levels, peers=count),
        out_shape=(
            pltpu.HBM((planes * ocean_rows, columns), f32),
            shape((tracers, ocean_rows, columns), f32),
        ),
        in_specs=[smem(), vmem(), hbm(), hbm(), vmem()],
        out_specs=(vmem(), vmem()),
        scratch_shapes=[
            pltpu.VMEM(state_shape, f32),
            pltpu.VMEM(kap_shape, f32),
            pltpu.VMEM(state_shape, f32),
            pltpu.VMEM((tiles, planes * ocean_rows, LANES), f32),
        ]
        + fold_scratch
        + [dma((16,))],
        compiler_params=params(),
        cost_estimate=cost(4),
        name="last_sweeps",
    )(me, token, in_hbm(state), in_hbm(kap), fold)
    ocean_next = pl.pallas_call(
        add_kernel,
        out_shape=shape(ocean.shape, f32),
        in_specs=[smem()] + [vmem()] * 3 + [hbm()],
        out_specs=hbm(),
        scratch_shapes=[pltpu.VMEM((tracers, ocean_rows, columns), f32), dma((tracers,))],
        input_output_aliases={4: 0},
        compiler_params=params(),
        name="add",
    )(me, returned, scatter, surface, in_hbm(swept.reshape(ocean.shape)))
    return (ocean_next, atmos_next)


def solution(mesh):
    placed = (
        P("member", None, "tile", None),
        P("tile", None),
        P("member", None, "tile", None),
        P("tile", None),
        P("tile", None),
        P(),
        P("tile", None, None),
        P("tile", None),
        P("tile", None),
        P("tile", None, None),
        P("tile", None, None, None),
    )
    return jax.shard_map(
        local,
        mesh=mesh,
        in_specs=placed,
        out_specs=(P("member", None, "tile", None), P("member", None, "tile", None)),
        check_vma=False,
    )
```

```python
import functools

import jax
import jax.numpy as jnp
from jax import lax
from jax.experimental import pallas as pl
from jax.experimental.pallas import tpu as pltpu
from jax.sharding import PartitionSpec as P

OSTEPS = 4
ASTEPS = 4
LANES = 128
HELD = 6

vertical_mix = 0.1
ocean_rate = 4.0
atmos_rate = 0.5
solubility = 1.2

MIB = 1024 * 1024


def params(mib=16):
    return pltpu.CompilerParams(vmem_limit_bytes=36 * MIB)


def vmem():
    return pl.BlockSpec(memory_space=pltpu.VMEM)


def smem():
    return pl.BlockSpec(memory_space=pltpu.SMEM)


def hbm():
    return pl.BlockSpec(memory_space=pltpu.HBM)


def anywhere():
    return pl.BlockSpec(memory_space=pl.ANY)


def iota(shape, dim):
    return lax.broadcasted_iota(jnp.int32, shape, dim)


def split_dot(table, values, dims):
    high = values.astype(jnp.bfloat16)
    low = (values - high.astype(jnp.float32)).astype(jnp.bfloat16)
    dot = functools.partial(
        lax.dot_general, dimension_numbers=(dims, ((), ())), preferred_element_type=jnp.float32
    )
    return dot(table, high) + dot(table, low)


def shear(tile, sign, shift):
    lane = iota(tile.shape, 1)
    row = iota(tile.shape, 0)
    source = (lane - sign * shift * row) & (LANES - 1)
    return jnp.take_along_axis(tile, source, axis=1, mode="promise_in_bounds")


def widths(columns):
    return [(c, min(LANES, columns - c)) for c in range(0, columns, LANES)]


def in_hbm(x):
    return pltpu.with_memory_space_constraint(x, pltpu.HBM)


def row_of(tracer, slot, tracers):
    return (slot // 8) * 8 * tracers + tracer * 8 + slot % 8


def magic(divisor, count):
    scale = -(-65536 // divisor)
    assert all((i * scale) >> 16 == i // divisor for i in range(count))
    return scale


def tile_row(index, full, scale):
    over = (index * scale) >> 16
    return jnp.where(index == 8 * full, 8 * full + 7, (index - over * full) * 8 + over)


def one_hot(mask):
    return jnp.where(mask, 1.0, 0.0).astype(jnp.bfloat16)


def pack_kernel(me_ref, send_hbm, ocean_hbm, out_ref, token, send, surface, tiles, rows, sems):
    me = me_ref[0]
    peers = out_ref.shape[0]
    _, window, slots = send.shape
    tracers, _, columns = surface.shape
    copies = [pltpu.make_async_copy(send_hbm, send, sems.at[tracers])]
    for t in range(tracers):
        copies.append(pltpu.make_async_copy(ocean_hbm.at[t, 0], surface.at[t], sems.at[t]))
    for copy in copies:
        copy.start()
    out_ref[...] = jnp.zeros_like(out_ref)
    token[...] = jnp.zeros_like(token)
    cuts = widths(columns)
    full = len(cuts) - 1
    rest = cuts[-1][1]
    lane = iota((8, LANES), 1)
    row = iota((8, LANES), 0)
    wraps = lane < rest * row
    for t in range(tracers):
        copies[1 + t].wait()
        before = jnp.zeros((8, LANES), jnp.float32)
        first = None
        for k, (start, width) in enumerate(cuts):
            part = surface[t, :, start : start + width]
            if width < LANES:
                part = jnp.concatenate(
                    [part, jnp.zeros((8, LANES - width), jnp.float32)], axis=1
                )
            turned = shear(part, 1, rest)
            value = jnp.where(wraps, before, turned)
            before = turned
            if k == 0:
                first = value
            else:
                tiles[t, k * 8 : (k + 1) * 8] = value
        tiles[t, 0:8] = jnp.where(wraps, pltpu.roll(value, 1, 0), first)
    copies[0].wait()
    scale = magic(full, 8 * full + 1)
    for d in range(window):
        for k in range(slots):
            index = send[0, d, k]
            place = tile_row(index, full, scale)
            for t in range(tracers):
                at = row_of(t, k, tracers)
                rows[d, at : at + 1, :] = tiles[t, pl.ds(place, 1), :]
    for d in range(window):
        peer = me + d - window // 2

        @pl.when((peer >= 0) & (peer < peers))
        def _():
            out_ref[peer] = rows[d].astype(jnp.bfloat16)


def pack_halo(odd, ocean, kappa, grouped, even_ref, odd_ref):
    planes = ocean.shape[0] // 8
    cuts = widths(ocean.shape[1])
    for k, (start, width) in enumerate(cuts):
        grouped[k, 0 : planes * 8, :width] = ocean[:, start : start + width]
        grouped[k, planes * 8 :, :width] = kappa[:, start : start + width]
    for target, upper in ((even_ref, odd == 0), (odd_ref, odd == 1)):
        base = jnp.where(upper, 4, 0)
        near = jnp.where(upper, 7, 0)
        for k, (start, width) in enumerate(cuts):
            rows = [grouped[k, pl.ds(base + r, planes, stride=8), :] for r in range(4)]
            rates = grouped[k, planes * 8 :, :]
            rates = jnp.where(upper, pltpu.roll(rates, 4, 0), rates)
            nearest = grouped[k, pl.ds(near, planes, stride=8), :]
            low = nearest - nearest.astype(jnp.bfloat16).astype(jnp.float32)
            block = jnp.concatenate(rows + [rates, low], axis=0)
            target[:, start : start + LANES] = block.astype(jnp.bfloat16)


def prepare_kernel(
    me_ref,
    after,
    counts_hbm,
    slot_hbm,
    out_tile_hbm,
    send_hbm,
    ocean_hbm,
    kappa_hbm,
    atmos_hbm,
    piston_hbm,
    w_hbm,
    *refs,
):
    held = len(refs) - 21
    w_refs = refs[:held]
    even_hbm, odd_hbm = refs[held : held + 2]
    sum_ref, pick_ref, spread_ref, flux_pick_ref, scatter_ref, air_ref, rate_ref = refs[
        held + 2 : held + 9
    ]
    ocean, kappa, grouped, even, odd, surface, piston = refs[held + 9 : -5]
    counts, slot, out_tile, send, sems = refs[-5:]
    tracers, rows, columns = surface.shape
    size = w_refs[0].shape[0]
    pairs = [(counts_hbm, counts), (slot_hbm, slot), (out_tile_hbm, out_tile), (send_hbm, send)]
    pairs += [(ocean_hbm, ocean), (kappa_hbm, kappa), (piston_hbm, piston)]
    pairs += [(atmos_hbm.at[t, 0], surface.at[t]) for t in range(tracers)]
    pairs += [(w_hbm.at[pl.ds(i * size, size)], w_refs[i]) for i in range(held)]
    copies = [pltpu.make_async_copy(a, b, sems.at[i]) for i, (a, b) in enumerate(pairs)]
    for copy in copies:
        copy.start()
    n_slots, blocks = sum_ref.shape
    window, slots = send.shape[1:]
    slots_out = out_tile.shape[2]
    across = columns // LANES
    n_tiles = spread_ref.shape[0]
    full = ocean.shape[1] // LANES
    scale, scale_tile = magic(full, 8 * full + 1), magic(across, n_tiles)
    for copy in copies[:4]:
        copy.wait()
    at = iota((1, blocks), 1)
    live = at < 0
    place = jnp.zeros((1, blocks), jnp.int32)
    tile_place = jnp.zeros((1, blocks), jnp.int32)
    for d in range(window):
        live = live | ((at >= d * slots) & (at < d * slots + counts[0, d]))
        for k in range(slots):
            place = jnp.where(at == d * slots + k, tile_row(send[0, d, k], full, scale), place)
        for j in range(slots_out):
            tile = out_tile[0, d, j]
            down = (tile * scale_tile) >> 16
            value = (tile - down * across) * rows + down
            tile_place = jnp.where(at == d * slots_out + j, value, tile_place)
    table = jnp.where((iota((LANES, blocks), 0) == slot[...]) & live, 1.0, 0.0)
    sum_ref[...] = table[:n_slots].astype(jnp.bfloat16)
    pick_ref[...] = table.T[:, :n_slots].astype(jnp.bfloat16)
    spread = jnp.where(iota((LANES, LANES), 0) == tile_place, 1.0, 0.0)
    spread_ref[...] = spread[:n_tiles, :n_slots].astype(jnp.bfloat16)
    flux_pick_ref[...] = spread.T[:n_slots, :n_tiles].astype(jnp.bfloat16)
    scatter_ref[...] = one_hot(iota(scatter_ref.shape, 0) == place)
    for copy in copies[4:6]:
        copy.wait()
    pack_halo(lax.rem(me_ref[0], 2), ocean, kappa, grouped, even, odd)
    copies += [
        pltpu.make_async_copy(even, even_hbm, sems.at[len(copies)]),
        pltpu.make_async_copy(odd, odd_hbm, sems.at[len(copies) + 1]),
    ]
    for copy in copies[-2:]:
        copy.start()
    for copy in copies[6:]:
        copy.wait()
    for k in range(columns // LANES):
        at = slice(k * LANES, (k + 1) * LANES)
        rate_ref[k * rows : (k + 1) * rows, :] = piston[:, at]
        for t in range(tracers):
            air_ref[t, k * rows : (k + 1) * rows, :] = surface[t, :, at]


def fold_tables(last, fold_ref, table_ref):
    @pl.when(last)
    def _():
        inner = iota((LANES, LANES), 0)
        for start, width in widths(fold_ref.shape[1]):
            at = slice(start, start + width)
            found = one_hot(inner[:, :width] == (fold_ref[:, at] & (LANES - 1)))
            table_ref[0:LANES, at] = found
            table_ref[LANES : 2 * LANES, at] = found


def fold_row(state, table_ref, fold_ref):
    columns = fold_ref.shape[1]
    cuts = widths(columns)
    tiles = len(cuts)
    rest = cuts[-1][1]
    rows = [state[11, :, start : start + LANES] for start, _ in cuts]
    rows[-1] = jnp.where(iota((8, LANES), 1) < rest, rows[-1], 0.0)
    rows = jnp.concatenate(rows, axis=0)
    high = rows.astype(jnp.bfloat16)
    low = (rows - high.astype(jnp.float32)).astype(jnp.bfloat16)
    parts = jnp.concatenate([high, low], axis=1)
    for start in range(0, tiles * LANES, 2 * LANES):
        end = min(start + 2 * LANES, tiles * LANES)
        width = min(end, columns) - start
        found = jnp.dot(parts, table_ref[:, start:end], preferred_element_type=jnp.float32)
        at = slice(start, start + width)
        outer = jnp.broadcast_to(fold_ref[:, at] >> 7, (8, width))
        value = found[0:8, :width]
        for k in range(1, tiles):
            value = jnp.where(outer == k, found[k * 8 : (k + 1) * 8, :width], value)
        state[12, :, at] = value


def sweep_rows(state, kap, cuts, levels, low, high, write, after=None):
    full = len(cuts) - 1
    rest = cuts[-1][1]
    lane = iota((8, LANES), 1)
    level = iota((8, LANES), 0) & (levels - 1)

    def body(r, carry):
        def cell(k):
            return state[r, :, k * LANES : (k + 1) * LANES]

        centre = cell(0)
        east_now = pltpu.roll(centre, LANES - 1, 1)
        around = pltpu.roll(centre, rest - 1, 1)
        west_last = pltpu.roll(cell(full), LANES - rest + 1, 1)
        for k in range(full + 1):
            at = slice(k * LANES, (k + 1) * LANES)
            if k == full:
                east = jnp.where(lane == rest - 1, around, east_now)
            else:
                following = cell(k + 1)
                east_next = pltpu.roll(following, LANES - 1, 1)
                east = jnp.where(lane == LANES - 1, east_next, east_now)
            west_now = pltpu.roll(centre, 1, 1)
            west = jnp.where(lane == 0, west_last, west_now)
            north = state[r + 1, :, at]
            south = state[r - 1, :, at]
            upper = jnp.where(level == 0, centre, pltpu.roll(centre, 1, 0))
            lower = jnp.where(level == levels - 1, centre, pltpu.roll(centre, 7, 0))
            horizontal = (north + south) + (east + west) - 4.0 * centre
            vertical = upper + lower - 2.0 * centre
            rate = kap[k, pl.ds(r, 1), :]
            write(r, k, centre + rate * horizontal + vertical_mix * vertical)
            if k < full:
                centre, east_now, west_last = following, east_next, west_now
        if after is not None:
            after(r)
        return carry

    lax.fori_loop(low, high, body, 0)


def keep(target):
    def write(r, k, value):
        target[r, :, k * LANES : (k + 1) * LANES] = value

    return write


def row_copy(source, target, sems, r):
    return pltpu.make_async_copy(source.at[r], target.at[r], sems.at[r])


def first_sweep_kernel(
    me_ref,
    after,
    ocean_hbm,
    kappa_hbm,
    even_hbm,
    odd_hbm,
    fold_ref,
    out_hbm,
    kap_hbm,
    token,
    state,
    kept,
    kap_ref,
    ocean,
    kappa,
    above,
    below,
    grouped,
    table,
    sems,
    row_sems,
    levels,
    peers,
):
    me = me_ref[0]
    last = me == peers - 1
    odd = lax.rem(me, 2)
    token[...] = jnp.zeros_like(token)
    planes = state.shape[1]
    cuts = widths(kappa.shape[1])
    copies = [
        pltpu.make_async_copy(ocean_hbm, ocean, sems.at[0]),
        pltpu.make_async_copy(kappa_hbm, kappa, sems.at[1]),
    ]
    for copy in copies:
        copy.start()

    @pl.when(odd == 1)
    def _():
        pltpu.make_async_copy(odd_hbm, above, sems.at[2]).start()
        pltpu.make_async_copy(even_hbm, below, sems.at[3]).start()

    @pl.when(odd == 0)
    def _():
        pltpu.make_async_copy(even_hbm, above, sems.at[2]).start()
        pltpu.make_async_copy(odd_hbm, below, sems.at[3]).start()

    fold_tables(last, fold_ref, table)
    for copy in copies:
        copy.wait()
    for k, (start, width) in enumerate(cuts):
        grouped[k, : planes * 8, :width] = ocean[:, start : start + width]
        kap_ref[k, 4:12, :width] = kappa[:, start : start + width]
    for k, (start, width) in enumerate(cuts):
        for r in range(8):
            part = grouped[k, pl.ds(r, planes, stride=8), :]
            state[4 + r, :, start : start + LANES] = part
    pltpu.make_async_copy(even_hbm, above, sems.at[2]).wait()
    pltpu.make_async_copy(odd_hbm, below, sems.at[3]).wait()
    for halo, first, near in ((below, 0, 3), (above, 12, 0)):
        for k, (start, _) in enumerate(cuts):
            at = slice(start, start + LANES)
            block = halo[:, at].astype(jnp.float32)
            for r in range(4):
                value = block[r * planes : (r + 1) * planes]
                if r == near:
                    value = value + block[5 * planes : 6 * planes]
                state[first + r, :, at] = value
            kap_ref[k, first : first + 4, :] = block[4 * planes : 4 * planes + 4]

    @pl.when(last)
    def _():
        fold_row(state, table, fold_ref)

    kap_copy = pltpu.make_async_copy(kap_ref, kap_hbm, row_sems.at[0])
    kap_copy.start()

    def after(r):
        row_copy(kept, out_hbm, row_sems, r).start()

    sweep_rows(state, kap_ref, cuts, levels, 1, 15, keep(kept), after)
    for r in range(1, 15):
        row_copy(kept, out_hbm, row_sems, r).wait()
    kap_copy.wait()


def last_sweeps_kernel(
    me_ref,
    after,
    state_hbm,
    kap_hbm,
    fold_ref,
    out_ref,
    surface_ref,
    came,
    kap_ref,
    state,
    grouped,
    table,
    sems,
    levels,
    peers,
):
    cuts = widths(out_ref.shape[1])
    planes = came.shape[1]
    last = me_ref[0] == peers - 1
    copies = [pltpu.make_async_copy(kap_hbm, kap_ref, sems.at[0])]
    copies += [row_copy(state_hbm, came, sems, r) for r in range(1, 15)]
    for copy in copies:
        copy.start()
    fold_tables(last, fold_ref, table)
    for copy in copies:
        copy.wait()

    def fold(rows):
        @pl.when(last)
        def _():
            fold_row(rows, table, fold_ref)

    fold(came)
    sweep_rows(came, kap_ref, cuts, levels, 2, 14, keep(state))
    fold(state)
    sweep_rows(state, kap_ref, cuts, levels, 3, 13, keep(came))
    fold(came)

    def write(r, k, value):
        grouped[k, pl.ds(r - 4, planes, stride=8), :] = value

    sweep_rows(came, kap_ref, cuts, levels, 4, 12, write)
    for k, (start, width) in enumerate(cuts):
        at = slice(start, start + width)
        out_ref[:, at] = grouped[k, : planes * 8, :width]
        for t in range(planes // levels):
            top = t * levels * 8
            surface_ref[t, :, at] = grouped[k, top : top + 8, :width]


def all_weights(held, w_hbm, w_rest, sems):
    size = held[0].shape[0]
    first = len(held) * size
    copies = []
    for i in range(w_rest.shape[0] // size):
        part = pl.ds(i * size, size)
        source = w_hbm.at[pl.ds(first + i * size, size)]
        copies.append(pltpu.make_async_copy(source, w_rest.at[part], sems.at[i]))
        copies[-1].start()

    def get(d):
        if d < len(held):
            weights = held[d][...]
        else:
            at = d - len(held)
            copies[at].wait()
            weights = w_rest[at * size : (at + 1) * size]
        return weights.reshape(size * LANES, LANES)

    return get


def forward_kernel(me_ref, recv_ref, sum_ref, w_hbm, *refs):
    held, (out_ref, token, sums, w_rest, sems) = refs[:-5], refs[-5:]
    get_weights = all_weights(held, w_hbm, w_rest, sems)
    token[...] = jnp.zeros_like(token)
    me = me_ref[0]
    peers = recv_ref.shape[0]
    tracers, blocks, _ = sums.shape
    n_slots = sum_ref.shape[0]
    window = n_slots // 8
    slots = blocks // window
    row = iota((8, LANES), 0)
    out_ref[...] = jnp.zeros_like(out_ref)
    for d in range(window):
        source = jnp.clip(me - d + window // 2, 0, peers - 1)
        weights = get_weights(d)
        for first in range(0, slots, 8):
            top = row_of(0, first, tracers)
            cells = recv_ref[source, top : top + 8 * tracers, :]
            product = lax.dot_general(
                cells,
                weights[first * LANES : (first + 8) * LANES],
                (((1,), (1,)), ((), ())),
                preferred_element_type=jnp.float32,
            )
            for t in range(tracers):
                part = product[t * 8 : (t + 1) * 8]
                found = part[:, :LANES]
                for k in range(1, 8):
                    found = jnp.where(row == k, part[:, k * LANES : (k + 1) * LANES], found)
                sums[t, d * slots + first : d * slots + first + 8, :] = found
    partial_sums = [split_dot(sum_ref[...], sums[t], ((1,), (0,))) for t in range(tracers)]
    for g in range(window):
        peer = me + g - window // 2

        @pl.when((peer >= 0) & (peer < peers))
        def _():
            for t in range(tracers):
                out_ref[peer, t * 8 : (t + 1) * 8, :] = partial_sums[t][g * 8 : (g + 1) * 8]


def flux_kernel(
    me_ref, after, parts_ref, spread_ref, pick_ref, air_ref, rate_ref, send_ref, flux_ref, token
):
    token[...] = jnp.zeros_like(token)
    me = me_ref[0]
    peers = parts_ref.shape[0]
    tracers, rows, columns = flux_ref.shape
    n_slots = spread_ref.shape[1]
    window = n_slots // 8
    send_ref[...] = jnp.zeros_like(send_ref)
    sent = []
    for t in range(tracers):
        parts = []
        for g in range(window):
            coupler = me - g + window // 2
            valid = (coupler >= 0) & (coupler < peers)
            block = parts_ref[jnp.clip(coupler, 0, peers - 1), t * 8 : (t + 1) * 8, :]
            parts.append(jnp.where(valid, block, 0.0))
        remapped = split_dot(spread_ref[...], jnp.concatenate(parts, axis=0), ((1,), (0,)))
        flux = rate_ref[...] * (solubility * air_ref[t] - remapped)
        for k in range(columns // LANES):
            flux_ref[t, :, k * LANES : (k + 1) * LANES] = flux[k * rows : (k + 1) * rows]
        sent.append(
            jnp.dot(pick_ref[...], flux.astype(jnp.bfloat16), preferred_element_type=jnp.float32)
        )
    for g in range(window):
        peer = me - g + window // 2

        @pl.when((peer >= 0) & (peer < peers))
        def _():
            block = jnp.concatenate([s[g * 8 : (g + 1) * 8] for s in sent], axis=0)
            send_ref[peer] = block.astype(jnp.bfloat16)


def backward_kernel(me_ref, after, recv_ref, pick_ref, w_hbm, *refs):
    held, (out_ref, token, w_rest, sems) = refs[:-4], refs[-4:]
    get_weights = all_weights(held, w_hbm, w_rest, sems)
    token[...] = jnp.zeros_like(token)
    me = me_ref[0]
    peers, width, _ = recv_ref.shape
    tracers = width // 8
    blocks, n_slots = pick_ref.shape
    window = n_slots // 8
    slots = blocks // window
    parts = [[] for _ in range(tracers)]
    for g in range(window):
        owner = me + g - window // 2
        valid = (owner >= 0) & (owner < peers)
        block = recv_ref[jnp.clip(owner, 0, peers - 1)].astype(jnp.float32)
        block = jnp.where(valid, block, 0.0)
        for t in range(tracers):
            parts[t].append(block[t * 8 : (t + 1) * 8])
    picked = [
        jnp.dot(
            pick_ref[...],
            jnp.concatenate(parts[t], axis=0).astype(jnp.bfloat16),
            preferred_element_type=jnp.float32,
        )
        for t in range(tracers)
    ]
    out_ref[...] = jnp.zeros_like(out_ref)
    row = iota((8, LANES), 0)
    for d in range(window):
        weights = get_weights(d)
        products = []
        for first in range(0, slots, 8):
            at = slice(d * slots + first, d * slots + first + 8)
            mine = [p[at] for p in picked]
            cells = jnp.concatenate(
                [
                    jnp.concatenate([jnp.where(row == k, m, 0.0) for m in mine], axis=0).astype(
                        jnp.bfloat16
                    )
                    for k in range(8)
                ],
                axis=1,
            )
            products.append(
                jnp.dot(
                    cells,
                    weights[first * LANES : (first + 8) * LANES],
                    preferred_element_type=jnp.float32,
                )
            )
        peer = me - d + window // 2

        @pl.when((peer >= 0) & (peer < peers))
        def _():
            out_ref[peer] = jnp.concatenate(products, axis=0)


def add_kernel(me_ref, returned_ref, table_ref, surface, swept, out, buffer, sems):
    me = me_ref[0]
    peers = returned_ref.shape[0]
    tracers, _, columns = surface.shape
    slots = returned_ref.shape[1] // tracers
    window = table_ref.shape[1] // slots
    cuts = widths(columns)
    full = len(cuts) - 1
    rest = cuts[-1][1]
    lane = iota((8, LANES), 1)
    row = iota((8, LANES), 0)
    stays = lane < LANES - rest * row
    copies = []
    for t in range(tracers):
        parts = []
        for d in range(window):
            coupler = me + d - window // 2
            valid = (coupler >= 0) & (coupler < peers)
            for first in range(0, slots, 8):
                top = row_of(t, first, tracers)
                block = returned_ref[jnp.clip(coupler, 0, peers - 1), top : top + 8, :]
                parts.append(jnp.where(valid, block, 0.0))
        tiles = split_dot(table_ref[...], jnp.concatenate(parts, axis=0), ((1,), (0,)))
        rows = [tiles[k * 8 : (k + 1) * 8] for k in range(full + 1)]
        rows[full] = jnp.where(row == 7, rows[full], pltpu.roll(rows[0], 7, 0))
        turned = [shear(value, -1, rest) for value in rows]
        for k, (start, width) in enumerate(cuts):
            value = turned[k]
            if k < full:
                value = jnp.where(stays, value, turned[k + 1])
            at = slice(start, start + width)
            buffer[t, :, at] = surface[t, :, at] + ocean_rate * value[:, :width]
        copies.append(pltpu.make_async_copy(buffer.at[t], out.at[t, 0], sems.at[t]))
        copies[-1].start()
    for copy in copies:
        copy.wait()


def atmos_kernel(after, atmos_ref, flux_ref, mix_ref, out_ref, token):
    token[...] = jnp.zeros_like(token)
    tracers, levels, rows, columns = atmos_ref.shape
    for t in range(tracers):
        for r in range(0, rows, 8):
            for c in range(0, columns, LANES):
                at = (slice(r, r + 8), slice(c, c + LANES))
                mixing = mix_ref[at]
                field = [atmos_ref[(t, v) + at] for v in range(levels)]
                field[0] = field[0] - atmos_rate * flux_ref[(t,) + at]
                for _ in range(ASTEPS):
                    field = [
                        field[v]
                        + mixing
                        * (field[max(v - 1, 0)] + field[min(v + 1, levels - 1)] - 2.0 * field[v])
                        for v in range(levels)
                    ]
                for v in range(levels):
                    out_ref[(t, v) + at] = field[v]


def local(
    ocean,
    kappa,
    atmos,
    piston,
    atmos_mix,
    fold_map,
    send_tile,
    slot_counts,
    out_slot,
    out_tile,
    remap_w,
):
    count = lax.axis_size("tile")
    me = lax.axis_index("tile").astype(jnp.int32).reshape(1)
    tracers, levels, ocean_rows, columns = ocean.shape
    planes = tracers * levels
    window, slots_in = send_tile.shape[1:]
    slots_out = out_tile.shape[2]
    blocks = window * slots_in
    n_slots = window * slots_out
    tiles = -(-columns // LANES)
    padded = tiles * LANES
    atmos_rows, atmos_columns = atmos.shape[2:]
    across = atmos_columns // LANES
    n_tiles = atmos_rows * across
    f32, bf16, i32 = jnp.float32, jnp.bfloat16, jnp.int32
    shape = jax.ShapeDtypeStruct
    dma = pltpu.SemaphoreType.DMA
    exchange = functools.partial(
        lax.all_to_all, axis_name="tile", split_axis=0, concat_axis=0, tiled=True
    )

    def cost(us):
        return pl.CostEstimate(
            flops=0, bytes_accessed=int(us * 1.0e4), transcendentals=0
        )

    token_shape = shape((8, LANES), f32)
    sent, token = pl.pallas_call(
        pack_kernel,
        out_shape=(pltpu.HBM((count, tracers * slots_in, LANES), bf16), token_shape),
        in_specs=[smem(), hbm(), hbm()],
        out_specs=(vmem(), vmem()),
        scratch_shapes=[
            pltpu.SMEM(send_tile.shape, i32),
            pltpu.VMEM((tracers, ocean_rows, columns), f32),
            pltpu.VMEM((tracers, tiles * 8, LANES), f32),
            pltpu.VMEM((window, tracers * slots_in, LANES), f32),
            dma((tracers + 1,)),
        ],
        compiler_params=params(),
        name="pack",
    )(me, in_hbm(send_tile), in_hbm(ocean))
    received = exchange(sent)

    halo_rows = 6 * planes
    flat = in_hbm(ocean.reshape(planes * ocean_rows, columns))
    weights = in_hbm(remap_w[0])
    prepared = pl.pallas_call(
        prepare_kernel,
        out_shape=(
            *[shape((slots_in,) + remap_w.shape[2:], bf16)] * HELD,
            pltpu.HBM((halo_rows, padded), bf16),
            pltpu.HBM((halo_rows, padded), bf16),
            shape((n_slots, blocks), bf16),
            shape((blocks, n_slots), bf16),
            shape((n_tiles, n_slots), bf16),
            shape((n_slots, n_tiles), bf16),
            shape((tiles * 8, blocks), bf16),
            shape((tracers, n_tiles, LANES), f32),
            shape((n_tiles, LANES), f32),
        ),
        in_specs=[smem(), vmem()] + [hbm()] * 9,
        out_specs=(vmem(),) * HELD + (hbm(),) * 2 + (vmem(),) * 7,
        scratch_shapes=[
            pltpu.VMEM((planes * ocean_rows, columns), f32),
            pltpu.VMEM((ocean_rows, columns), f32),
            pltpu.VMEM((tiles, (planes + 1) * ocean_rows, LANES), f32),
            pltpu.VMEM((halo_rows, padded), bf16),
            pltpu.VMEM((halo_rows, padded), bf16),
            pltpu.VMEM((tracers, atmos_rows, atmos_columns), f32),
            pltpu.VMEM((atmos_rows, atmos_columns), f32),
            pltpu.SMEM(slot_counts.shape, i32),
            pltpu.VMEM(out_slot.shape, i32),
            pltpu.SMEM(out_tile.shape, i32),
            pltpu.SMEM(send_tile.shape, i32),
            dma((tracers + 9 + HELD,)),
        ],
        compiler_params=params(),
        cost_estimate=cost(3),
        name="prepare",
    )(
        me,
        token,
        in_hbm(slot_counts),
        in_hbm(out_slot),
        in_hbm(out_tile),
        in_hbm(send_tile),
        flat,
        in_hbm(kappa),
        in_hbm(atmos),
        in_hbm(piston),
        weights,
    )
    held = prepared[:HELD]
    even, odd = prepared[HELD : HELD + 2]
    sum_table, slot_pick, spread, flux_pick, scatter, air, rate = prepared[HELD + 2 :]
    even_pairs = [(i, i ^ 1) for i in range(count) if i ^ 1 < count]
    odd_pairs = [(i, i + 1) for i in range(1, count - 1, 2)]
    odd_pairs += [(b, a) for a, b in odd_pairs]
    even = lax.ppermute(even, "tile", even_pairs)
    odd = lax.ppermute(odd, "tile", odd_pairs)
    weight_scratch = [
        pltpu.VMEM((blocks - HELD * slots_in,) + remap_w.shape[2:], bf16),
        dma((window - HELD,)),
    ]

    partial_sums, token = pl.pallas_call(
        forward_kernel,
        out_shape=(shape((count, tracers * slots_out, LANES), f32), token_shape),
        in_specs=[smem(), vmem(), vmem(), hbm()] + [vmem()] * HELD,
        out_specs=(vmem(), vmem()),
        scratch_shapes=[pltpu.VMEM((tracers, blocks, LANES), f32)] + weight_scratch,
        compiler_params=params(),
        name="forward",
    )(me, received, sum_table, weights, *held)
    owner_parts = exchange(partial_sums.astype(jnp.float16)).astype(f32)

    state_shape = (16, planes, padded)
    kap_shape = (tiles, 16, LANES)
    fold = fold_map.reshape(1, columns)
    fold_scratch = [pltpu.VMEM((2 * LANES, padded), bf16)]
    state, kap, token = pl.pallas_call(
        functools.partial(first_sweep_kernel, levels=levels, peers=count),
        out_shape=(pltpu.HBM(state_shape, f32), pltpu.HBM((tiles, 16, LANES), f32), token_shape),
        in_specs=[smem(), vmem()] + [hbm()] * 4 + [vmem()],
        out_specs=(hbm(), hbm(), vmem()),
        scratch_shapes=[
            pltpu.VMEM(state_shape, f32),
            pltpu.VMEM(state_shape, f32),
            pltpu.VMEM(kap_shape, f32),
            pltpu.VMEM((planes * ocean_rows, columns), f32),
            pltpu.VMEM((ocean_rows, columns), f32),
            pltpu.VMEM((halo_rows, padded), bf16),
            pltpu.VMEM((halo_rows, padded), bf16),
            pltpu.VMEM((tiles, (planes + 1) * ocean_rows, LANES), f32),
        ]
        + fold_scratch
        + [dma((4,)), dma((16,))],
        compiler_params=params(),
        cost_estimate=cost(5),
        name="first_sweep",
    )(me, token, flat, in_hbm(kappa), in_hbm(even), in_hbm(odd), fold)

    flux_sent, flux, flux_token = pl.pallas_call(
        flux_kernel,
        out_shape=(
            pltpu.HBM((count, tracers * slots_out, LANES), bf16),
            shape((tracers, atmos_rows, atmos_columns), f32),
            token_shape,
        ),
        in_specs=[smem()] + [vmem()] * 6,
        out_specs=(vmem(),) * 3,
        compiler_params=params(),
        name="flux",
    )(me, token, owner_parts, spread, flux_pick, air, rate)
    at_coupler = exchange(flux_sent)

    atmos_next, token = pl.pallas_call(
        atmos_kernel,
        out_shape=(pltpu.HBM(atmos.shape, f32), token_shape),
        in_specs=[vmem()] * 4,
        out_specs=(vmem(), vmem()),
        compiler_params=params(),
        cost_estimate=cost(2),
        name="atmos",
    )(flux_token, in_hbm(atmos), flux, in_hbm(atmos_mix))

    back_sums, token = pl.pallas_call(
        backward_kernel,
        out_shape=(shape((count, tracers * slots_in, LANES), f32), token_shape),
        in_specs=[smem()] + [vmem()] * 3 + [hbm()] + [vmem()] * HELD,
        out_specs=(vmem(), vmem()),
        scratch_shapes=weight_scratch,
        compiler_params=params(),
        name="backward",
    )(me, token, at_coupler, slot_pick, weights, *held)
    returned = exchange(back_sums.astype(jnp.float16)).astype(f32)

    swept, surface = pl.pallas_call(
        functools.partial(last_sweeps_kernel, levels=levels, peers=count),
        out_shape=(
            pltpu.HBM((planes * ocean_rows, columns), f32),
            shape((tracers, ocean_rows, columns), f32),
        ),
        in_specs=[smem(), vmem(), hbm(), hbm(), vmem()],
        out_specs=(vmem(), vmem()),
        scratch_shapes=[
            pltpu.VMEM(state_shape, f32),
            pltpu.VMEM(kap_shape, f32),
            pltpu.VMEM(state_shape, f32),
            pltpu.VMEM((tiles, (planes + 1) * ocean_rows, LANES), f32),
        ]
        + fold_scratch
        + [dma((16,))],
        compiler_params=params(),
        cost_estimate=cost(4),
        name="last_sweeps",
    )(me, token, in_hbm(state), in_hbm(kap), fold)
    ocean_next = pl.pallas_call(
        add_kernel,
        out_shape=shape(ocean.shape, f32),
        in_specs=[smem()] + [vmem()] * 3 + [hbm()],
        out_specs=hbm(),
        scratch_shapes=[pltpu.VMEM((tracers, ocean_rows, columns), f32), dma((tracers,))],
        input_output_aliases={4: 0},
        compiler_params=params(),
        name="add",
    )(me, returned, scatter, surface, in_hbm(swept.reshape(ocean.shape)))
    return (ocean_next, atmos_next)


def solution(mesh):
    placed = (
        P("member", None, "tile", None),
        P("tile", None),
        P("member", None, "tile", None),
        P("tile", None),
        P("tile", None),
        P(),
        P("tile", None, None),
        P("tile", None),
        P("tile", None),
        P("tile", None, None),
        P("tile", None, None, None),
    )
    return jax.shard_map(
        local,
        mesh=mesh,
        in_specs=placed,
        out_specs=(P("member", None, "tile", None), P("member", None, "tile", None)),
        check_vma=False,
    )
```
